32 devices in a mesh: seq: 4 (over x, core), tp: 8 (over z, y).
Axes of the slice: x: 2, y: 2, z: 4, core: 2. Of those that a mesh axis runs over, the one named last changes fastest.
Arguments:
- tokens: bfloat16 [1024, 4096], P('seq', 'tp'), may hold values from -12 to 12
- norm_gain: float32 [2, 4096], replicated, may hold values from 0.5 to 1.5
- w_in: bfloat16 [2, 4096, 2, 8192], P(None, None, None, 'tp'), may hold values from -0.09375 to 0.09375
- w_low: bfloat16 [2, 4096, 288], P(None, 'tp'), may hold values from -0.09375 to 0.09375
- w_dt: bfloat16 [2, 256, 8192], P(None, None, 'tp'), may hold values from -0.75 to 0.75
- a_rate: float32 [2, 16, 8192], P(None, None, 'tp'), may hold values from 0.00048828125 to 0.2
- dt_bias: float32 [2, 8192], P(None, 'tp'), may hold values from -5 to -1
- skip_gain: float32 [2, 8192], P(None, 'tp'), may hold values from 0.5 to 1.5
- threshold: float32 [2, 8192], P(None, 'tp'), may hold values from 0.1 to 0.8
- w_out: bfloat16 [2, 8192, 4096], P(None, 'tp'), may hold values from -0.09375 to 0.09375
Outputs:
- hidden: bfloat16 [1024, 4096], P('seq', 'tp')
The draws below stay inside these ranges and needn't reach their ends.
All inputs are finite; a program needn't handle non-finite values.
Results may differ from the reference program's by a relative error of at most 0.019.
Values may be sent and summed in bfloat16 or wider, within the bound.
No kernel may reach another device: no remote copies, remote signals or barrier semaphores. Data moves between devices by JAX's collectives and lax.ppermute only.
A program may use at most 192 MiB of HBM per device.

```python
import math
import jax
import jax.numpy as jnp
from jax import lax

D = 4096
CHANNELS = 8192
STATE = 16
RANK = 256
GROUP = 128
LAYERS = 2
TOK_DEV = 256
TOKENS = 1024
CH_DEV = 1024
N_TP = 8


def draw_tokens(key, part):
    key_noise = jax.random.fold_in(key, 11)
    key_amp = jax.random.fold_in(key, 12)
    key_dir = jax.random.fold_in(key, 13)
    block_count = TOKENS // TOK_DEV
    noise = jnp.clip(jax.random.normal(key_noise, (TOKENS, D), jnp.float32), -4.0, 4.0)
    amp = jax.random.uniform(key_amp, (block_count, 1), jnp.float32, -2.5, 2.5)
    dir_vec = jnp.clip(jax.random.normal(key_dir, (1, D), jnp.float32), -3.0, 3.0)
    offset = jnp.repeat(amp, TOK_DEV, axis=0) * dir_vec
    return jnp.clip(noise + offset, -12.0, 12.0).astype(jnp.bfloat16)


def spiked(values, own_key, source, target, parts, factor):
    owner, partner = [(jnp.arange(values.shape[dim]) // (values.shape[dim] // parts)).reshape([-1 if axis == dim else 1 for axis in range(values.ndim)]) for dim in (source, target)]
    chosen = jax.random.permutation(own_key, parts)[partner]
    strong = (owner == chosen) | (owner == (partner + parts // 2) % parts)
    return jnp.where(strong, factor * values, values)


def block_scale(key, shape, split, low, top_value):
    def one(position, parts):
        steps = jax.random.uniform(jax.random.fold_in(jax.random.fold_in(key, 6), position), (parts,), jnp.float32, low / len(split), top_value / len(split))
        return jnp.repeat(jnp.exp(steps), shape[position] // parts).reshape((-1,) + (1,) * (len(shape) - position - 1))

    loudness = one(*split[0])
    for cut in split[1:]:
        loudness = loudness * one(*cut)
    return loudness


def normal_values(stream_key, shape, deviation, most, shards=(), dtype=jnp.bfloat16):
    drawn = jax.random.normal(stream_key, shape, jnp.float32) * deviation
    if len(shards) > 0:
        drawn = block_scale(stream_key, shape, shards, -0.22, 0.18) * drawn
    return jnp.clip(drawn, min=-most, max=most).astype(dtype)


def noise_with(own_key, shape, spread, limit, pieces, heavy, held_as=jnp.bfloat16):
    result = spread * jax.random.normal(own_key, shape, jnp.float32)
    if pieces:
        result = result * block_scale(own_key, shape, pieces, -0.22, 0.18)
    return jnp.clip(spiked(result, jax.random.fold_in(own_key, 3), *heavy), -limit, limit).astype(held_as)


def setup_inputs(seed: int = 0) -> dict:
    arg_keys = jax.random.split(jax.random.key(seed), 11)
    return {
        "tokens": draw_tokens(jax.random.fold_in(arg_keys[10], 71), 0),
        "norm_gain": jnp.clip(1.0 + 0.1 * jax.random.normal(arg_keys[1], (LAYERS, D), jnp.float32), 0.5, 1.5),
        "w_in": normal_values(arg_keys[2], (LAYERS, D, 2, CHANNELS), D ** -0.5, 0.09375, ((3, 8),)),
        "w_low": normal_values(arg_keys[3], (LAYERS, D, RANK + 2 * STATE), D ** -0.5, 0.09375, ((1, 8),)),
        "w_dt": normal_values(arg_keys[4], (LAYERS, RANK, CHANNELS), (RANK // 4) ** -0.5, 0.75, ((2, 8),)),
        "a_rate": jnp.clip(jnp.exp(math.log(0.2) - 6.015181 * jax.random.uniform(arg_keys[5], (LAYERS, STATE, CHANNELS), jnp.float32) ** block_scale(arg_keys[5], (LAYERS, STATE, CHANNELS), ((2, 8),), -0.2, 0.2)), 0.00048828125, 0.2),
        "dt_bias": jnp.clip(-5.0 + 4.0 * jax.random.uniform(arg_keys[6], (LAYERS, CHANNELS), jnp.float32) ** block_scale(arg_keys[6], (LAYERS, CHANNELS), ((1, 8),), -0.2, 0.2), -5.0, -1.0),
        "skip_gain": jnp.clip(0.5 + 1.0 * jax.random.uniform(arg_keys[7], (LAYERS, CHANNELS), jnp.float32) ** block_scale(arg_keys[7], (LAYERS, CHANNELS), ((1, 8),), -0.2, 0.2), 0.5, 1.5),
        "threshold": jnp.clip(0.1 + 0.7 * jax.random.uniform(arg_keys[8], (LAYERS, CHANNELS), jnp.float32) ** block_scale(arg_keys[8], (LAYERS, CHANNELS), ((1, 8),), -0.2, 0.2), 0.1, 0.8),
        "w_out": noise_with(arg_keys[9], (LAYERS, CHANNELS, D), CHANNELS ** -0.5, 0.09375, ((1, 8),), (1, 2, 8, 2.0)),
    }


def rms_rows(values_in, gain_row):
    values = values_in.astype(jnp.float32)
    factor = lax.rsqrt(lax.optimization_barrier(jnp.mean(values * values, axis=-1, keepdims=True)) + 1e-05)
    return (values * factor * gain_row).astype(jnp.bfloat16)

def shrink_gate(mixed_out, gate_pre, thresh_row):
    row_count, chan_width = mixed_out.shape
    grouped = mixed_out.reshape(row_count, chan_width // GROUP, GROUP)
    factor = lax.rsqrt(lax.optimization_barrier(jnp.mean(grouped * grouped, axis=-1, keepdims=True)) + 1e-05)
    normal_out = (grouped * factor).reshape(row_count, chan_width)
    shrunk = jax.nn.relu(normal_out - thresh_row) - jax.nn.relu(-normal_out - thresh_row)
    return (shrunk * jax.nn.silu(gate_pre)).astype(jnp.bfloat16)

def ref_layer(hidden, gain_row, w_in_l, w_low_l, w_dt_l, rates, bias_row, skip_row, thresh_row, w_out_l):
    normed = rms_rows(hidden, gain_row)
    projected = jnp.dot(normed, w_in_l.reshape(D, 2 * CHANNELS), preferred_element_type=jnp.float32)
    current = projected[:, :CHANNELS]
    gate_pre = projected[:, CHANNELS:]
    selectors = jnp.dot(normed, w_low_l, preferred_element_type=jnp.float32)
    rank_part = selectors[:, :RANK].astype(jnp.bfloat16)
    in_sel = selectors[:, RANK:RANK + STATE]
    out_sel = selectors[:, RANK + STATE:]
    step_size = jax.nn.softplus(jnp.dot(rank_part, w_dt_l, preferred_element_type=jnp.float32) + bias_row)
    drive_in = step_size * current

    def advance(state_now, inputs):
        step_row, drive_row, in_row, out_row = inputs
        state_now = jnp.exp(-step_row[None, :] * rates) * state_now + in_row[:, None] * drive_row[None, :]
        return (state_now, lax.optimization_barrier(jnp.sum(out_row[:, None] * state_now, axis=0)))
    final_state, mixed_out = lax.scan(advance, jnp.zeros((STATE, CHANNELS), jnp.float32), (step_size, drive_in, in_sel, out_sel))
    mixed_out = mixed_out + skip_row * current
    gated_out = shrink_gate(mixed_out, gate_pre, thresh_row)
    slabs_gate = gated_out.reshape(TOKENS, N_TP, CH_DEV).transpose(1, 0, 2)
    slabs_weight = w_out_l.reshape(N_TP, CH_DEV, D)

    def add_slab(running, pair):
        term = jnp.dot(pair[0], pair[1], preferred_element_type=jnp.float32)
        rounded = lax.optimization_barrier(term.astype(jnp.bfloat16)).astype(jnp.float32)
        return (running + rounded, None)
    summed, unused = lax.scan(add_slab, jnp.zeros((TOKENS, D), jnp.float32), (slabs_gate, slabs_weight))
    return (hidden.astype(jnp.float32) + summed).astype(jnp.bfloat16)

def reference(tokens, norm_gain, w_in, w_low, w_dt, a_rate, dt_bias, skip_gain, threshold, w_out):
    hidden = tokens
    for layer_index in range(LAYERS):
        hidden = ref_layer(hidden, norm_gain[layer_index], w_in[layer_index], w_low[layer_index], w_dt[layer_index], a_rate[layer_index], dt_bias[layer_index], skip_gain[layer_index], threshold[layer_index], w_out[layer_index])
    return hidden
```

```python
import functools
import math

import jax
import jax.numpy as jnp
from jax import lax
from jax.experimental import pallas as pl
from jax.experimental.pallas import tpu as pltpu
from jax.sharding import PartitionSpec as P

LANES = 128
EPS = 1e-05
DEPTH = 4
LIMIT = 48 * 1024 * 1024
F32 = jnp.float32
BF16 = jnp.bfloat16


def vmem():
    return pl.BlockSpec(memory_space=pltpu.VMEM)


def row_factor(square_sum, width):
    return lax.rsqrt(square_sum / width + EPS)


def proj_kernel(count, first, layer, place_ref, *refs):
    shards = refs[:count]
    gain_ref, w_ref = refs[count : count + 2]
    before = refs[count + 2 : -3]
    cur_ref, gate_ref, square_ref = refs[-3:]
    step = pl.program_id(0)

    @pl.when(step == 0)
    def _():
        for out, source in zip((cur_ref, gate_ref, square_ref), before or (None,) * 3):
            out[...] = jnp.zeros_like(out) if source is None else source[...]

    for j in range(count):

        @pl.when(step == j)
        def _():
            values = shards[j][...].astype(F32)
            scaled = (values * gain_ref[layer : layer + 1, :]).astype(BF16)
            cur_ref[...] += jnp.dot(scaled, w_ref[0], preferred_element_type=F32)
            gate_ref[...] += jnp.dot(scaled, w_ref[1], preferred_element_type=F32)
            square_ref[...] += jnp.sum(values * values, axis=1, keepdims=True)


def project(layer, shards, places, norm_gain, w_lanes, before):
    count = len(shards)
    rows, width = shards[0].shape
    chans = w_lanes.shape[-1]
    layers = norm_gain.shape[0]
    whole = lambda shape: pl.BlockSpec(shape, lambda i, p: (0,) * len(shape))
    state = ((rows, chans), (rows, chans), (rows, 1))
    in_specs = [whole((rows, width))] * count
    in_specs += [
        pl.BlockSpec((layers, width), lambda i, p: (0, p[i])),
        pl.BlockSpec((2, width, chans), lambda i, p: (0, p[i], 0)),
    ]
    operands = [places, *shards, norm_gain, w_lanes]
    aliases = {}
    if before is not None:
        aliases = {len(operands) + j: j for j in range(3)}
        in_specs += [whole(s) for s in state]
        operands += list(before)
    return pl.pallas_call(
        functools.partial(proj_kernel, count, before is None, layer),
        out_shape=[jax.ShapeDtypeStruct(s, F32) for s in state],
        grid_spec=pltpu.PrefetchScalarGridSpec(
            num_scalar_prefetch=1,
            grid=(count,),
            in_specs=in_specs,
            out_specs=[whole(s) for s in state],
        ),
        input_output_aliases=aliases,
        compiler_params=pltpu.CompilerParams(vmem_limit_bytes=LIMIT),
        cost_estimate=pl.CostEstimate(
            flops=4 * count * rows * width * chans,
            bytes_accessed=count * (4 * width * chans + 2 * rows * width),
            transcendentals=0,
        ),
        name="project",
    )(*operands)


def scan_kernel(
    layer,
    states,
    sel_ref,
    low_ref,
    square_ref,
    cur_ref,
    w_dt_ref,
    bias_ref,
    rate_ref,
    out_ref,
    time_ref,
    final_ref,
    step_s,
    drive_s,
    width,
):
    rows, chans = cur_ref.shape
    fold = chans // LANES
    rank = w_dt_ref.shape[1]
    factor = row_factor(square_ref[...], width)
    rank_part = (low_ref[:, :rank].astype(F32) * factor).astype(BF16)
    piece = 2 * LANES
    for begin in range(0, chans, piece):
        cols = slice(begin, begin + piece)
        pre = jnp.dot(rank_part, w_dt_ref[0, :, cols], preferred_element_type=F32)
        pre = pre + bias_ref[layer : layer + 1, cols]
        step = jnp.maximum(pre, 0.0) + jnp.log1p(jnp.exp(-jnp.abs(pre)))
        drive = step * (cur_ref[:, cols] * factor)
        for q in range(piece // LANES):
            part = slice(q * LANES, (q + 1) * LANES)
            place = pl.ds(begin // LANES + q, rows, stride=fold)
            step_s[place, :] = step[:, part]
            drive_s[place, :] = drive[:, part]

    def advance(t, carried):
        time, held = carried
        here = pl.ds(pl.multiple_of(t * fold, fold), fold)
        step = step_s[here, :]
        drive = drive_s[here, :]
        sums = [None] * 4
        after = []
        for s in range(states):
            decay = jnp.exp2(step * rate_ref[s])
            now = decay * held[s] + drive * sel_ref[t, s]
            term = now * sel_ref[t, states + s]
            sums[s % 4] = term if sums[s % 4] is None else sums[s % 4] + term
            after.append(now)
        time = time + step
        out_ref[here, :] = (sums[0] + sums[1]) + (sums[2] + sums[3])
        time_ref[here, :] = time
        return time, tuple(after)

    zero = jnp.zeros((fold, LANES), F32)
    time, held = lax.fori_loop(0, rows, advance, (zero, (zero,) * states), unroll=4)
    for s in range(states):
        final_ref[s] = held[s]
    final_ref[states] = time


def local_scan(layer, width, selectors, low, square, cur, w_dt, dt_bias, rate):
    rows, chans = cur.shape
    states, fold, _ = rate.shape
    layers, rank, _ = w_dt.shape
    folded = jax.ShapeDtypeStruct((rows * fold, LANES), F32)
    whole = lambda shape: pl.BlockSpec(shape, lambda i: (0,) * len(shape))
    return pl.pallas_call(
        functools.partial(scan_kernel, layer, states, width=width),
        grid=(1,),
        out_shape=[folded, folded, jax.ShapeDtypeStruct((states + 1, fold, LANES), F32)],
        in_specs=[
            pl.BlockSpec(memory_space=pltpu.SMEM),
            whole(low.shape),
            whole(square.shape),
            whole(cur.shape),
            pl.BlockSpec((1, rank, chans), lambda i: (layer, 0, 0)),
            whole(dt_bias.shape),
            whole(rate.shape),
        ],
        out_specs=[whole(folded.shape), whole(folded.shape), whole((states + 1, fold, LANES))],
        scratch_shapes=[pltpu.VMEM(folded.shape, F32), pltpu.VMEM(folded.shape, F32)],
        compiler_params=pltpu.CompilerParams(vmem_limit_bytes=LIMIT),
        cost_estimate=pl.CostEstimate(
            flops=8 * rows * states * chans,
            bytes_accessed=20 * rows * chans,
            transcendentals=rows * states * chans,
        ),
        name="local_scan",
    )(selectors, low, square, cur, w_dt, dt_bias, rate)


def close_kernel(layer, states, arrived, count, width, places_ref, *refs):
    sel_ref, out_ref, time_ref, cur_ref, gate_ref, square_ref = refs[:6]
    entries = refs[6 : 6 + arrived]
    rate_ref, skip_ref, thresh_ref, w_ref = refs[6 + arrived : 10 + arrived]
    gated_ref = refs[10 + arrived]
    chunks = refs[11 + arrived : 11 + arrived + count]
    enter_s, mixed_s = refs[-2:]
    rows, chans = cur_ref.shape
    fold = chans // LANES
    step_id = pl.program_id(0)

    @pl.when(step_id == 0)
    def _():
        for s in range(states):
            state = jnp.zeros((fold, LANES), F32)
            for entry in reversed(entries):
                state = jnp.exp2(entry[states] * rate_ref[s]) * state + entry[s]
            enter_s[s] = state

        def correct(t, carried):
            here = pl.ds(pl.multiple_of(t * fold, fold), fold)
            time = time_ref[here, :]
            sums = [out_ref[here, :], None, None, None]
            for s in range(states):
                term = jnp.exp2(time * rate_ref[s]) * (enter_s[s] * sel_ref[t, states + s])
                sums[s % 4] = term if sums[s % 4] is None else sums[s % 4] + term
            mixed_s[here, :] = (sums[0] + sums[1]) + (sums[2] + sums[3])
            return carried

        lax.fori_loop(0, rows, correct, 0, unroll=4)

        factor = row_factor(square_ref[...], width)
        for r in range(fold):
            cols = slice(r * LANES, (r + 1) * LANES)
            current = cur_ref[:, cols] * factor
            mixed = mixed_s[pl.ds(r, rows, stride=fold), :] + skip_ref[layer : layer + 1, cols] * current
            normal = mixed * lax.rsqrt(jnp.mean(mixed * mixed, axis=1, keepdims=True) + EPS)
            thresh = thresh_ref[layer : layer + 1, cols]
            shrunk = jnp.maximum(normal - thresh, 0.0) - jnp.maximum(-normal - thresh, 0.0)
            gate = gate_ref[:, cols] * factor
            gated_ref[:, cols] = (shrunk * (gate * jax.nn.sigmoid(gate))).astype(BF16)

    product = jnp.dot(gated_ref[...], w_ref[0], preferred_element_type=F32).astype(BF16)
    for j in range(count):

        @pl.when(step_id == j)
        def _():
            chunks[j][...] = product


def close_layer(
    layer, width, places, feat, selectors, out, time, cur, gate, square, entries, rate, skip, thresh, w_out
):
    rows, chans = cur.shape
    states, fold, _ = rate.shape
    count = places.shape[0]
    whole = lambda shape: pl.BlockSpec(shape, lambda i, p: (0,) * len(shape))
    operands = [selectors, out, time, cur, gate, square, *entries, rate, skip, thresh]
    in_specs = [pl.BlockSpec(memory_space=pltpu.SMEM)] + [whole(a.shape) for a in operands[1:]]
    in_specs += [pl.BlockSpec((1, chans, feat), lambda i, p: (layer, 0, p[i]))]
    chunk = jax.ShapeDtypeStruct((rows, feat), BF16)
    results = pl.pallas_call(
        functools.partial(close_kernel, layer, states, len(entries), count, width),
        out_shape=[jax.ShapeDtypeStruct((rows, chans), BF16)] + [chunk] * count,
        grid_spec=pltpu.PrefetchScalarGridSpec(
            num_scalar_prefetch=1,
            grid=(count,),
            in_specs=in_specs,
            out_specs=[whole((rows, chans))] + [whole(chunk.shape)] * count,
            scratch_shapes=[
                pltpu.VMEM((states, fold, LANES), F32),
                pltpu.VMEM((rows * fold, LANES), F32),
            ],
        ),
        compiler_params=pltpu.CompilerParams(vmem_limit_bytes=LIMIT),
        cost_estimate=pl.CostEstimate(
            flops=6 * rows * states * chans + 2 * count * rows * chans * feat,
            bytes_accessed=20 * rows * chans + 2 * count * chans * feat,
            transcendentals=rows * states * chans,
        ),
        name="close_layer",
    )(places, *operands, w_out)
    return results[0], results[1:]


def expand_kernel(count, places_ref, gated_ref, w_ref, *chunks):
    product = jnp.dot(gated_ref[...], w_ref[0], preferred_element_type=F32).astype(BF16)
    for j in range(count):

        @pl.when(pl.program_id(0) == j)
        def _():
            chunks[j][...] = product


def expand(layer, places, feat, gated, w_out):
    rows, chans = gated.shape
    count = places.shape[0]
    whole = lambda shape: pl.BlockSpec(shape, lambda i, p: (0,) * len(shape))
    chunk = jax.ShapeDtypeStruct((rows, feat), BF16)
    return pl.pallas_call(
        functools.partial(expand_kernel, count),
        out_shape=[chunk] * count,
        grid_spec=pltpu.PrefetchScalarGridSpec(
            num_scalar_prefetch=1,
            grid=(count,),
            in_specs=[
                whole(gated.shape),
                pl.BlockSpec((1, chans, feat), lambda i, p: (layer, 0, p[i])),
            ],
            out_specs=[whole(chunk.shape)] * count,
        ),
        compiler_params=pltpu.CompilerParams(vmem_limit_bytes=LIMIT),
        cost_estimate=pl.CostEstimate(
            flops=2 * count * rows * chans * feat,
            bytes_accessed=2 * count * chans * feat + 2 * (count + 2) * rows * feat,
            transcendentals=0,
        ),
        name="expand",
    )(places, gated, w_out)


class Grid:
    def __init__(self, count):
        self.depth = DEPTH if count % DEPTH == 0 else 1
        self.side = count // self.depth

    def pairs(self, deep, across):
        places = [(z, y) for z in range(self.depth) for y in range(self.side)]
        at = lambda z, y: (z % self.depth) * self.side + y % self.side
        return [(at(z, y), at(z + deep, y + across)) for z, y in places]

    def send(self, value, deep, across):
        return lax.ppermute(value, "tp", self.pairs(deep, across))

    def index(self, deep, across):
        own = lax.axis_index("tp")
        z, y = own // self.side, own % self.side
        return ((z + deep + self.depth) % self.depth) * self.side + (y + across + self.side) % self.side


def gather(grid, own):
    columns = [own] + [grid.send(own, a, 0) for a in range(1, grid.depth)]
    return [
        [column] + [grid.send(column, 0, b) for b in range(1, grid.side)] for column in columns
    ]


def sum_selectors(grid, partial):
    rows, width = partial.shape
    total = partial.astype(F32)
    for b in range(1, grid.side):
        total = total + grid.send(partial, 0, b).astype(F32)
    part = rows // grid.depth
    total = total.astype(BF16)
    own_z = lax.axis_index("tp") // grid.side
    piece = lambda z: lax.dynamic_slice_in_dim(total, ((z + grid.depth) % grid.depth) * part, part, 0)
    own = piece(own_z).astype(F32)
    for a in range(1, grid.depth):
        own = own + grid.send(piece(own_z + a), a, 0).astype(F32)
    own = own.astype(BF16)
    result = jnp.zeros((rows, width), BF16)
    for a in range(grid.depth):
        got = own if a == 0 else grid.send(own, a, 0)
        place = ((own_z - a + grid.depth) % grid.depth) * part
        result = lax.dynamic_update_slice_in_dim(result, got, place, 0)
    return result


def per_device(
    n_tp, n_seq, tokens, norm_gain, w_in, w_low, w_dt, a_rate, dt_bias, skip_gain, threshold, w_out
):
    grid = Grid(n_tp)
    feat = tokens.shape[1]
    layers, width, _, chans = w_in.shape
    states = a_rate.shape[1]
    rank = w_dt.shape[1]
    fold = chans // LANES
    place = lambda a, b: grid.index(a, b).astype(jnp.int32)
    own_place = lax.axis_index("tp") * feat
    rates = (a_rate * (-math.log2(math.e))).reshape(layers, states, fold, LANES)
    own_rows = tokens
    for layer in range(layers):
        w_lanes = jnp.transpose(w_in[layer], (1, 0, 2))
        shards = gather(grid, own_rows)
        gain = lax.dynamic_slice_in_dim(norm_gain[layer : layer + 1], own_place, feat, 1)
        scaled = (own_rows.astype(F32) * gain).astype(BF16)
        low = jnp.dot(scaled, w_low[layer], preferred_element_type=F32).astype(BF16)
        low = sum_selectors(grid, low)
        state = None
        for a in range(grid.depth):
            places = jnp.stack([place(-a, -b) for b in range(grid.side)])
            state = project(layer, shards[a], places, norm_gain, w_lanes, state)
        cur, gate, square = state
        selectors = low[:, rank:].astype(F32) * row_factor(square, width)
        out, time, final = local_scan(
            layer, width, selectors, low, square, cur, w_dt, dt_bias, rates[layer]
        )
        entries = [
            lax.ppermute(final, "seq", [(i, i + k) for i in range(n_seq - k)])
            for k in range(1, n_seq)
        ]
        order = [(a, b) for a in range(grid.depth) for b in range(1, grid.side)]
        order = order[grid.side - 1 :] + order[: grid.side - 1]
        gated, chunks = close_layer(
            layer,
            width,
            jnp.stack([place(a, b) for a, b in order]),
            feat,
            selectors,
            out,
            time,
            cur,
            gate,
            square,
            entries,
            rates[layer],
            skip_gain,
            threshold,
            w_out,
        )
        crossed = {(a, b): grid.send(chunk, 0, b) for (a, b), chunk in zip(order, chunks)}
        depths = list(range(1, grid.depth)) + [0]
        own_chunks = expand(
            layer, jnp.stack([place(a, 0) for a in depths]), feat, gated, w_out
        )
        total = own_rows.astype(F32)
        for a, chunk in zip(depths, own_chunks):
            part = chunk.astype(F32)
            for b in range(1, grid.side):
                part = part + crossed[a, b].astype(F32)
            if a:
                part = grid.send(part.astype(BF16), a, 0).astype(F32)
            total = total + part
        own_rows = total.astype(BF16)
    return own_rows


def solution(mesh):
    in_specs = (
        P("seq", "tp"),
        P(),
        P(None, None, None, "tp"),
        P(None, "tp", None),
        P(None, None, "tp"),
        P(None, None, "tp"),
        P(None, "tp"),
        P(None, "tp"),
        P(None, "tp"),
        P(None, "tp", None),
    )
    return jax.shard_map(
        functools.partial(per_device, mesh.shape["tp"], mesh.shape["seq"]),
        mesh=mesh,
        in_specs=in_specs,
        out_specs=P("seq", "tp"),
        check_vma=False,
    )
```

```python
import functools
import math

import jax
import jax.numpy as jnp
from jax import lax
from jax.experimental import pallas as pl
from jax.experimental.pallas import tpu as pltpu
from jax.sharding import PartitionSpec as P

LANES = 128
WIDE = 256
EPS = 1e-05
DEPTH = 4
LIMIT = 40 * 1024 * 1024
F32 = jnp.float32
BF16 = jnp.bfloat16
VMEM = pl.BlockSpec(memory_space=pltpu.VMEM)
SMEM = pl.BlockSpec(memory_space=pltpu.SMEM)
HBM = pl.BlockSpec(memory_space=pl.ANY)


def row_factor(square_sum, width):
    return lax.rsqrt(square_sum / width + EPS)


def params():
    return pltpu.CompilerParams(vmem_limit_bytes=LIMIT)


def proj_kernel(count, first, layer, table_at, depth, table_ref, *refs):
    shards = refs[:count]
    gain_ref, w_ref = refs[count : count + 2]
    cur_ref, gate_ref, square_ref, raw_s, split_s, sems = refs[-6:]
    rows, width = shards[0].shape
    chans = cur_ref.shape[1]
    per = 2 * chans // LANES
    pieces = width // depth
    size = depth * per
    begins = [pl.multiple_of(table_ref[table_at + j] * width, width) for j in range(count)]

    def copy(j, q):
        n = j * pieces + q
        return pltpu.make_async_copy(
            w_ref.at[layer, pl.ds(pl.multiple_of((begins[j] + q * depth) * per, size), size), :],
            raw_s.at[n],
            sems.at[n],
        )

    for j in range(count):
        for q in range(pieces):
            copy(j, q).start()
    squares = None if first else square_ref[...]
    for j in range(count):
        values = shards[j][...].astype(F32)
        gain = gain_ref[layer : layer + 1, pl.ds(begins[j], width)]
        scaled = (values * gain).astype(BF16)
        term = jnp.sum(values * values, axis=1, keepdims=True)
        squares = term if squares is None else squares + term
        for q in range(pieces):
            copy(j, q).wait()
            slot = (j * pieces + q) % 2
            split_s[slot] = raw_s[j * pieces + q].astype(F32)
            left = scaled[:, q * depth : (q + 1) * depth]
            for e, out in enumerate((cur_ref, gate_ref)):
                for begin in range(0, chans, WIDE):
                    tiles = [
                        split_s[slot, pl.ds(2 * t + e, depth, stride=per), :].astype(BF16)
                        for t in range(begin // LANES, (begin + WIDE) // LANES)
                    ]
                    product = jnp.dot(
                        left, jnp.concatenate(tiles, axis=1), preferred_element_type=F32
                    )
                    cols = slice(begin, begin + WIDE)
                    if first and j == 0 and q == 0:
                        out[:, cols] = product
                    else:
                        out[:, cols] += product
    square_ref[...] = squares


def project(layer, shards, table, table_at, norm_gain, w_raw, chans, before):
    count = len(shards)
    rows, width = shards[0].shape
    depth = min(width, WIDE)
    pieces = count * (width // depth)
    size = depth * 2 * chans // LANES
    state = [jax.ShapeDtypeStruct(s, F32) for s in ((rows, chans), (rows, chans), (rows, 1))]
    operands = [table, *shards, norm_gain, w_raw]
    in_specs = [SMEM] + [VMEM] * (count + 1) + [HBM]
    aliases = {}
    if before is not None:
        aliases = {len(operands) + j: j for j in range(3)}
        in_specs += [VMEM] * 3
        operands += list(before)
    return pl.pallas_call(
        functools.partial(proj_kernel, count, before is None, layer, table_at, depth),
        out_shape=state,
        in_specs=in_specs,
        out_specs=[VMEM] * 3,
        scratch_shapes=[
            pltpu.VMEM((pieces, size, LANES), BF16),
            pltpu.VMEM((2, size, LANES), F32),
            pltpu.SemaphoreType.DMA((pieces,)),
        ],
        input_output_aliases=aliases,
        compiler_params=params(),
        cost_estimate=pl.CostEstimate(
            flops=4 * count * rows * width * chans,
            bytes_accessed=count * (4 * width * chans + 2 * rows * width),
            transcendentals=0,
        ),
        name="project",
    )(*operands)


def scan_kernel(
    layer,
    states,
    width,
    sel_ref,
    low_ref,
    square_ref,
    cur_ref,
    w_dt_ref,
    bias_ref,
    rate_ref,
    out_ref,
    time_ref,
    final_ref,
    step_s,
    drive_s,
):
    rows, chans = cur_ref.shape
    fold = chans // LANES
    rank = w_dt_ref.shape[1]
    factor = row_factor(square_ref[...], width)
    rank_part = (low_ref[:, :rank].astype(F32) * factor).astype(BF16)
    twice = factor * factor
    for begin in range(0, chans, WIDE):
        cols = slice(begin, begin + WIDE)
        pre = jnp.dot(rank_part, w_dt_ref[layer, :, cols], preferred_element_type=F32)
        pre = pre + bias_ref[layer : layer + 1, cols]
        step = jnp.maximum(pre, 0.0) + jnp.log1p(jnp.exp(-jnp.abs(pre)))
        drive = step * (cur_ref[:, cols] * twice)
        for q in range(WIDE // LANES):
            part = slice(q * LANES, (q + 1) * LANES)
            place = pl.ds(begin // LANES + q, rows, stride=fold)
            step_s[place, :] = step[:, part]
            drive_s[place, :] = drive[:, part]

    def advance(t, carried):
        time, held = carried
        here = pl.ds(pl.multiple_of(t * fold, fold), fold)
        step = step_s[here, :]
        drive = drive_s[here, :]
        sums = [None] * 4
        after = []
        for s in range(states):
            decay = jnp.exp2(step * rate_ref[layer, s])
            now = decay * held[s] + drive * sel_ref[t, s]
            term = now * sel_ref[t, states + s]
            sums[s % 4] = term if sums[s % 4] is None else sums[s % 4] + term
            after.append(now)
        time = time + step
        out_ref[here, :] = (sums[0] + sums[1]) + (sums[2] + sums[3])
        time_ref[here, :] = time
        return time, tuple(after)

    zero = jnp.zeros((fold, LANES), F32)
    time, held = lax.fori_loop(0, rows, advance, (zero, (zero,) * states), unroll=4)
    for s in range(states):
        final_ref[s] = held[s].astype(BF16)
    final_ref[states] = time.astype(BF16)


def local_scan(layer, width, selectors, low, square, cur, w_dt, dt_bias, rate):
    rows, chans = cur.shape
    _, states, fold, _ = rate.shape
    folded = (rows * fold, LANES)
    return pl.pallas_call(
        functools.partial(scan_kernel, layer, states, width),
        out_shape=[
            jax.ShapeDtypeStruct(folded, F32),
            jax.ShapeDtypeStruct(folded, F32),
            jax.ShapeDtypeStruct((states + 1, fold, LANES), BF16),
        ],
        in_specs=[SMEM] + [VMEM] * 6,
        out_specs=[VMEM] * 3,
        scratch_shapes=[pltpu.VMEM(folded, F32), pltpu.VMEM(folded, F32)],
        compiler_params=params(),
        cost_estimate=pl.CostEstimate(
            flops=8 * rows * states * chans,
            bytes_accessed=20 * rows * chans,
            transcendentals=rows * states * chans,
        ),
        name="local_scan",
    )(selectors, low, square, cur, w_dt, dt_bias, rate)


def emit_chunks(layer, table_at, feat, gated_ref, table_ref, w_ref, chunks, w_s, sems, before=None):
    def copy(j):
        begin = pl.multiple_of(table_ref[table_at[j]] * feat, feat)
        return pltpu.make_async_copy(w_ref.at[layer, :, pl.ds(begin, feat)], w_s.at[j], sems.at[j])

    for j in range(len(chunks)):
        copy(j).start()
    if before is not None:
        before()
    for j, chunk in enumerate(chunks):
        copy(j).wait()
        for begin in range(0, feat, WIDE):
            cols = slice(begin, begin + WIDE)
            chunk[:, cols] = jnp.dot(
                gated_ref[...], w_s[j, :, cols], preferred_element_type=F32
            ).astype(BF16)


def close_kernel(layer, states, table_at, feat, width, table_ref, place_ref, sel_ref, *refs):
    out_ref, time_ref, cur_ref, gate_ref, square_ref, final_ref = refs[:6]
    rate_ref, skip_ref, thresh_ref, w_ref, gated_ref = refs[6:11]
    chunks = refs[11 : 11 + len(table_at)]
    enter_s, mixed_s, w_s, sems = refs[-4:]
    rows, chans = cur_ref.shape
    fold = chans // LANES

    def gate_all():
        def enter(p, state):
            time = final_ref[p, states].astype(F32)
            return tuple(
                jnp.exp2(time * rate_ref[layer, s]) * state[s] + final_ref[p, s].astype(F32)
                for s in range(states)
            )

        zero = jnp.zeros((fold, LANES), F32)
        state = lax.fori_loop(0, place_ref[0], enter, (zero,) * states)
        for s in range(states):
            enter_s[s] = state[s]

        def correct(t, carried):
            here = pl.ds(pl.multiple_of(t * fold, fold), fold)
            time = time_ref[here, :]
            sums = [out_ref[here, :], None, None, None]
            for s in range(states):
                term = jnp.exp2(time * rate_ref[layer, s]) * (enter_s[s] * sel_ref[t, states + s])
                sums[s % 4] = term if sums[s % 4] is None else sums[s % 4] + term
            mixed_s[here, :] = (sums[0] + sums[1]) + (sums[2] + sums[3])
            return carried

        lax.fori_loop(0, rows, correct, 0, unroll=4)

        factor = row_factor(square_ref[...], width)
        for r in range(fold):
            cols = slice(r * LANES, (r + 1) * LANES)
            skip = skip_ref[layer : layer + 1, cols]
            mixed = mixed_s[pl.ds(r, rows, stride=fold), :] + skip * cur_ref[:, cols]
            mixed = mixed * factor
            normal = mixed * lax.rsqrt(jnp.mean(mixed * mixed, axis=1, keepdims=True) + EPS)
            thresh = thresh_ref[layer : layer + 1, cols]
            shrunk = jnp.maximum(normal - thresh, 0.0) - jnp.maximum(-normal - thresh, 0.0)
            gate = gate_ref[:, cols] * factor
            gated_ref[:, cols] = (shrunk * (gate * jax.nn.sigmoid(gate))).astype(BF16)

    emit_chunks(layer, table_at, feat, gated_ref, table_ref, w_ref, chunks, w_s, sems, gate_all)


def close_layer(
    layer, width, table, table_at, feat, seq_place, selectors, values, rate, skip, thresh, w_out
):
    rows, chans = values[2].shape
    _, states, fold, _ = rate.shape
    count = len(table_at)
    chunk = jax.ShapeDtypeStruct((rows, feat), BF16)
    results = pl.pallas_call(
        functools.partial(close_kernel, layer, states, table_at, feat, width),
        out_shape=[jax.ShapeDtypeStruct((rows, chans), BF16)] + [chunk] * count,
        in_specs=[SMEM] * 3 + [VMEM] * 9 + [HBM],
        out_specs=[VMEM] * (1 + count),
        scratch_shapes=[
            pltpu.VMEM((states, fold, LANES), F32),
            pltpu.VMEM((rows * fold, LANES), F32),
            pltpu.VMEM((count, chans, feat), BF16),
            pltpu.SemaphoreType.DMA((count,)),
        ],
        compiler_params=params(),
        cost_estimate=pl.CostEstimate(
            flops=6 * rows * states * chans + 2 * count * rows * chans * feat,
            bytes_accessed=20 * rows * chans + 2 * count * chans * feat,
            transcendentals=rows * states * chans,
        ),
        name="close_layer",
    )(table, seq_place, selectors, *values, rate, skip, thresh, w_out)
    return results[0], results[1:]


def expand_kernel(layer, table_at, feat, table_ref, gated_ref, w_ref, *refs):
    chunks = refs[: len(table_at)]
    emit_chunks(layer, table_at, feat, gated_ref, table_ref, w_ref, chunks, *refs[-2:])


def expand(layer, table, table_at, feat, gated, w_out):
    rows, chans = gated.shape
    count = len(table_at)
    return pl.pallas_call(
        functools.partial(expand_kernel, layer, table_at, feat),
        out_shape=[jax.ShapeDtypeStruct((rows, feat), BF16)] * count,
        in_specs=[SMEM, VMEM, HBM],
        out_specs=[VMEM] * count,
        scratch_shapes=[
            pltpu.VMEM((count, chans, feat), BF16),
            pltpu.SemaphoreType.DMA((count,)),
        ],
        compiler_params=params(),
        cost_estimate=pl.CostEstimate(
            flops=2 * count * rows * chans * feat,
            bytes_accessed=2 * count * chans * feat + 2 * (count + 2) * rows * feat,
            transcendentals=0,
        ),
        name="expand",
    )(table, gated, w_out)


class Grid:
    def __init__(self, count):
        self.depth = DEPTH if count % DEPTH == 0 else 1
        self.side = count // self.depth

    def places(self):
        return [(z, y) for z in range(self.depth) for y in range(self.side)]

    def at(self, z, y):
        return (z % self.depth) * self.side + y % self.side

    def send(self, value, deep, across):
        pairs = [(self.at(z, y), self.at(z + deep, y + across)) for z, y in self.places()]
        return lax.ppermute(value, "tp", pairs)

    def swap(self, value, bit):
        pairs = [(self.at(z, y), self.at(z ^ bit, y)) for z, y in self.places()]
        return lax.ppermute(value, "tp", pairs)

    def table(self):
        own = lax.axis_index("tp")
        z, y = own // self.side, own % self.side
        offsets = jnp.arange(self.depth * self.side, dtype=jnp.int32)
        a, b = offsets // self.side, offsets % self.side
        both = []
        for sign in (-1, 1):
            deep = (z + sign * a + self.depth) % self.depth
            both.append(deep * self.side + (y + sign * b + self.side) % self.side)
        return jnp.concatenate(both).astype(jnp.int32)


def gather(grid, own):
    columns = {0: own}
    half = grid.depth // 2
    for a in range(1, grid.depth - half + 1):
        columns[a] = grid.send(columns[a - 1], 1, 0)
        back = grid.depth - a
        if back > a:
            columns[back] = grid.send(columns[(back + 1) % grid.depth], -1, 0)
    return {
        (a, b): grid.send(columns[a], 0, b) if b else columns[a]
        for a in columns
        for b in range(grid.side)
    }


def scatter_order(grid):
    order = []
    for a in range(grid.depth - grid.depth // 2, 0, -1):
        if grid.depth - a > a:
            order.append(grid.depth - a)
        order.append(a)
    return order + [0]


def scatter_sum(grid, own_rows, chunks):
    crossed = {
        (a, b): grid.send(chunks[a, b], 0, b)
        for a in scatter_order(grid)
        for b in range(1, grid.side)
    }
    half = grid.depth - grid.depth // 2
    arriving = {}
    for a in scatter_order(grid):
        part = chunks[a, 0].astype(F32)
        for b in range(1, grid.side):
            part = part + crossed[a, b].astype(F32)
        if a == 0:
            total = own_rows.astype(F32) + part
        elif a <= half:
            if a in arriving:
                part = part + arriving[a].astype(F32)
            arriving[a - 1] = grid.send(part.astype(BF16), 1, 0)
        else:
            if a in arriving:
                part = part + arriving[a].astype(F32)
            after = (a + 1) % grid.depth
            moved = grid.send(part.astype(BF16), -1, 0)
            if after == 0:
                last = moved
            else:
                arriving[after] = moved
    if grid.depth > 1:
        total = total + arriving[0].astype(F32)
    if grid.depth > 2:
        total = total + last.astype(F32)
    return total.astype(BF16)


def sum_selectors(grid, partial):
    rows = partial.shape[0]
    part = rows // grid.side
    own_y = lax.axis_index("tp") % grid.side
    piece = lambda y: lax.dynamic_slice_in_dim(partial, (y % grid.side) * part, part, 0)
    total = piece(own_y).astype(F32)
    for b in range(1, grid.side):
        total = total + grid.send(piece(own_y + b), 0, b).astype(F32)
    bit = 1
    while bit < grid.depth:
        total = total + grid.swap(total.astype(BF16), bit).astype(F32)
        bit *= 2
    total = total.astype(BF16)
    result = jnp.zeros_like(partial)
    for b in range(grid.side):
        got = grid.send(total, 0, b) if b else total
        place = ((own_y - b + grid.side) % grid.side) * part
        result = lax.dynamic_update_slice_in_dim(result, got, place, 0)
    return result


def per_device(
    n_tp, tokens, norm_gain, w_in, w_low, w_dt, a_rate, dt_bias, skip_gain, threshold, w_out
):
    grid = Grid(n_tp)
    feat = tokens.shape[1]
    layers, width, _, chans = w_in.shape
    states = a_rate.shape[1]
    rank = w_dt.shape[1]
    fold = chans // LANES
    table = grid.table()
    forth = lambda a, b: n_tp + a * grid.side + b
    seq_place = lax.axis_index("seq").astype(jnp.int32).reshape(1)
    own_place = lax.axis_index("tp") * feat
    rates = (a_rate * (-math.log2(math.e))).reshape(layers, states, fold, LANES)
    w_raw = w_in.reshape(layers, width, 2, fold, LANES).transpose(0, 1, 3, 2, 4)
    w_raw = w_raw.reshape(layers, width * 2 * fold, LANES)
    own_gain = lax.dynamic_slice_in_dim(norm_gain, own_place, feat, 1)
    order = scatter_order(grid)
    own_rows = tokens
    for layer in range(layers):
        shards = gather(grid, own_rows)
        scaled = (own_rows.astype(F32) * own_gain[layer]).astype(BF16)
        low = jnp.dot(scaled, w_low[layer], preferred_element_type=F32).astype(BF16)
        low = sum_selectors(grid, low)
        selectors = low[:, rank:].astype(F32)
        state = None
        for a in reversed(order):
            arrived = [shards[a, b] for b in range(grid.side)]
            state = project(
                layer, arrived, table, a * grid.side, norm_gain, w_raw, chans, state
            )
        cur, gate, square = state
        out, time, final = local_scan(
            layer, width, selectors, low, square, cur, w_dt, dt_bias, rates
        )
        finals = lax.all_gather(final, "seq")
        keys = [(a, b) for a in order for b in range(1, grid.side)]
        keys += [(a, 0) for a in order]
        lead = grid.side - 1
        gated, chunks = close_layer(
            layer,
            width,
            table,
            [forth(*key) for key in keys[:lead]],
            feat,
            seq_place,
            selectors,
            (out, time, cur, gate, square, finals),
            rates,
            skip_gain,
            threshold,
            w_out,
        )
        others = expand(layer, table, [forth(*key) for key in keys[lead:]], feat, gated, w_out)
        own_rows = scatter_sum(grid, own_rows, dict(zip(keys, [*chunks, *others])))
    return own_rows


def solution(mesh):
    in_specs = (
        P("seq", "tp"),
        P(),
        P(None, None, None, "tp"),
        P(None, "tp", None),
        P(None, None, "tp"),
        P(None, None, "tp"),
        P(None, "tp"),
        P(None, "tp"),
        P(None, "tp"),
        P(None, "tp", None),
    )
    return jax.shard_map(
        functools.partial(per_device, mesh.shape["tp"]),
        mesh=mesh,
        in_specs=in_specs,
        out_specs=P("seq", "tp"),
        check_vma=False,
    )
```

```python
import functools
import math

import jax
import jax.numpy as jnp
from jax import lax
from jax.experimental import pallas as pl
from jax.experimental.pallas import tpu as pltpu
from jax.sharding import PartitionSpec as P

LANES = 128
WIDE = 256
STRIDE = 3
EPS = 1e-05
DEPTH = 4
LIMIT = 40 * 1024 * 1024
F32 = jnp.float32
BF16 = jnp.bfloat16
VMEM = pl.BlockSpec(memory_space=pltpu.VMEM)
SMEM = pl.BlockSpec(memory_space=pltpu.SMEM)
HBM = pl.BlockSpec(memory_space=pl.ANY)


def row_factor(square_sum, width):
    return lax.rsqrt(square_sum / width + EPS)


def fold_stride(count):
    return STRIDE * count + 1


def params():
    return pltpu.CompilerParams(vmem_limit_bytes=LIMIT)


def proj_kernel(count, first, layer, table_at, depth, table_ref, *refs):
    shards = refs[:count]
    gain_ref, w_ref = refs[count : count + 2]
    cur_ref, gate_ref, square_ref, raw_s, split_s, sems = refs[-6:]
    rows, width = shards[0].shape
    chans = cur_ref.shape[1]
    per = 2 * chans // LANES
    pieces = width // depth
    size = depth * per
    apart = fold_stride(depth)
    begins = [pl.multiple_of(table_ref[table_at + j] * width, width) for j in range(count)]

    def copy(j, q):
        n = j * pieces + q
        return pltpu.make_async_copy(
            w_ref.at[layer, pl.ds(pl.multiple_of((begins[j] + q * depth) * per, size), size), :],
            raw_s.at[n],
            sems.at[n],
        )

    for j in range(count):
        for q in range(pieces):
            copy(j, q).start()
    squares = None if first else square_ref[...]
    for j in range(count):
        values = shards[j][...].astype(F32)
        gain = gain_ref[layer : layer + 1, pl.ds(begins[j], width)]
        scaled = (values * gain).astype(BF16)
        term = jnp.sum(values * values, axis=1, keepdims=True)
        squares = term if squares is None else squares + term
        for q in range(pieces):
            copy(j, q).wait()
            slot = (j * pieces + q) % 2
            raw = raw_s.at[j * pieces + q]

            def spread(n, carried):
                taken = max(per, 16)
                values = raw[pl.ds(pl.multiple_of(n * taken, taken), taken), :].astype(F32)
                for k in range(taken // per):
                    d = n * (taken // per) + k
                    part = values[k * per : (k + 1) * per]
                    split_s[slot, pl.ds(d * STRIDE, per, stride=apart), :] = part
                return carried

            lax.fori_loop(0, size // max(per, 16), spread, 0, unroll=16)
            left = scaled[:, q * depth : (q + 1) * depth]
            for e, out in enumerate((cur_ref, gate_ref)):
                for begin in range(0, chans, WIDE):
                    tiles = [
                        split_s[slot, pl.ds((2 * t + e) * apart, depth, stride=STRIDE), :].astype(BF16)
                        for t in range(begin // LANES, (begin + WIDE) // LANES)
                    ]
                    product = jnp.dot(
                        left, jnp.concatenate(tiles, axis=1), preferred_element_type=F32
                    )
                    cols = slice(begin, begin + WIDE)
                    if first and j == 0 and q == 0:
                        out[:, cols] = product
                    else:
                        out[:, cols] += product
    square_ref[...] = squares


def project(layer, shards, table, table_at, norm_gain, w_raw, chans, before):
    count = len(shards)
    rows, width = shards[0].shape
    depth = min(width, WIDE)
    pieces = count * (width // depth)
    size = depth * 2 * chans // LANES
    state = [jax.ShapeDtypeStruct(s, F32) for s in ((rows, chans), (rows, chans), (rows, 1))]
    operands = [table, *shards, norm_gain, w_raw]
    in_specs = [SMEM] + [VMEM] * (count + 1) + [HBM]
    aliases = {}
    if before is not None:
        aliases = {len(operands) + j: j for j in range(3)}
        in_specs += [VMEM] * 3
        operands += list(before)
    return pl.pallas_call(
        functools.partial(proj_kernel, count, before is None, layer, table_at, depth),
        out_shape=state,
        in_specs=in_specs,
        out_specs=[VMEM] * 3,
        scratch_shapes=[
            pltpu.VMEM((pieces, size, LANES), BF16),
            pltpu.VMEM((2, 2 * chans // LANES * fold_stride(depth), LANES), F32),
            pltpu.SemaphoreType.DMA((pieces,)),
        ],
        input_output_aliases=aliases,
        compiler_params=params(),
        cost_estimate=pl.CostEstimate(
            flops=4 * count * rows * width * chans,
            bytes_accessed=count * (4 * width * chans + 2 * rows * width),
            transcendentals=0,
        ),
        name="project",
    )(*operands)


def scan_kernel(
    layer,
    states,
    width,
    sel_ref,
    low_ref,
    square_ref,
    cur_ref,
    w_dt_ref,
    bias_ref,
    rate_ref,
    out_ref,
    time_ref,
    final_ref,
    step_s,
    drive_s,
):
    rows, chans = cur_ref.shape
    fold = chans // LANES
    rank = w_dt_ref.shape[1]
    factor = row_factor(square_ref[...], width)
    rank_part = (low_ref[:, :rank].astype(F32) * factor).astype(BF16)
    apart = fold_stride(rows)
    twice = factor * factor
    for begin in range(0, chans, WIDE):
        cols = slice(begin, begin + WIDE)
        pre = jnp.dot(rank_part, w_dt_ref[layer, :, cols], preferred_element_type=F32)
        pre = pre + bias_ref[layer : layer + 1, cols]
        step = jnp.maximum(pre, 0.0) + jnp.log1p(jnp.exp(-jnp.abs(pre)))
        drive = step * (cur_ref[:, cols] * twice)
        for q in range(WIDE // LANES):
            part = slice(q * LANES, (q + 1) * LANES)
            place = pl.ds((begin // LANES + q) * apart, rows, stride=STRIDE)
            step_s[place, :] = step[:, part]
            drive_s[place, :] = drive[:, part]

    def advance(t, carried):
        time, held = carried
        here = pl.ds(t * STRIDE, fold, stride=apart)
        step = step_s[here, :]
        drive = drive_s[here, :]
        sums = [None] * 4
        after = []
        for s in range(states):
            decay = jnp.exp2(step * rate_ref[layer, s])
            now = decay * held[s] + drive * sel_ref[t, s]
            term = now * sel_ref[t, states + s]
            sums[s % 4] = term if sums[s % 4] is None else sums[s % 4] + term
            after.append(now)
        time = time + step
        out_ref[here, :] = (sums[0] + sums[1]) + (sums[2] + sums[3])
        time_ref[here, :] = time
        return time, tuple(after)

    zero = jnp.zeros((fold, LANES), F32)
    time, held = lax.fori_loop(0, rows, advance, (zero, (zero,) * states), unroll=4)
    for s in range(states):
        final_ref[s] = held[s].astype(BF16)
    final_ref[states] = time.astype(BF16)


def local_scan(layer, width, selectors, low, square, cur, w_dt, dt_bias, rate):
    rows, chans = cur.shape
    _, states, fold, _ = rate.shape
    folded = (fold * fold_stride(rows), LANES)
    return pl.pallas_call(
        functools.partial(scan_kernel, layer, states, width),
        out_shape=[
            jax.ShapeDtypeStruct(folded, F32),
            jax.ShapeDtypeStruct(folded, F32),
            jax.ShapeDtypeStruct((states + 1, fold, LANES), BF16),
        ],
        in_specs=[SMEM] + [VMEM] * 6,
        out_specs=[VMEM] * 3,
        scratch_shapes=[pltpu.VMEM(folded, F32), pltpu.VMEM(folded, F32)],
        compiler_params=params(),
        cost_estimate=pl.CostEstimate(
            flops=8 * rows * states * chans,
            bytes_accessed=20 * rows * chans,
            transcendentals=rows * states * chans,
        ),
        name="local_scan",
    )(selectors, low, square, cur, w_dt, dt_bias, rate)


def emit_chunks(layer, table_at, feat, gated_ref, table_ref, w_ref, chunks, w_s, sems, before=None):
    def copy(j):
        begin = pl.multiple_of(table_ref[table_at[j]] * feat, feat)
        return pltpu.make_async_copy(w_ref.at[layer, :, pl.ds(begin, feat)], w_s.at[j], sems.at[j])

    for j in range(len(chunks)):
        copy(j).start()
    if before is not None:
        before()
    for j, chunk in enumerate(chunks):
        copy(j).wait()
        for begin in range(0, feat, WIDE):
            cols = slice(begin, begin + WIDE)
            chunk[:, cols] = jnp.dot(
                gated_ref[...], w_s[j, :, cols], preferred_element_type=F32
            ).astype(BF16)


def close_kernel(layer, states, table_at, feat, width, table_ref, place_ref, sel_ref, *refs):
    out_ref, time_ref, cur_ref, gate_ref, square_ref, final_ref = refs[:6]
    rate_ref, skip_ref, thresh_ref, w_ref, gated_ref = refs[6:11]
    chunks = refs[11 : 11 + len(table_at)]
    enter_s, mixed_s, w_s, sems = refs[-4:]
    rows, chans = cur_ref.shape
    fold = chans // LANES
    apart = fold_stride(rows)

    def gate_all():
        def enter(p, state):
            time = final_ref[p, states].astype(F32)
            return tuple(
                jnp.exp2(time * rate_ref[layer, s]) * state[s] + final_ref[p, s].astype(F32)
                for s in range(states)
            )

        zero = jnp.zeros((fold, LANES), F32)
        state = lax.fori_loop(0, place_ref[0], enter, (zero,) * states)
        for s in range(states):
            enter_s[s] = state[s]

        def correct(t, carried):
            here = pl.ds(t * STRIDE, fold, stride=apart)
            time = time_ref[here, :]
            sums = [out_ref[here, :], None, None, None]
            for s in range(states):
                term = jnp.exp2(time * rate_ref[layer, s]) * (enter_s[s] * sel_ref[t, states + s])
                sums[s % 4] = term if sums[s % 4] is None else sums[s % 4] + term
            mixed_s[here, :] = (sums[0] + sums[1]) + (sums[2] + sums[3])
            return carried

        lax.fori_loop(0, rows, correct, 0, unroll=4)

        factor = row_factor(square_ref[...], width)
        for r in range(fold):
            cols = slice(r * LANES, (r + 1) * LANES)
            skip = skip_ref[layer : layer + 1, cols]
            mixed = mixed_s[pl.ds(r * apart, rows, stride=STRIDE), :] + skip * cur_ref[:, cols]
            mixed = mixed * factor
            normal = mixed * lax.rsqrt(jnp.mean(mixed * mixed, axis=1, keepdims=True) + EPS)
            thresh = thresh_ref[layer : layer + 1, cols]
            shrunk = jnp.maximum(normal - thresh, 0.0) - jnp.maximum(-normal - thresh, 0.0)
            gate = gate_ref[:, cols] * factor
            gated_ref[:, cols] = (shrunk * (gate * jax.nn.sigmoid(gate))).astype(BF16)

    emit_chunks(layer, table_at, feat, gated_ref, table_ref, w_ref, chunks, w_s, sems, gate_all)


def close_layer(
    layer, width, table, table_at, feat, seq_place, selectors, values, rate, skip, thresh, w_out
):
    rows, chans = values[2].shape
    _, states, fold, _ = rate.shape
    count = len(table_at)
    chunk = jax.ShapeDtypeStruct((rows, feat), BF16)
    results = pl.pallas_call(
        functools.partial(close_kernel, layer, states, table_at, feat, width),
        out_shape=[jax.ShapeDtypeStruct((rows, chans), BF16)] + [chunk] * count,
        in_specs=[SMEM] * 3 + [VMEM] * 9 + [HBM],
        out_specs=[VMEM] * (1 + count),
        scratch_shapes=[
            pltpu.VMEM((states, fold, LANES), F32),
            pltpu.VMEM((fold * fold_stride(rows), LANES), F32),
            pltpu.VMEM((count, chans, feat), BF16),
            pltpu.SemaphoreType.DMA((count,)),
        ],
        compiler_params=params(),
        cost_estimate=pl.CostEstimate(
            flops=6 * rows * states * chans + 2 * count * rows * chans * feat,
            bytes_accessed=20 * rows * chans + 2 * count * chans * feat,
            transcendentals=rows * states * chans,
        ),
        name="close_layer",
    )(table, seq_place, selectors, *values, rate, skip, thresh, w_out)
    return results[0], results[1:]


def expand_kernel(layer, table_at, feat, table_ref, gated_ref, w_ref, *refs):
    chunks = refs[: len(table_at)]
    emit_chunks(layer, table_at, feat, gated_ref, table_ref, w_ref, chunks, *refs[-2:])


def expand(layer, table, table_at, feat, gated, w_out):
    rows, chans = gated.shape
    count = len(table_at)
    return pl.pallas_call(
        functools.partial(expand_kernel, layer, table_at, feat),
        out_shape=[jax.ShapeDtypeStruct((rows, feat), BF16)] * count,
        in_specs=[SMEM, VMEM, HBM],
        out_specs=[VMEM] * count,
        scratch_shapes=[
            pltpu.VMEM((count, chans, feat), BF16),
            pltpu.SemaphoreType.DMA((count,)),
        ],
        compiler_params=params(),
        cost_estimate=pl.CostEstimate(
            flops=2 * count * rows * chans * feat,
            bytes_accessed=2 * count * chans * feat + 2 * (count + 2) * rows * feat,
            transcendentals=0,
        ),
        name="expand",
    )(table, gated, w_out)


class Grid:
    def __init__(self, count):
        self.depth = DEPTH if count % DEPTH == 0 else 1
        self.side = count // self.depth

    def places(self):
        return [(z, y) for z in range(self.depth) for y in range(self.side)]

    def at(self, z, y):
        return (z % self.depth) * self.side + y % self.side

    def send(self, value, deep, across):
        pairs = [(self.at(z, y), self.at(z + deep, y + across)) for z, y in self.places()]
        return lax.ppermute(value, "tp", pairs)

    def swap(self, value, bit):
        pairs = [(self.at(z, y), self.at(z ^ bit, y)) for z, y in self.places()]
        return lax.ppermute(value, "tp", pairs)

    def table(self):
        own = lax.axis_index("tp")
        z, y = own // self.side, own % self.side
        offsets = jnp.arange(self.depth * self.side, dtype=jnp.int32)
        a, b = offsets // self.side, offsets % self.side
        both = []
        for sign in (-1, 1):
            deep = (z + sign * a + self.depth) % self.depth
            both.append(deep * self.side + (y + sign * b + self.side) % self.side)
        return jnp.concatenate(both).astype(jnp.int32)


def after(value, *others):
    return lax.optimization_barrier((value, others))[0]


def gather_columns(grid, own):
    columns = {0: own}
    half = grid.depth // 2
    for a in range(1, grid.depth - half + 1):
        columns[a] = grid.send(columns[a - 1], 1, 0)
        back = grid.depth - a
        if back > a:
            columns[back] = grid.send(columns[(back + 1) % grid.depth], -1, 0)
    return columns


def scatter_order(grid):
    order = []
    for a in range(grid.depth - grid.depth // 2, 0, -1):
        if grid.depth - a > a:
            order.append(grid.depth - a)
        order.append(a)
    return order + [0]


def scatter_sum(grid, own_rows, chunks):
    crossed = {
        (a, b): grid.send(chunks[a, b], 0, b)
        for a in scatter_order(grid)
        for b in range(1, grid.side)
    }
    half = grid.depth - grid.depth // 2
    arriving = {}
    for a in scatter_order(grid):
        part = chunks[a, 0].astype(F32)
        for b in range(1, grid.side):
            part = part + crossed[a, b].astype(F32)
        if a == 0:
            total = own_rows.astype(F32) + part
        elif a <= half:
            if a in arriving:
                part = part + arriving[a].astype(F32)
            arriving[a - 1] = grid.send(part.astype(BF16), 1, 0)
        else:
            if a in arriving:
                part = part + arriving[a].astype(F32)
            after = (a + 1) % grid.depth
            moved = grid.send(part.astype(BF16), -1, 0)
            if after == 0:
                last = moved
            else:
                arriving[after] = moved
    if grid.depth > 1:
        total = total + arriving[0].astype(F32)
    if grid.depth > 2:
        total = total + last.astype(F32)
    return total.astype(BF16)


def sum_selectors(grid, partial, arrivals):
    arrivals = list(arrivals)
    rows = partial.shape[0]
    part = rows // grid.side
    own_y = lax.axis_index("tp") % grid.side
    piece = lambda y: lax.dynamic_slice_in_dim(partial, (y % grid.side) * part, part, 0)
    total = piece(own_y).astype(F32)
    for b in range(1, grid.side):
        total = total + grid.send(piece(own_y + b), 0, b).astype(F32)
    bit = 1
    while bit < grid.depth:
        total = after(total.astype(BF16), arrivals.pop(0))
        total = total.astype(F32) + grid.swap(total, bit).astype(F32)
        bit *= 2
    total = after(total.astype(BF16), arrivals.pop(0))
    result = jnp.zeros_like(partial)
    for b in range(grid.side):
        got = grid.send(total, 0, b) if b else total
        place = ((own_y - b + grid.side) % grid.side) * part
        result = lax.dynamic_update_slice_in_dim(result, got, place, 0)
    return result


def per_device(
    n_tp, tokens, norm_gain, w_in, w_low, w_dt, a_rate, dt_bias, skip_gain, threshold, w_out
):
    grid = Grid(n_tp)
    feat = tokens.shape[1]
    layers, width, _, chans = w_in.shape
    states = a_rate.shape[1]
    rank = w_dt.shape[1]
    fold = chans // LANES
    table = grid.table()
    forth = lambda a, b: n_tp + a * grid.side + b
    seq_place = lax.axis_index("seq").astype(jnp.int32).reshape(1)
    own_place = lax.axis_index("tp") * feat
    rates = (a_rate * (-math.log2(math.e))).reshape(layers, states, fold, LANES)
    w_raw = w_in.reshape(layers, width, 2, fold, LANES).transpose(0, 1, 3, 2, 4)
    w_raw = w_raw.reshape(layers, width * 2 * fold, LANES)
    own_gain = lax.dynamic_slice_in_dim(norm_gain, own_place, feat, 1)
    order = scatter_order(grid)
    own_rows = tokens
    for layer in range(layers):
        columns = gather_columns(grid, own_rows)
        arrivals = order[::-1]
        scaled = (own_rows.astype(F32) * own_gain[layer]).astype(BF16)
        low = jnp.dot(scaled, w_low[layer], preferred_element_type=F32).astype(BF16)
        low = sum_selectors(grid, low, [columns[a] for a in arrivals[1:]])
        selectors = low[:, rank:].astype(F32)
        state = None
        squares = []
        for n, a in enumerate(arrivals):
            column = after(columns[a], squares[n - 2]) if n > 1 else columns[a]
            arrived = [column] + [grid.send(column, 0, b) for b in range(1, grid.side)]
            state = project(
                layer, arrived, table, a * grid.side, norm_gain, w_raw, chans, state
            )
            squares.append(state[2])
        cur, gate, square = state
        out, time, final = local_scan(
            layer, width, selectors, low, square, cur, w_dt, dt_bias, rates
        )
        finals = lax.all_gather(final, "seq")
        keys = [(a, b) for a in order for b in range(1, grid.side)]
        keys += [(a, 0) for a in order]
        lead = grid.side - 1
        gated, chunks = close_layer(
            layer,
            width,
            table,
            [forth(*key) for key in keys[:lead]],
            feat,
            seq_place,
            selectors,
            (out, time, cur, gate, square, finals),
            rates,
            skip_gain,
            threshold,
            w_out,
        )
        others = expand(layer, table, [forth(*key) for key in keys[lead:]], feat, gated, w_out)
        own_rows = scatter_sum(grid, own_rows, dict(zip(keys, [*chunks, *others])))
    return own_rows


def solution(mesh):
    in_specs = (
        P("seq", "tp"),
        P(),
        P(None, None, None, "tp"),
        P(None, "tp", None),
        P(None, None, "tp"),
        P(None, None, "tp"),
        P(None, "tp"),
        P(None, "tp"),
        P(None, "tp"),
        P(None, "tp", None),
    )
    return jax.shard_map(
        functools.partial(per_device, mesh.shape["tp"]),
        mesh=mesh,
        in_specs=in_specs,
        out_specs=P("seq", "tp"),
        check_vma=False,
    )
```

```python
import functools
import math

import jax
import jax.numpy as jnp
from jax import lax
from jax.experimental import pallas as pl
from jax.experimental.pallas import tpu as pltpu
from jax.sharding import PartitionSpec as P

LANES = 128
WIDE = 256
STRIDE = 3
EPS = 1e-05
DEPTH = 4
LIMIT = 28 * 1024 * 1024
F32 = jnp.float32
BF16 = jnp.bfloat16
VMEM = pl.BlockSpec(memory_space=pltpu.VMEM)
SMEM = pl.BlockSpec(memory_space=pltpu.SMEM)
HBM = pl.BlockSpec(memory_space=pl.ANY)
COST = pl.CostEstimate(flops=1, bytes_accessed=1, transcendentals=0)
LONG = pl.CostEstimate(flops=10**10, bytes_accessed=1, transcendentals=0)


def row_factor(square_sum, width):
    return lax.rsqrt(square_sum / width + EPS)


def fold_stride(count):
    return STRIDE * count + 1


def params():
    return pltpu.CompilerParams(vmem_limit_bytes=LIMIT)


def unpack_kernel(count, layer, table_at, width, depth, table_ref, w_ref, *refs):
    out_ref, token_ref, raw_s, split_s, sems = refs[-5:]
    chans = out_ref.shape[2]
    per = 2 * chans // LANES
    pieces = width // depth
    size = depth * per
    apart = fold_stride(depth)
    taken = max(per, 16)

    def copy(n):
        begin = table_ref[table_at + n // pieces] * width + (n % pieces) * depth
        rows = pl.ds(pl.multiple_of(begin * per, size), size)
        return pltpu.make_async_copy(w_ref.at[layer, rows, :], raw_s.at[n], sems.at[n])

    for n in range(count * pieces):
        copy(n).start()
    token_ref[...] = jnp.zeros_like(token_ref)
    for n in range(count * pieces):
        copy(n).wait()
        slot = n % 2

        def spread(m, carried):
            values = raw_s[n, pl.ds(pl.multiple_of(m * taken, taken), taken), :].astype(F32)
            for k in range(taken // per):
                d = m * (taken // per) + k
                part = values[k * per : (k + 1) * per]
                split_s[slot, pl.ds(d * STRIDE, per, stride=apart), :] = part
            return carried

        lax.fori_loop(0, size // taken, spread, 0, unroll=32)
        for e in range(2):
            for t in range(chans // LANES):
                place = pl.ds((2 * t + e) * apart, depth, stride=STRIDE)
                values = split_s[slot, place, :].astype(BF16)
                out_ref[e, n * depth : (n + 1) * depth, t * LANES : (t + 1) * LANES] = values


def unpack(layer, table, table_at, count, width, chans, w_raw, earlier):
    depth = min(width, LANES)
    pieces = count * width // depth
    size = depth * 2 * chans // LANES
    return pl.pallas_call(
        functools.partial(unpack_kernel, count, layer, table_at, width, depth),
        out_shape=[
            jax.ShapeDtypeStruct((2, count * width, chans), BF16),
            jax.ShapeDtypeStruct((8, LANES), F32),
        ],
        in_specs=[SMEM, HBM] + [HBM] * len(earlier),
        out_specs=[VMEM, VMEM],
        scratch_shapes=[
            pltpu.VMEM((pieces, size, LANES), BF16),
            pltpu.VMEM((2, 2 * chans // LANES * fold_stride(depth), LANES), F32),
            pltpu.SemaphoreType.DMA((pieces,)),
        ],
        compiler_params=params(),
        cost_estimate=COST,
        name="unpack",
    )(table, w_raw, *earlier)


def proj_kernel(count, first, layer, table_at, table_ref, *refs):
    shards = refs[:count]
    gain_ref, w_ref = refs[count : count + 2]
    cur_ref, gate_ref, square_ref = refs[-3:]
    rows, width = shards[0].shape
    chans = cur_ref.shape[1]
    squares = jnp.zeros((rows, 1), F32) if first else square_ref[...]
    parts = []
    for j in range(count):
        values = shards[j][...].astype(F32)
        begin = pl.multiple_of(table_ref[table_at + j] * width, width)
        parts.append((values * gain_ref[layer : layer + 1, pl.ds(begin, width)]).astype(BF16))
        squares = squares + jnp.sum(values * values, axis=1, keepdims=True)
    square_ref[...] = squares
    left = jnp.concatenate(parts, axis=1)
    for e, out in enumerate((cur_ref, gate_ref)):
        for begin in range(0, chans, WIDE):
            cols = slice(begin, begin + WIDE)
            product = jnp.dot(left, w_ref[e, :, cols], preferred_element_type=F32)
            if first:
                out[:, cols] = product
            else:
                out[:, cols] += product


def project(layer, shards, table, table_at, norm_gain, w_lanes, before, earlier):
    count = len(shards)
    rows, width = shards[0].shape
    chans = w_lanes.shape[2]
    state = [jax.ShapeDtypeStruct(s, F32) for s in ((rows, chans), (rows, chans), (rows, 1))]
    operands = [table, *shards, norm_gain, w_lanes]
    in_specs = [SMEM] + [VMEM] * (count + 2)
    aliases = {}
    if before is not None:
        aliases = {len(operands) + j: j for j in range(3)}
        in_specs += [VMEM] * 3
        operands += list(before)
    in_specs += [HBM] * len(earlier)
    operands += earlier
    return pl.pallas_call(
        functools.partial(proj_kernel, count, before is None, layer, table_at),
        out_shape=state,
        in_specs=in_specs,
        out_specs=[VMEM] * 3,
        input_output_aliases=aliases,
        compiler_params=params(),
        cost_estimate=LONG,
        name="project",
    )(*operands)


def low_kernel(layer, table_ref, rows_ref, gain_ref, w_ref, *refs):
    width = rows_ref.shape[1]
    begin = pl.multiple_of(table_ref[0] * width, width)
    gain = gain_ref[layer : layer + 1, pl.ds(begin, width)]
    scaled = (rows_ref[...].astype(F32) * gain).astype(BF16)
    product = jnp.dot(scaled, w_ref[layer], preferred_element_type=F32)
    refs[-1][...] = product.astype(BF16)


def project_low(layer, table, own_rows, norm_gain, w_low, earlier):
    return pl.pallas_call(
        functools.partial(low_kernel, layer),
        out_shape=jax.ShapeDtypeStruct((own_rows.shape[0], w_low.shape[2]), BF16),
        in_specs=[SMEM] + [VMEM] * 3 + [HBM] * len(earlier),
        out_specs=VMEM,
        compiler_params=params(),
        cost_estimate=COST,
        name="project_low",
    )(table, own_rows, norm_gain, w_low, *earlier)


def scan_kernel(
    layer,
    states,
    width,
    sel_ref,
    low_ref,
    square_ref,
    cur_ref,
    w_dt_ref,
    bias_ref,
    rate_ref,
    out_ref,
    time_ref,
    final_ref,
    step_s,
    drive_s,
):
    rows, chans = cur_ref.shape
    fold = chans // LANES
    rank = w_dt_ref.shape[1]
    factor = row_factor(square_ref[...], width)
    rank_part = (low_ref[:, :rank].astype(F32) * factor).astype(BF16)
    apart = fold_stride(rows)
    twice = factor * factor
    for begin in range(0, chans, WIDE):
        cols = slice(begin, begin + WIDE)
        pre = jnp.dot(rank_part, w_dt_ref[layer, :, cols], preferred_element_type=F32)
        pre = pre + bias_ref[layer : layer + 1, cols]
        step = jnp.maximum(pre, 0.0) + jnp.log1p(jnp.exp(-jnp.abs(pre)))
        drive = step * (cur_ref[:, cols] * twice)
        for q in range(WIDE // LANES):
            part = slice(q * LANES, (q + 1) * LANES)
            place = pl.ds((begin // LANES + q) * apart, rows, stride=STRIDE)
            step_s[place, :] = step[:, part]
            drive_s[place, :] = drive[:, part]

    def advance(t, carried):
        time, held = carried
        here = pl.ds(t * STRIDE, fold, stride=apart)
        step = step_s[here, :]
        drive = drive_s[here, :]
        sums = [None] * 4
        after = []
        for s in range(states):
            decay = jnp.exp2(step * rate_ref[layer, s])
            now = decay * held[s] + drive * sel_ref[t, s]
            term = now * sel_ref[t, states + s]
            sums[s % 4] = term if sums[s % 4] is None else sums[s % 4] + term
            after.append(now)
        time = time + step
        out_ref[here, :] = (sums[0] + sums[1]) + (sums[2] + sums[3])
        time_ref[here, :] = time
        return time, tuple(after)

    zero = jnp.zeros((fold, LANES), F32)
    time, held = lax.fori_loop(0, rows, advance, (zero, (zero,) * states), unroll=4)
    for s in range(states):
        final_ref[s] = held[s].astype(BF16)
    final_ref[states] = time.astype(BF16)


def local_scan(layer, width, selectors, low, square, cur, w_dt, dt_bias, rate):
    rows, chans = cur.shape
    _, states, fold, _ = rate.shape
    folded = (fold * fold_stride(rows), LANES)
    return pl.pallas_call(
        functools.partial(scan_kernel, layer, states, width),
        out_shape=[
            jax.ShapeDtypeStruct(folded, F32),
            jax.ShapeDtypeStruct(folded, F32),
            jax.ShapeDtypeStruct((states + 1, fold, LANES), BF16),
        ],
        in_specs=[SMEM] + [VMEM] * 6,
        out_specs=[VMEM] * 3,
        scratch_shapes=[pltpu.VMEM(folded, F32), pltpu.VMEM(folded, F32)],
        compiler_params=params(),
        cost_estimate=COST,
        name="local_scan",
    )(selectors, low, square, cur, w_dt, dt_bias, rate)


def emit_chunks(layer, table_at, feat, gated_ref, table_ref, w_ref, chunks, w_s, sems, before=None):
    def copy(j):
        begin = pl.multiple_of(table_ref[table_at[j]] * feat, feat)
        return pltpu.make_async_copy(w_ref.at[layer, :, pl.ds(begin, feat)], w_s.at[j], sems.at[j])

    for j in range(len(chunks)):
        copy(j).start()
    if before is not None:
        before()
    for j, chunk in enumerate(chunks):
        copy(j).wait()
        for begin in range(0, feat, WIDE):
            cols = slice(begin, begin + WIDE)
            chunk[:, cols] = jnp.dot(
                gated_ref[...], w_s[j, :, cols], preferred_element_type=F32
            ).astype(BF16)


def close_kernel(layer, states, table_at, feat, width, table_ref, place_ref, sel_ref, *refs):
    out_ref, time_ref, cur_ref, gate_ref, square_ref, final_ref = refs[:6]
    rate_ref, skip_ref, thresh_ref, w_ref, gated_ref = refs[6:11]
    chunks = refs[11 : 11 + len(table_at)]
    enter_s, mixed_s, w_s, sems = refs[-4:]
    rows, chans = cur_ref.shape
    fold = chans // LANES
    apart = fold_stride(rows)

    def gate_all():
        def enter(p, state):
            time = final_ref[p, states].astype(F32)
            return tuple(
                jnp.exp2(time * rate_ref[layer, s]) * state[s] + final_ref[p, s].astype(F32)
                for s in range(states)
            )

        zero = jnp.zeros((fold, LANES), F32)
        state = lax.fori_loop(0, place_ref[0], enter, (zero,) * states)
        for s in range(states):
            enter_s[s] = state[s]

        def correct(t, carried):
            here = pl.ds(t * STRIDE, fold, stride=apart)
            time = time_ref[here, :]
            sums = [out_ref[here, :], None, None, None]
            for s in range(states):
                term = jnp.exp2(time * rate_ref[layer, s]) * (enter_s[s] * sel_ref[t, states + s])
                sums[s % 4] = term if sums[s % 4] is None else sums[s % 4] + term
            mixed_s[here, :] = (sums[0] + sums[1]) + (sums[2] + sums[3])
            return carried

        lax.fori_loop(0, rows, correct, 0, unroll=4)

        factor = row_factor(square_ref[...], width)
        for r in range(fold):
            cols = slice(r * LANES, (r + 1) * LANES)
            skip = skip_ref[layer : layer + 1, cols]
            mixed = mixed_s[pl.ds(r * apart, rows, stride=STRIDE), :] + skip * cur_ref[:, cols]
            mixed = mixed * factor
            normal = mixed * lax.rsqrt(jnp.mean(mixed * mixed, axis=1, keepdims=True) + EPS)
            thresh = thresh_ref[layer : layer + 1, cols]
            shrunk = jnp.maximum(normal - thresh, 0.0) - jnp.maximum(-normal - thresh, 0.0)
            gate = gate_ref[:, cols] * factor
            gated_ref[:, cols] = (shrunk * (gate * jax.nn.sigmoid(gate))).astype(BF16)

    emit_chunks(layer, table_at, feat, gated_ref, table_ref, w_ref, chunks, w_s, sems, gate_all)


def close_layer(
    layer, width, table, table_at, feat, seq_place, selectors, values, rate, skip, thresh, w_out
):
    rows, chans = values[2].shape
    _, states, fold, _ = rate.shape
    count = len(table_at)
    chunk = jax.ShapeDtypeStruct((rows, feat), BF16)
    results = pl.pallas_call(
        functools.partial(close_kernel, layer, states, table_at, feat, width),
        out_shape=[jax.ShapeDtypeStruct((rows, chans), BF16)] + [chunk] * count,
        in_specs=[SMEM] * 3 + [VMEM] * 9 + [HBM],
        out_specs=[VMEM] * (1 + count),
        scratch_shapes=[
            pltpu.VMEM((states, fold, LANES), F32),
            pltpu.VMEM((fold * fold_stride(rows), LANES), F32),
            pltpu.VMEM((count, chans, feat), BF16),
            pltpu.SemaphoreType.DMA((count,)),
        ],
        compiler_params=params(),
        cost_estimate=COST,
        name="close_layer",
    )(table, seq_place, selectors, *values, rate, skip, thresh, w_out)
    return results[0], results[1:]


def expand_kernel(layer, table_at, feat, table_ref, gated_ref, w_ref, *refs):
    chunks = refs[: len(table_at)]
    emit_chunks(layer, table_at, feat, gated_ref, table_ref, w_ref, chunks, *refs[-2:])


def expand(layer, table, table_at, feat, gated, w_out):
    rows, chans = gated.shape
    count = len(table_at)
    return pl.pallas_call(
        functools.partial(expand_kernel, layer, table_at, feat),
        out_shape=[jax.ShapeDtypeStruct((rows, feat), BF16)] * count,
        in_specs=[SMEM, VMEM, HBM],
        out_specs=[VMEM] * count,
        scratch_shapes=[
            pltpu.VMEM((count, chans, feat), BF16),
            pltpu.SemaphoreType.DMA((count,)),
        ],
        compiler_params=params(),
        cost_estimate=COST,
        name="expand",
    )(table, gated, w_out)


class Grid:
    def __init__(self, count):
        self.depth = DEPTH if count % DEPTH == 0 else 1
        self.side = count // self.depth

    def places(self):
        return [(z, y) for z in range(self.depth) for y in range(self.side)]

    def at(self, z, y):
        return (z % self.depth) * self.side + y % self.side

    def send(self, value, deep, across):
        pairs = [(self.at(z, y), self.at(z + deep, y + across)) for z, y in self.places()]
        return lax.ppermute(value, "tp", pairs)

    def swap(self, value, bit):
        pairs = [(self.at(z, y), self.at(z ^ bit, y)) for z, y in self.places()]
        return lax.ppermute(value, "tp", pairs)

    def table(self):
        own = lax.axis_index("tp")
        z, y = own // self.side, own % self.side
        offsets = jnp.arange(self.depth * self.side, dtype=jnp.int32)
        a, b = offsets // self.side, offsets % self.side
        both = []
        for sign in (-1, 1):
            deep = (z + sign * a + self.depth) % self.depth
            both.append(deep * self.side + (y + sign * b + self.side) % self.side)
        return jnp.concatenate(both).astype(jnp.int32)


def gather_columns(grid, own):
    columns = {0: own}
    half = grid.depth // 2
    for a in range(1, grid.depth - half + 1):
        columns[a] = grid.send(columns[a - 1], 1, 0)
        back = grid.depth - a
        if back > a:
            columns[back] = grid.send(columns[(back + 1) % grid.depth], -1, 0)
    return columns


def scatter_order(grid):
    order = []
    for a in range(grid.depth - grid.depth // 2, 0, -1):
        if grid.depth - a > a:
            order.append(grid.depth - a)
        order.append(a)
    return order + [0]


def scatter_sum(grid, own_rows, chunks, aside):
    crossed = {
        (a, b): grid.send(chunks[a, b], 0, b)
        for a in scatter_order(grid)
        for b in range(1, grid.side)
    }
    half = grid.depth - grid.depth // 2
    arriving = {}
    waiting = ()
    for a in scatter_order(grid):
        part = chunks[a, 0].astype(F32)
        for b in range(1, grid.side):
            part = part + crossed[a, b].astype(F32)
        others = waiting
        waiting = aside(a, crossed.get((a, 1), chunks[a, 0]))
        for token in others:
            part = part + token[0, 0]
        if a == 0:
            total = own_rows.astype(F32) + part
        elif a <= half:
            if a in arriving:
                part = part + arriving[a].astype(F32)
            arriving[a - 1] = grid.send(part.astype(BF16), 1, 0)
        else:
            if a in arriving:
                part = part + arriving[a].astype(F32)
            target = (a + 1) % grid.depth
            moved = grid.send(part.astype(BF16), -1, 0)
            if target == 0:
                last = moved
            else:
                arriving[target] = moved
    for token in waiting:
        total = total + token[0, 0]
    if grid.depth > 1:
        total = total + arriving[0].astype(F32)
    if grid.depth > 2:
        total = total + last.astype(F32)
    return total.astype(BF16)


def sum_selectors(grid, partial):
    rows = partial.shape[0]
    part = rows // grid.side
    own_y = lax.axis_index("tp") % grid.side
    piece = lambda y: lax.dynamic_slice_in_dim(partial, (y % grid.side) * part, part, 0)
    total = piece(own_y).astype(F32)
    for b in range(1, grid.side):
        total = total + grid.send(piece(own_y + b), 0, b).astype(F32)
    bit = 1
    stages = []
    while bit < grid.depth:
        total = total.astype(BF16)
        stages.append(total)
        total = total.astype(F32) + grid.swap(total, bit).astype(F32)
        bit *= 2
    total = total.astype(BF16)
    stages.append(total)
    result = jnp.zeros_like(partial)
    for b in range(grid.side):
        got = grid.send(total, 0, b) if b else total
        place = ((own_y - b + grid.side) % grid.side) * part
        result = lax.dynamic_update_slice_in_dim(result, got, place, 0)
    return result, stages


def per_device(
    n_tp, tokens, norm_gain, w_in, w_low, w_dt, a_rate, dt_bias, skip_gain, threshold, w_out
):
    grid = Grid(n_tp)
    feat = tokens.shape[1]
    layers, width, _, chans = w_in.shape
    states = a_rate.shape[1]
    rank = w_dt.shape[1]
    fold = chans // LANES
    table = grid.table()
    forth = lambda a, b: n_tp + a * grid.side + b
    seq_place = lax.axis_index("seq").astype(jnp.int32).reshape(1)
    rates = (a_rate * (-math.log2(math.e))).reshape(layers, states, fold, LANES)
    w_raw = w_in.reshape(layers, width, 2, fold, LANES).transpose(0, 1, 3, 2, 4)
    w_raw = w_raw.reshape(layers, width * 2 * fold, LANES)
    order = scatter_order(grid)
    own_rows = tokens
    open_weights = lambda layer, a, earlier: unpack(
        layer, table, a * grid.side, grid.side, feat, chans, w_raw, earlier
    )
    weights = {}
    arrivals = order[::-1]
    for layer in range(layers):
        columns = gather_columns(grid, own_rows)
        across = {
            a: [columns[a]] + [grid.send(columns[a], 0, b) for b in range(1, grid.side)]
            for a in arrivals
        }
        earlier = [*across[0][1:], columns[arrivals[1]]]
        if not weights:
            weights[0], token = open_weights(layer, 0, [])
            earlier.append(token)
        low = project_low(layer, table, own_rows, norm_gain, w_low, earlier)
        low, stages = sum_selectors(grid, low)
        selectors = low[:, rank:].astype(F32)
        state = None
        for n, a in enumerate(arrivals):
            if a not in weights:
                weights[a], _ = open_weights(layer, a, across[arrivals[n - 1]][1:])
            earlier = stages[n - 1 : n] if n else []
            state = project(
                layer, across[a], table, a * grid.side, norm_gain, weights[a], state, earlier
            )
        cur, gate, square = state
        out, time, final = local_scan(
            layer, width, selectors, low, square, cur, w_dt, dt_bias, rates
        )
        finals = lax.all_gather(final, "seq")
        keys = [(a, b) for a in order for b in range(1, grid.side)]
        keys += [(a, 0) for a in order]
        lead = grid.side - 1
        gated, chunks = close_layer(
            layer,
            width,
            table,
            [forth(*key) for key in keys[:lead]],
            feat,
            seq_place,
            selectors,
            (out, time, cur, gate, square, finals),
            rates,
            skip_gain,
            threshold,
            w_out,
        )
        others = expand(layer, table, [forth(*key) for key in keys[lead:]], feat, gated, w_out)
        coming = {}

        def aside(a, value):
            if layer + 1 == layers:
                return ()
            a = grid.depth - 1 - a
            coming[a], token = open_weights(layer + 1, a, [value])
            return (token,)

        own_rows = scatter_sum(grid, own_rows, dict(zip(keys, [*chunks, *others])), aside)
        weights = coming
    return own_rows


def solution(mesh):
    in_specs = (
        P("seq", "tp"),
        P(),
        P(None, None, None, "tp"),
        P(None, "tp", None),
        P(None, None, "tp"),
        P(None, None, "tp"),
        P(None, "tp"),
        P(None, "tp"),
        P(None, "tp"),
        P(None, "tp", None),
    )
    return jax.shard_map(
        functools.partial(per_device, mesh.shape["tp"]),
        mesh=mesh,
        in_specs=in_specs,
        out_specs=P("seq", "tp"),
        check_vma=False,
    )
```

```python
import functools
import math

import jax
import jax.numpy as jnp
from jax import lax
from jax.experimental import pallas as pl
from jax.experimental.pallas import tpu as pltpu
from jax.sharding import PartitionSpec as P

LANES = 128
WIDE = 256
STRIDE = 3
EPS = 1e-05
DEPTH = 4
LIMIT = 40 * 1024 * 1024
F32 = jnp.float32
BF16 = jnp.bfloat16
VMEM = pl.BlockSpec(memory_space=pltpu.VMEM)
SMEM = pl.BlockSpec(memory_space=pltpu.SMEM)
HBM = pl.BlockSpec(memory_space=pltpu.HBM)
ANY = pl.BlockSpec(memory_space=pl.ANY)
COST = pl.CostEstimate(flops=1, bytes_accessed=1, transcendentals=0)
LONG = pl.CostEstimate(flops=10**10, bytes_accessed=1, transcendentals=0)


def row_factor(square_sum, width):
    return lax.rsqrt(square_sum / width + EPS)


def fold_stride(count):
    return STRIDE * count + 1


def params():
    return pltpu.CompilerParams(vmem_limit_bytes=LIMIT)


def proj_kernel(count, first, layer, table_at, with_low, table_ref, *refs):
    shards = refs[:count]
    gain_ref, w_ref = refs[count : count + 2]
    low_w_ref = refs[count + 2] if with_low else None
    raw_s, split_s, sems = refs[-3:]
    cur_ref, gate_ref, square_ref = refs[-6 - with_low : -3 - with_low]
    rows, width = shards[0].shape
    chans = cur_ref.shape[1]
    pieces, size, _ = raw_s.shape
    pieces //= count
    per = 2 * chans // LANES
    depth = size // per
    apart = fold_stride(depth)
    taken = max(per, 16)
    places = [table_ref[table_at + j] for j in range(count)]

    def copy(j, q):
        n = j * pieces + q
        begin = (places[j] * width + q * depth) * per
        source = w_ref.at[layer, pl.ds(pl.multiple_of(begin, size), size), :]
        return pltpu.make_async_copy(source, raw_s.at[n], sems.at[n])

    for j in range(count):
        for q in range(pieces):
            copy(j, q).start()
    squares = jnp.zeros((rows, 1), F32) if first else square_ref[...]
    for j in range(count):
        values = shards[j][...].astype(F32)
        gain = gain_ref[layer : layer + 1, pl.ds(pl.multiple_of(places[j] * width, width), width)]
        left = (values * gain).astype(BF16)
        squares = squares + jnp.sum(values * values, axis=1, keepdims=True)
        if with_low:
            low_ref = refs[-4]
            term = lax.dot_general(
                left, low_w_ref[places[j]], (((1,), (1,)), ((), ())), preferred_element_type=F32
            )
            if first and j == 0:
                low_ref[...] = term
            else:
                low_ref[...] += term
        for q in range(pieces):
            copy(j, q).wait()
            slot = (j * pieces + q) % split_s.shape[0]
            for begin in range(0, size, taken):
                part = raw_s[j * pieces + q, begin : begin + taken, :].astype(F32)
                for k in range(taken // per):
                    d = begin // per + k
                    place = pl.ds(d * STRIDE, per, stride=apart)
                    split_s[slot, place, :] = part[k * per : (k + 1) * per]
        for e, out in enumerate((cur_ref, gate_ref)):
            for begin in range(0, chans, WIDE):
                tiles = [
                    jnp.concatenate(
                        [
                            split_s[
                                (j * pieces + q) % split_s.shape[0],
                                pl.ds((2 * t + e) * apart, depth, stride=STRIDE),
                                :,
                            ].astype(BF16)
                            for q in range(pieces)
                        ],
                        axis=0,
                    )
                    for t in range(begin // LANES, (begin + WIDE) // LANES)
                ]
                product = jnp.dot(left, jnp.concatenate(tiles, axis=1), preferred_element_type=F32)
                cols = slice(begin, begin + WIDE)
                if first and j == 0:
                    out[:, cols] = product
                else:
                    out[:, cols] += product
    square_ref[...] = squares


def project(layer, shards, table, table_at, norm_gain, w_raw, chans, low_w, before, earlier):
    count = len(shards)
    rows, width = shards[0].shape
    with_low = low_w is not None
    depth = min(width, WIDE)
    pieces = count * (width // depth)
    per = 2 * chans // LANES
    shapes = [(rows, chans), (rows, chans), (rows, 1)]
    operands = [table, *shards, norm_gain, w_raw]
    in_specs = [SMEM] + [VMEM] * (count + 1) + [HBM]
    if with_low:
        shapes.append((rows, low_w.shape[1]))
        operands.append(low_w)
        in_specs.append(VMEM)
    aliases = {}
    if before is not None:
        aliases = {len(operands) + j: j for j in range(len(shapes))}
        in_specs += [VMEM] * len(shapes)
        operands += list(before)
    in_specs += [ANY] * len(earlier)
    operands += earlier
    return pl.pallas_call(
        functools.partial(proj_kernel, count, before is None, layer, table_at, with_low),
        out_shape=[jax.ShapeDtypeStruct(shape, F32) for shape in shapes],
        in_specs=in_specs,
        out_specs=[VMEM] * len(shapes),
        scratch_shapes=[
            pltpu.VMEM((pieces, depth * per, LANES), BF16),
            pltpu.VMEM((pieces, per * fold_stride(depth), LANES), F32),
            pltpu.SemaphoreType.DMA((pieces,)),
        ],
        input_output_aliases=aliases,
        compiler_params=params(),
        cost_estimate=LONG,
        name="project",
    )(*operands)


def low_kernel(layer, table_ref, rows_ref, gain_ref, w_ref, *refs):
    width = rows_ref.shape[1]
    begin = pl.multiple_of(table_ref[0] * width, width)
    gain = gain_ref[layer : layer + 1, pl.ds(begin, width)]
    scaled = (rows_ref[...].astype(F32) * gain).astype(BF16)
    product = lax.dot_general(
        scaled, w_ref[layer], (((1,), (1,)), ((), ())), preferred_element_type=F32
    )
    refs[-1][...] = product.astype(BF16)


def project_low(layer, table, own_rows, norm_gain, w_low, earlier):
    return pl.pallas_call(
        functools.partial(low_kernel, layer),
        out_shape=jax.ShapeDtypeStruct((own_rows.shape[0], w_low.shape[1]), BF16),
        in_specs=[SMEM] + [VMEM] * 3 + [ANY] * len(earlier),
        out_specs=VMEM,
        compiler_params=params(),
        cost_estimate=COST,
        name="project_low",
    )(table, own_rows, norm_gain, w_low, *earlier)


def scan_kernel(
    layer,
    states,
    width,
    sel_ref,
    low_ref,
    square_ref,
    cur_ref,
    w_dt_ref,
    bias_ref,
    rate_ref,
    out_ref,
    time_ref,
    final_ref,
    step_s,
    drive_s,
):
    rows, chans = cur_ref.shape
    fold = chans // LANES
    rank = w_dt_ref.shape[1]
    factor = row_factor(square_ref[...], width)
    rank_part = (low_ref[:, :rank].astype(F32) * factor).astype(BF16)
    apart = fold_stride(rows)
    twice = factor * factor
    for begin in range(0, chans, WIDE):
        cols = slice(begin, begin + WIDE)
        pre = jnp.dot(rank_part, w_dt_ref[layer, :, cols], preferred_element_type=F32)
        pre = pre + bias_ref[layer : layer + 1, cols]
        step = jnp.maximum(pre, 0.0) + jnp.log1p(jnp.exp(-jnp.abs(pre)))
        drive = step * (cur_ref[:, cols] * twice)
        for q in range(WIDE // LANES):
            part = slice(q * LANES, (q + 1) * LANES)
            place = pl.ds((begin // LANES + q) * apart, rows, stride=STRIDE)
            step_s[place, :] = step[:, part]
            drive_s[place, :] = drive[:, part]

    def advance(t, carried):
        time, held = carried
        here = pl.ds(t * STRIDE, fold, stride=apart)
        step = step_s[here, :]
        drive = drive_s[here, :]
        sums = [None] * 4
        after = []
        for s in range(states):
            decay = jnp.exp2(step * rate_ref[layer, s])
            now = decay * held[s] + drive * sel_ref[t, s]
            term = now * sel_ref[t, states + s]
            sums[s % 4] = term if sums[s % 4] is None else sums[s % 4] + term
            after.append(now)
        time = time + step
        out_ref[here, :] = (sums[0] + sums[1]) + (sums[2] + sums[3])
        time_ref[here, :] = time
        return time, tuple(after)

    zero = jnp.zeros((fold, LANES), F32)
    time, held = lax.fori_loop(0, rows, advance, (zero, (zero,) * states), unroll=4)
    for s in range(states):
        final_ref[s] = held[s].astype(BF16)
    final_ref[states] = time.astype(BF16)


def local_scan(layer, width, selectors, low, square, cur, w_dt, dt_bias, rate):
    rows, chans = cur.shape
    _, states, fold, _ = rate.shape
    folded = (fold * fold_stride(rows), LANES)
    return pl.pallas_call(
        functools.partial(scan_kernel, layer, states, width),
        out_shape=[
            jax.ShapeDtypeStruct(folded, F32),
            jax.ShapeDtypeStruct(folded, F32),
            jax.ShapeDtypeStruct((states + 1, fold, LANES), BF16),
        ],
        in_specs=[SMEM] + [VMEM] * 6,
        out_specs=[VMEM] * 3,
        scratch_shapes=[pltpu.VMEM(folded, F32), pltpu.VMEM(folded, F32)],
        compiler_params=params(),
        cost_estimate=COST,
        name="local_scan",
    )(selectors, low, square, cur, w_dt, dt_bias, rate)


def emit_chunks(layer, table_at, feat, gated_ref, table_ref, w_ref, chunks, w_s, sems, before=None):
    def copy(j):
        begin = pl.multiple_of(table_ref[table_at[j]] * feat, feat)
        return pltpu.make_async_copy(w_ref.at[layer, :, pl.ds(begin, feat)], w_s.at[j], sems.at[j])

    for j in range(len(chunks)):
        copy(j).start()
    if before is not None:
        before()
    for j, chunk in enumerate(chunks):
        copy(j).wait()
        for begin in range(0, feat, WIDE):
            cols = slice(begin, begin + WIDE)
            chunk[:, cols] = jnp.dot(
                gated_ref[...], w_s[j, :, cols], preferred_element_type=F32
            ).astype(BF16)


def close_kernel(layer, states, table_at, feat, width, table_ref, place_ref, sel_ref, *refs):
    out_ref, time_ref, cur_ref, gate_ref, square_ref, final_ref = refs[:6]
    rate_ref, skip_ref, thresh_ref, w_ref, gated_ref = refs[6:11]
    chunks = refs[11 : 11 + len(table_at)]
    enter_s, mixed_s, w_s, sems = refs[-4:]
    rows, chans = cur_ref.shape
    fold = chans // LANES
    apart = fold_stride(rows)

    def gate_all():
        def enter(p, state):
            time = final_ref[p, states].astype(F32)
            return tuple(
                jnp.exp2(time * rate_ref[layer, s]) * state[s] + final_ref[p, s].astype(F32)
                for s in range(states)
            )

        zero = jnp.zeros((fold, LANES), F32)
        state = lax.fori_loop(0, place_ref[0], enter, (zero,) * states)
        for s in range(states):
            enter_s[s] = state[s]

        def correct(t, carried):
            here = pl.ds(t * STRIDE, fold, stride=apart)
            time = time_ref[here, :]
            sums = [out_ref[here, :], None, None, None]
            for s in range(states):
                term = jnp.exp2(time * rate_ref[layer, s]) * (enter_s[s] * sel_ref[t, states + s])
                sums[s % 4] = term if sums[s % 4] is None else sums[s % 4] + term
            mixed_s[here, :] = (sums[0] + sums[1]) + (sums[2] + sums[3])
            return carried

        lax.fori_loop(0, rows, correct, 0, unroll=4)

        factor = row_factor(square_ref[...], width)
        for r in range(fold):
            cols = slice(r * LANES, (r + 1) * LANES)
            skip = skip_ref[layer : layer + 1, cols]
            mixed = mixed_s[pl.ds(r * apart, rows, stride=STRIDE), :] + skip * cur_ref[:, cols]
            mixed = mixed * factor
            normal = mixed * lax.rsqrt(jnp.mean(mixed * mixed, axis=1, keepdims=True) + EPS)
            thresh = thresh_ref[layer : layer + 1, cols]
            shrunk = jnp.maximum(normal - thresh, 0.0) - jnp.maximum(-normal - thresh, 0.0)
            gate = gate_ref[:, cols] * factor
            gated_ref[:, cols] = (shrunk * (gate * jax.nn.sigmoid(gate))).astype(BF16)

    emit_chunks(layer, table_at, feat, gated_ref, table_ref, w_ref, chunks, w_s, sems, gate_all)


def close_layer(
    layer, width, table, table_at, feat, seq_place, selectors, values, rate, skip, thresh, w_out
):
    rows, chans = values[2].shape
    _, states, fold, _ = rate.shape
    count = len(table_at)
    chunk = jax.ShapeDtypeStruct((rows, feat), BF16)
    results = pl.pallas_call(
        functools.partial(close_kernel, layer, states, table_at, feat, width),
        out_shape=[jax.ShapeDtypeStruct((rows, chans), BF16)] + [chunk] * count,
        in_specs=[SMEM] * 3 + [VMEM] * 9 + [HBM],
        out_specs=[VMEM] * (1 + count),
        scratch_shapes=[
            pltpu.VMEM((states, fold, LANES), F32),
            pltpu.VMEM((fold * fold_stride(rows), LANES), F32),
            pltpu.VMEM((count, chans, feat), BF16),
            pltpu.SemaphoreType.DMA((count,)),
        ],
        compiler_params=params(),
        cost_estimate=COST,
        name="close_layer",
    )(table, seq_place, selectors, *values, rate, skip, thresh, w_out)
    return results[0], results[1:]


def expand_kernel(layer, table_at, feat, table_ref, gated_ref, w_ref, *refs):
    chunks = refs[: len(table_at)]
    emit_chunks(layer, table_at, feat, gated_ref, table_ref, w_ref, chunks, *refs[-2:])


def expand(layer, table, table_at, feat, gated, w_out):
    rows, chans = gated.shape
    count = len(table_at)
    return pl.pallas_call(
        functools.partial(expand_kernel, layer, table_at, feat),
        out_shape=[jax.ShapeDtypeStruct((rows, feat), BF16)] * count,
        in_specs=[SMEM, VMEM, HBM],
        out_specs=[VMEM] * count,
        scratch_shapes=[
            pltpu.VMEM((count, chans, feat), BF16),
            pltpu.SemaphoreType.DMA((count,)),
        ],
        compiler_params=params(),
        cost_estimate=COST,
        name="expand",
    )(table, gated, w_out)


class Grid:
    def __init__(self, count):
        self.depth = DEPTH if count % DEPTH == 0 else 1
        self.side = count // self.depth

    def places(self):
        return [(z, y) for z in range(self.depth) for y in range(self.side)]

    def at(self, z, y):
        return (z % self.depth) * self.side + y % self.side

    def send(self, value, deep, across):
        pairs = [(self.at(z, y), self.at(z + deep, y + across)) for z, y in self.places()]
        return lax.ppermute(value, "tp", pairs)

    def swap(self, value, bit):
        pairs = [(self.at(z, y), self.at(z ^ bit, y)) for z, y in self.places()]
        return lax.ppermute(value, "tp", pairs)

    def table(self):
        own = lax.axis_index("tp")
        z, y = own // self.side, own % self.side
        offsets = jnp.arange(self.depth * self.side, dtype=jnp.int32)
        a, b = offsets // self.side, offsets % self.side
        both = []
        for sign in (-1, 1):
            deep = (z + sign * a + self.depth) % self.depth
            both.append(deep * self.side + (y + sign * b + self.side) % self.side)
        return jnp.concatenate(both).astype(jnp.int32)


def gather_columns(grid, own):
    columns = {0: own}
    half = grid.depth // 2
    for a in range(1, grid.depth - half + 1):
        columns[a] = grid.send(columns[a - 1], 1, 0)
        back = grid.depth - a
        if back > a:
            columns[back] = grid.send(columns[(back + 1) % grid.depth], -1, 0)
    return columns


def scatter_order(grid):
    order = []
    for a in range(grid.depth - grid.depth // 2, 0, -1):
        if grid.depth - a > a:
            order.append(grid.depth - a)
        order.append(a)
    return order + [0]


def scatter_sum(grid, own_rows, chunks):
    crossed = {
        (a, b): grid.send(chunks[a, b], 0, b)
        for a in scatter_order(grid)
        for b in range(1, grid.side)
    }
    half = grid.depth - grid.depth // 2
    arriving = {}
    for a in scatter_order(grid):
        part = chunks[a, 0].astype(F32)
        for b in range(1, grid.side):
            part = part + crossed[a, b].astype(F32)
        if a == 0:
            total = own_rows.astype(F32) + part
        elif a <= half:
            if a in arriving:
                part = part + arriving[a].astype(F32)
            arriving[a - 1] = grid.send(part.astype(BF16), 1, 0)
        else:
            if a in arriving:
                part = part + arriving[a].astype(F32)
            target = (a + 1) % grid.depth
            moved = grid.send(part.astype(BF16), -1, 0)
            if target == 0:
                last = moved
            else:
                arriving[target] = moved
    if grid.depth > 1:
        total = total + arriving[0].astype(F32)
    if grid.depth > 2:
        total = total + last.astype(F32)
    return total.astype(BF16)


def sum_selectors(grid, partial):
    rows = partial.shape[0]
    part = rows // grid.side
    own_y = lax.axis_index("tp") % grid.side
    piece = lambda y: lax.dynamic_slice_in_dim(partial, (y % grid.side) * part, part, 0)
    total = piece(own_y).astype(F32)
    for b in range(1, grid.side):
        total = total + grid.send(piece(own_y + b), 0, b).astype(F32)
    bit = 1
    stages = []
    while bit < grid.depth:
        total = total.astype(BF16)
        stages.append(total)
        total = total.astype(F32) + grid.swap(total, bit).astype(F32)
        bit *= 2
    total = total.astype(BF16)
    stages.append(total)
    result = jnp.zeros_like(partial)
    for b in range(grid.side):
        got = grid.send(total, 0, b) if b else total
        place = ((own_y - b + grid.side) % grid.side) * part
        result = lax.dynamic_update_slice_in_dim(result, got, place, 0)
    return result, stages


def per_device(
    n_tp, tokens, norm_gain, w_in, w_low, w_dt, a_rate, dt_bias, skip_gain, threshold, w_out
):
    grid = Grid(n_tp)
    feat = tokens.shape[1]
    layers, width, _, chans = w_in.shape
    states = a_rate.shape[1]
    rank = w_dt.shape[1]
    fold = chans // LANES
    table = grid.table()
    forth = lambda a, b: n_tp + a * grid.side + b
    seq_place = lax.axis_index("seq").astype(jnp.int32).reshape(1)
    rates = (a_rate * (-math.log2(math.e))).reshape(layers, states, fold, LANES)
    w_raw = w_in.reshape(layers, width, 2, fold, LANES).transpose(0, 1, 3, 2, 4)
    w_raw = w_raw.reshape(layers, width * 2 * fold, LANES)
    order = scatter_order(grid)
    own_rows = tokens
    low_t = jnp.swapaxes(w_low, 1, 2)
    low_all = [None] + [lax.all_gather(low_t[layer], "tp") for layer in range(1, layers)]
    arrivals = order[::-1]
    for layer in range(layers):
        columns = gather_columns(grid, own_rows)
        across = {
            a: [columns[a]] + [grid.send(columns[a], 0, b) for b in range(1, grid.side)]
            for a in arrivals
        }
        stages = []
        if low_all[layer] is None:
            earlier = [*across[0][1:], columns[arrivals[1]]]
            low = project_low(layer, table, own_rows, norm_gain, low_t, earlier)
            low, stages = sum_selectors(grid, low)
        state = None
        for n, a in enumerate(arrivals):
            earlier = stages[n - 1 : n] if n else []
            state = project(
                layer,
                across[a],
                table,
                a * grid.side,
                norm_gain,
                w_raw,
                chans,
                low_all[layer],
                state,
                earlier,
            )
        if low_all[layer] is not None:
            *state, low = state
        selectors = low[:, rank:].astype(F32)
        cur, gate, square = state
        out, time, final = local_scan(
            layer, width, selectors, low, square, cur, w_dt, dt_bias, rates
        )
        finals = lax.all_gather(final, "seq")
        keys = [(a, b) for a in order for b in range(1, grid.side)]
        keys += [(a, 0) for a in order]
        lead = grid.side - 1
        gated, chunks = close_layer(
            layer,
            width,
            table,
            [forth(*key) for key in keys[:lead]],
            feat,
            seq_place,
            selectors,
            (out, time, cur, gate, square, finals),
            rates,
            skip_gain,
            threshold,
            w_out,
        )
        others = expand(layer, table, [forth(*key) for key in keys[lead:]], feat, gated, w_out)
        own_rows = scatter_sum(grid, own_rows, dict(zip(keys, [*chunks, *others])))
    return own_rows


def solution(mesh):
    in_specs = (
        P("seq", "tp"),
        P(),
        P(None, None, None, "tp"),
        P(None, "tp", None),
        P(None, None, "tp"),
        P(None, None, "tp"),
        P(None, "tp"),
        P(None, "tp"),
        P(None, "tp"),
        P(None, "tp", None),
    )
    return jax.shard_map(
        functools.partial(per_device, mesh.shape["tp"]),
        mesh=mesh,
        in_specs=in_specs,
        out_specs=P("seq", "tp"),
        check_vma=False,
    )
```

```python
import functools
import math

import jax
import jax.numpy as jnp
from jax import lax
from jax.experimental import pallas as pl
from jax.experimental.pallas import tpu as pltpu
from jax.sharding import PartitionSpec as P

LANES = 128
WIDE = 256
STRIDE = 3
EPS = 1e-05
DEPTH = 4
LIMIT = 40 * 1024 * 1024
F32 = jnp.float32
BF16 = jnp.bfloat16
VMEM = pl.BlockSpec(memory_space=pltpu.VMEM)
SMEM = pl.BlockSpec(memory_space=pltpu.SMEM)
HBM = pl.BlockSpec(memory_space=pltpu.HBM)
ANY = pl.BlockSpec(memory_space=pl.ANY)
COST = pl.CostEstimate(flops=1, bytes_accessed=1, transcendentals=0)
LONG = pl.CostEstimate(flops=10**10, bytes_accessed=1, transcendentals=0)


def row_factor(square_sum, width):
    return lax.rsqrt(square_sum / width + EPS)


def fold_stride(count):
    return STRIDE * count + 1


def params():
    return pltpu.CompilerParams(vmem_limit_bytes=LIMIT)


def proj_kernel(count, first, layer, table_at, with_low, table_ref, *refs):
    shards = refs[:count]
    gain_ref, w_ref = refs[count : count + 2]
    low_w_ref = refs[count + 2] if with_low else None
    raw_s, split_s, sems = refs[-3:]
    cur_ref, gate_ref, square_ref = refs[-6 - with_low : -3 - with_low]
    rows, width = shards[0].shape
    chans = cur_ref.shape[1]
    pieces, size, _ = raw_s.shape
    pieces //= count
    per = 2 * chans // LANES
    depth = size // per
    apart = fold_stride(depth)
    taken = max(per, 16)
    places = [table_ref[table_at + j] for j in range(count)]

    def copy(j, q):
        n = j * pieces + q
        begin = (places[j] * width + q * depth) * per
        source = w_ref.at[layer, pl.ds(pl.multiple_of(begin, size), size), :]
        return pltpu.make_async_copy(source, raw_s.at[n], sems.at[n])

    for j in range(count):
        for q in range(pieces):
            copy(j, q).start()
    squares = jnp.zeros((rows, 1), F32) if first else square_ref[...]
    for j in range(count):
        values = shards[j][...].astype(F32)
        gain = gain_ref[layer : layer + 1, pl.ds(pl.multiple_of(places[j] * width, width), width)]
        left = (values * gain).astype(BF16)
        squares = squares + jnp.sum(values * values, axis=1, keepdims=True)
        if with_low:
            low_ref = refs[-4]
            term = lax.dot_general(
                left, low_w_ref[places[j]], (((1,), (1,)), ((), ())), preferred_element_type=F32
            )
            if first and j == 0:
                low_ref[...] = term
            else:
                low_ref[...] += term
        for q in range(pieces):
            copy(j, q).wait()
            slot = (j * pieces + q) % split_s.shape[0]
            for begin in range(0, size, taken):
                part = raw_s[j * pieces + q, begin : begin + taken, :].astype(F32)
                for k in range(taken // per):
                    d = begin // per + k
                    place = pl.ds(d * STRIDE, per, stride=apart)
                    split_s[slot, place, :] = part[k * per : (k + 1) * per]
        for e, out in enumerate((cur_ref, gate_ref)):
            for begin in range(0, chans, WIDE):
                tiles = [
                    jnp.concatenate(
                        [
                            split_s[
                                (j * pieces + q) % split_s.shape[0],
                                pl.ds((2 * t + e) * apart, depth, stride=STRIDE),
                                :,
                            ].astype(BF16)
                            for q in range(pieces)
                        ],
                        axis=0,
                    )
                    for t in range(begin // LANES, (begin + WIDE) // LANES)
                ]
                product = jnp.dot(left, jnp.concatenate(tiles, axis=1), preferred_element_type=F32)
                cols = slice(begin, begin + WIDE)
                if first and j == 0:
                    out[:, cols] = product
                else:
                    out[:, cols] += product
    square_ref[...] = squares


def project(layer, shards, table, table_at, norm_gain, w_raw, chans, low_w, before, earlier):
    count = len(shards)
    rows, width = shards[0].shape
    with_low = low_w is not None
    depth = min(width, WIDE)
    pieces = count * (width // depth)
    per = 2 * chans // LANES
    shapes = [(rows, chans), (rows, chans), (rows, 1)]
    operands = [table, *shards, norm_gain, w_raw]
    in_specs = [SMEM] + [VMEM] * (count + 1) + [HBM]
    if with_low:
        shapes.append((rows, low_w.shape[1]))
        operands.append(low_w)
        in_specs.append(VMEM)
    aliases = {}
    if before is not None:
        aliases = {len(operands) + j: j for j in range(len(shapes))}
        in_specs += [VMEM] * len(shapes)
        operands += list(before)
    in_specs += [ANY] * len(earlier)
    operands += earlier
    return pl.pallas_call(
        functools.partial(proj_kernel, count, before is None, layer, table_at, with_low),
        out_shape=[jax.ShapeDtypeStruct(shape, F32) for shape in shapes],
        in_specs=in_specs,
        out_specs=[VMEM] * len(shapes),
        scratch_shapes=[
            pltpu.VMEM((pieces, depth * per, LANES), BF16),
            pltpu.VMEM((pieces, per * fold_stride(depth), LANES), F32),
            pltpu.SemaphoreType.DMA((pieces,)),
        ],
        input_output_aliases=aliases,
        compiler_params=params(),
        cost_estimate=LONG,
        name="project",
    )(*operands)


def low_kernel(layer, table_ref, rows_ref, gain_ref, w_ref, *refs):
    width = rows_ref.shape[1]
    begin = pl.multiple_of(table_ref[0] * width, width)
    gain = gain_ref[layer : layer + 1, pl.ds(begin, width)]
    scaled = (rows_ref[...].astype(F32) * gain).astype(BF16)
    product = lax.dot_general(
        scaled, w_ref[layer], (((1,), (1,)), ((), ())), preferred_element_type=F32
    )
    refs[-1][...] = product.astype(BF16)


def project_low(layer, table, own_rows, norm_gain, w_low, earlier):
    return pl.pallas_call(
        functools.partial(low_kernel, layer),
        out_shape=jax.ShapeDtypeStruct((own_rows.shape[0], w_low.shape[1]), BF16),
        in_specs=[SMEM] + [VMEM] * 3 + [ANY] * len(earlier),
        out_specs=VMEM,
        compiler_params=params(),
        cost_estimate=COST,
        name="project_low",
    )(table, own_rows, norm_gain, w_low, *earlier)


def scan_kernel(
    layer,
    states,
    width,
    sel_ref,
    low_ref,
    square_ref,
    cur_ref,
    w_dt_ref,
    bias_ref,
    rate_ref,
    out_ref,
    time_ref,
    final_ref,
    step_s,
    drive_s,
):
    rows, chans = cur_ref.shape
    fold = chans // LANES
    rank = w_dt_ref.shape[1]
    factor = row_factor(square_ref[...], width)
    rank_part = (low_ref[:, :rank] * factor).astype(BF16)
    apart = fold_stride(rows)
    twice = factor * factor
    for begin in range(0, chans, WIDE):
        cols = slice(begin, begin + WIDE)
        pre = jnp.dot(rank_part, w_dt_ref[layer, :, cols], preferred_element_type=F32)
        pre = pre + bias_ref[layer : layer + 1, cols]
        step = jnp.maximum(pre, 0.0) + jnp.log1p(jnp.exp(-jnp.abs(pre)))
        drive = step * (cur_ref[:, cols] * twice)
        for q in range(WIDE // LANES):
            part = slice(q * LANES, (q + 1) * LANES)
            place = pl.ds((begin // LANES + q) * apart, rows, stride=STRIDE)
            step_s[place, :] = step[:, part]
            drive_s[place, :] = drive[:, part]

    def advance(t, carried):
        time, held = carried
        here = pl.ds(t * STRIDE, fold, stride=apart)
        step = step_s[here, :]
        drive = drive_s[here, :]
        sums = [None] * 4
        after = []
        for s in range(states):
            decay = jnp.exp2(step * rate_ref[layer, s])
            now = decay * held[s] + drive * sel_ref[t, s]
            term = now * sel_ref[t, states + s]
            sums[s % 4] = term if sums[s % 4] is None else sums[s % 4] + term
            after.append(now)
        time = time + step
        out_ref[here, :] = (sums[0] + sums[1]) + (sums[2] + sums[3])
        time_ref[here, :] = time
        return time, tuple(after)

    zero = jnp.zeros((fold, LANES), F32)
    time, held = lax.fori_loop(0, rows, advance, (zero, (zero,) * states), unroll=4)
    for s in range(states):
        final_ref[s] = held[s].astype(BF16)
    final_ref[states] = time.astype(BF16)


def local_scan(layer, width, selectors, low, square, cur, w_dt, dt_bias, rate):
    rows, chans = cur.shape
    _, states, fold, _ = rate.shape
    folded = (fold * fold_stride(rows), LANES)
    return pl.pallas_call(
        functools.partial(scan_kernel, layer, states, width),
        out_shape=[
            jax.ShapeDtypeStruct(folded, F32),
            jax.ShapeDtypeStruct(folded, F32),
            jax.ShapeDtypeStruct((states + 1, fold, LANES), BF16),
        ],
        in_specs=[SMEM] + [VMEM] * 6,
        out_specs=[VMEM] * 3,
        scratch_shapes=[pltpu.VMEM(folded, F32), pltpu.VMEM(folded, F32)],
        compiler_params=params(),
        cost_estimate=COST,
        name="local_scan",
    )(selectors, low, square, cur, w_dt, dt_bias, rate)


def emit_chunks(layer, table_at, feat, gated_ref, table_ref, w_ref, chunks, w_s, sems, before=None):
    def copy(j):
        begin = pl.multiple_of(table_ref[table_at[j]] * feat, feat)
        return pltpu.make_async_copy(w_ref.at[layer, :, pl.ds(begin, feat)], w_s.at[j], sems.at[j])

    for j in range(len(chunks)):
        copy(j).start()
    if before is not None:
        before()
    for j, chunk in enumerate(chunks):
        copy(j).wait()
        for begin in range(0, feat, WIDE):
            cols = slice(begin, begin + WIDE)
            chunk[:, cols] = jnp.dot(
                gated_ref[...], w_s[j, :, cols], preferred_element_type=F32
            ).astype(BF16)


def close_kernel(layer, states, table_at, feat, width, table_ref, place_ref, sel_ref, *refs):
    out_ref, time_ref, cur_ref, gate_ref, square_ref, final_ref = refs[:6]
    rate_ref, skip_ref, thresh_ref, w_ref, gated_ref = refs[6:11]
    chunks = refs[11 : 11 + len(table_at)]
    enter_s, mixed_s, w_s, sems = refs[-4:]
    rows, chans = cur_ref.shape
    fold = chans // LANES
    apart = fold_stride(rows)

    def gate_all():
        def enter(p, state):
            time = final_ref[p, states].astype(F32)
            return tuple(
                jnp.exp2(time * rate_ref[layer, s]) * state[s] + final_ref[p, s].astype(F32)
                for s in range(states)
            )

        zero = jnp.zeros((fold, LANES), F32)
        state = lax.fori_loop(0, place_ref[0], enter, (zero,) * states)
        for s in range(states):
            enter_s[s] = state[s]

        def correct(t, carried):
            here = pl.ds(t * STRIDE, fold, stride=apart)
            time = time_ref[here, :]
            sums = [out_ref[here, :], None, None, None]
            for s in range(states):
                term = jnp.exp2(time * rate_ref[layer, s]) * (enter_s[s] * sel_ref[t, states + s])
                sums[s % 4] = term if sums[s % 4] is None else sums[s % 4] + term
            mixed_s[here, :] = (sums[0] + sums[1]) + (sums[2] + sums[3])
            return carried

        lax.fori_loop(0, rows, correct, 0, unroll=4)

        factor = row_factor(square_ref[...], width)
        for r in range(fold):
            cols = slice(r * LANES, (r + 1) * LANES)
            skip = skip_ref[layer : layer + 1, cols]
            mixed = mixed_s[pl.ds(r * apart, rows, stride=STRIDE), :] + skip * cur_ref[:, cols]
            mixed = mixed * factor
            normal = mixed * lax.rsqrt(jnp.mean(mixed * mixed, axis=1, keepdims=True) + EPS)
            thresh = thresh_ref[layer : layer + 1, cols]
            shrunk = jnp.maximum(normal - thresh, 0.0) - jnp.maximum(-normal - thresh, 0.0)
            gate = gate_ref[:, cols] * factor
            gated_ref[:, cols] = (shrunk * (gate * jax.nn.sigmoid(gate))).astype(BF16)

    emit_chunks(layer, table_at, feat, gated_ref, table_ref, w_ref, chunks, w_s, sems, gate_all)


def close_layer(
    layer, width, table, table_at, feat, seq_place, selectors, values, rate, skip, thresh, w_out
):
    rows, chans = values[2].shape
    _, states, fold, _ = rate.shape
    count = len(table_at)
    chunk = jax.ShapeDtypeStruct((rows, feat), BF16)
    results = pl.pallas_call(
        functools.partial(close_kernel, layer, states, table_at, feat, width),
        out_shape=[jax.ShapeDtypeStruct((rows, chans), BF16)] + [chunk] * count,
        in_specs=[SMEM] * 3 + [VMEM] * 9 + [HBM],
        out_specs=[VMEM] * (1 + count),
        scratch_shapes=[
            pltpu.VMEM((states, fold, LANES), F32),
            pltpu.VMEM((fold * fold_stride(rows), LANES), F32),
            pltpu.VMEM((count, chans, feat), BF16),
            pltpu.SemaphoreType.DMA((count,)),
        ],
        compiler_params=params(),
        cost_estimate=COST,
        name="close_layer",
    )(table, seq_place, selectors, *values, rate, skip, thresh, w_out)
    return results[0], results[1:]


def expand_kernel(layer, table_at, feat, table_ref, gated_ref, w_ref, *refs):
    chunks = refs[: len(table_at)]
    emit_chunks(layer, table_at, feat, gated_ref, table_ref, w_ref, chunks, *refs[-2:])


def expand(layer, table, table_at, feat, gated, w_out):
    rows, chans = gated.shape
    count = len(table_at)
    return pl.pallas_call(
        functools.partial(expand_kernel, layer, table_at, feat),
        out_shape=[jax.ShapeDtypeStruct((rows, feat), BF16)] * count,
        in_specs=[SMEM, VMEM, HBM],
        out_specs=[VMEM] * count,
        scratch_shapes=[
            pltpu.VMEM((count, chans, feat), BF16),
            pltpu.SemaphoreType.DMA((count,)),
        ],
        compiler_params=params(),
        cost_estimate=COST,
        name="expand",
    )(table, gated, w_out)


class Grid:
    def __init__(self, count):
        self.depth = DEPTH if count % DEPTH == 0 else 1
        self.side = count // self.depth

    def places(self):
        return [(z, y) for z in range(self.depth) for y in range(self.side)]

    def at(self, z, y):
        return (z % self.depth) * self.side + y % self.side

    def send(self, value, deep, across):
        pairs = [(self.at(z, y), self.at(z + deep, y + across)) for z, y in self.places()]
        return lax.ppermute(value, "tp", pairs)

    def swap(self, value, bit):
        pairs = [(self.at(z, y), self.at(z ^ bit, y)) for z, y in self.places()]
        return lax.ppermute(value, "tp", pairs)

    def table(self):
        own = lax.axis_index("tp")
        z, y = own // self.side, own % self.side
        offsets = jnp.arange(self.depth * self.side, dtype=jnp.int32)
        a, b = offsets // self.side, offsets % self.side
        both = []
        for sign in (-1, 1):
            deep = (z + sign * a + self.depth) % self.depth
            both.append(deep * self.side + (y + sign * b + self.side) % self.side)
        return jnp.concatenate(both).astype(jnp.int32)


def gather_columns(grid, own):
    columns = {0: own}
    half = grid.depth // 2
    for a in range(1, grid.depth - half + 1):
        back = grid.depth - a
        if back > a:
            columns[back] = grid.send(columns[(back + 1) % grid.depth], -1, 0)
        before = columns[a - 1]
        if a > 1:
            before = hold(before, columns[grid.depth - a + 1])
        columns[a] = grid.send(before, 1, 0)
    return columns


def scatter_order(grid):
    order = []
    for a in range(grid.depth - grid.depth // 2, 0, -1):
        if grid.depth - a > a:
            order.append(grid.depth - a)
        order.append(a)
    return order + [0]


def scatter_sum(grid, own_rows, chunks):
    crossed = {
        (a, b): grid.send(chunks[a, b], 0, b)
        for a in scatter_order(grid)
        for b in range(1, grid.side)
    }
    half = grid.depth - grid.depth // 2
    arriving = {}
    for a in scatter_order(grid):
        part = chunks[a, 0].astype(F32)
        for b in range(1, grid.side):
            part = part + crossed[a, b].astype(F32)
        if a == 0:
            total = own_rows.astype(F32) + part
        elif a <= half:
            if a in arriving:
                part = part + arriving[a].astype(F32)
            arriving[a - 1] = grid.send(part.astype(BF16), 1, 0)
        else:
            if a in arriving:
                part = part + arriving[a].astype(F32)
            target = (a + 1) % grid.depth
            moved = grid.send(part.astype(BF16), -1, 0)
            if target == 0:
                last = moved
            else:
                arriving[target] = moved
    if grid.depth > 1:
        total = total + arriving[0].astype(F32)
    if grid.depth > 2:
        total = total + last.astype(F32)
    return total.astype(BF16)


def sum_selectors(grid, partial):
    total = partial.astype(F32)
    for b in range(1, grid.side):
        total = total + grid.send(partial, 0, b).astype(F32)
    stages = []
    bit = 1
    while bit < grid.depth:
        rounded = total.astype(BF16)
        stages.append(rounded)
        total = rounded.astype(F32) + grid.swap(rounded, bit).astype(F32)
        bit *= 2
    return total, stages


def hold(value, *others):
    nothing = sum(other[(0,) * other.ndim].astype(F32) * 0.0 for other in others)
    return (value.astype(F32) + nothing).astype(value.dtype)


def per_device(
    n_tp, tokens, norm_gain, w_in, w_low, w_dt, a_rate, dt_bias, skip_gain, threshold, w_out
):
    grid = Grid(n_tp)
    feat = tokens.shape[1]
    layers, width, _, chans = w_in.shape
    states = a_rate.shape[1]
    rank = w_dt.shape[1]
    fold = chans // LANES
    table = grid.table()
    forth = lambda a, b: n_tp + a * grid.side + b
    seq_place = lax.axis_index("seq").astype(jnp.int32).reshape(1)
    rates = (a_rate * (-math.log2(math.e))).reshape(layers, states, fold, LANES)
    w_raw = w_in.reshape(layers, width, 2, fold, LANES).transpose(0, 1, 3, 2, 4)
    w_raw = w_raw.reshape(layers, width * 2 * fold, LANES)
    order = scatter_order(grid)
    own_rows = tokens
    low_t = jnp.swapaxes(w_low, 1, 2)
    arrivals = order[::-1]
    for layer in range(layers):
        columns = gather_columns(grid, own_rows)
        cross = lambda column: [grid.send(column, 0, b) for b in range(1, grid.side)]
        beside = {0: cross(own_rows)}
        low = project_low(layer, table, own_rows, norm_gain, low_t, beside[0])
        low, stages = sum_selectors(grid, low)
        selectors = low[:, rank:]
        state = None
        squares = []
        for n, a in enumerate(arrivals):
            if n:
                beside[a] = cross(hold(columns[a], squares[n - 2]) if n > 1 else columns[a])
            state = project(
                layer,
                [columns[a], *beside[a]],
                table,
                a * grid.side,
                norm_gain,
                w_raw,
                chans,
                None,
                state,
                stages[n - 1 : n] if n else [],
            )
            squares.append(state[2])
        cur, gate, square = state
        out, time, final = local_scan(
            layer, width, selectors, low, square, cur, w_dt, dt_bias, rates
        )
        finals = lax.all_gather(final, "seq")
        keys = [(a, b) for a in order for b in range(1, grid.side)]
        keys += [(a, 0) for a in order]
        lead = grid.side - 1
        gated, chunks = close_layer(
            layer,
            width,
            table,
            [forth(*key) for key in keys[:lead]],
            feat,
            seq_place,
            selectors,
            (out, time, cur, gate, square, finals),
            rates,
            skip_gain,
            threshold,
            w_out,
        )
        others = expand(layer, table, [forth(*key) for key in keys[lead:]], feat, gated, w_out)
        own_rows = scatter_sum(grid, own_rows, dict(zip(keys, [*chunks, *others])))
    return own_rows


def solution(mesh):
    in_specs = (
        P("seq", "tp"),
        P(),
        P(None, None, None, "tp"),
        P(None, "tp", None),
        P(None, None, "tp"),
        P(None, None, "tp"),
        P(None, "tp"),
        P(None, "tp"),
        P(None, "tp"),
        P(None, "tp", None),
    )
    return jax.shard_map(
        functools.partial(per_device, mesh.shape["tp"]),
        mesh=mesh,
        in_specs=in_specs,
        out_specs=P("seq", "tp"),
        check_vma=False,
    )
```

```python
import functools
import math

import jax
import jax.numpy as jnp
from jax import lax
from jax.experimental import pallas as pl
from jax.experimental.pallas import tpu as pltpu
from jax.sharding import PartitionSpec as P

LANES = 128
WIDE = 256
STRIDE = 3
EPS = 1e-05
DEPTH = 4
LIMIT = 40 * 1024 * 1024
F32 = jnp.float32
BF16 = jnp.bfloat16
VMEM = pl.BlockSpec(memory_space=pltpu.VMEM)
SMEM = pl.BlockSpec(memory_space=pltpu.SMEM)
HBM = pl.BlockSpec(memory_space=pltpu.HBM)
ANY = pl.BlockSpec(memory_space=pl.ANY)
COST = pl.CostEstimate(flops=1, bytes_accessed=1, transcendentals=0)
LONG = pl.CostEstimate(flops=10**10, bytes_accessed=1, transcendentals=0)


def row_factor(square_sum, width):
    return lax.rsqrt(square_sum / width + EPS)


def fold_stride(count):
    return STRIDE * count + 1


def params():
    return pltpu.CompilerParams(vmem_limit_bytes=LIMIT)


def proj_kernel(count, first, layer, table_at, with_low, table_ref, *refs):
    shards = refs[:count]
    gain_ref, w_ref = refs[count : count + 2]
    low_w_ref = refs[count + 2] if with_low else None
    raw_s, split_s, sems = refs[-3:]
    cur_ref, gate_ref, square_ref = refs[-6 - with_low : -3 - with_low]
    rows, width = shards[0].shape
    chans = cur_ref.shape[1]
    pieces, size, _ = raw_s.shape
    pieces //= count
    per = 2 * chans // LANES
    depth = size // per
    apart = fold_stride(depth)
    taken = max(per, 16)
    places = [table_ref[table_at + j] for j in range(count)]

    def copy(j, q):
        n = j * pieces + q
        begin = (places[j] * width + q * depth) * per
        source = w_ref.at[layer, pl.ds(pl.multiple_of(begin, size), size), :]
        return pltpu.make_async_copy(source, raw_s.at[n], sems.at[n])

    for j in range(count):
        for q in range(pieces):
            copy(j, q).start()
    squares = jnp.zeros((rows, 1), F32) if first else square_ref[...]
    for j in range(count):
        values = shards[j][...].astype(F32)
        gain = gain_ref[layer : layer + 1, pl.ds(pl.multiple_of(places[j] * width, width), width)]
        left = (values * gain).astype(BF16)
        squares = squares + jnp.sum(values * values, axis=1, keepdims=True)
        if with_low:
            low_ref = refs[-4]
            term = lax.dot_general(
                left, low_w_ref[places[j]], (((1,), (1,)), ((), ())), preferred_element_type=F32
            )
            if first and j == 0:
                low_ref[...] = term
            else:
                low_ref[...] += term
        for q in range(pieces):
            copy(j, q).wait()
            slot = (j * pieces + q) % split_s.shape[0]
            for begin in range(0, size, taken):
                part = raw_s[j * pieces + q, begin : begin + taken, :].astype(F32)
                for k in range(taken // per):
                    d = begin // per + k
                    place = pl.ds(d * STRIDE, per, stride=apart)
                    split_s[slot, place, :] = part[k * per : (k + 1) * per]
        for e, out in enumerate((cur_ref, gate_ref)):
            for begin in range(0, chans, WIDE):
                tiles = [
                    jnp.concatenate(
                        [
                            split_s[
                                (j * pieces + q) % split_s.shape[0],
                                pl.ds((2 * t + e) * apart, depth, stride=STRIDE),
                                :,
                            ].astype(BF16)
                            for q in range(pieces)
                        ],
                        axis=0,
                    )
                    for t in range(begin // LANES, (begin + WIDE) // LANES)
                ]
                product = jnp.dot(left, jnp.concatenate(tiles, axis=1), preferred_element_type=F32)
                cols = slice(begin, begin + WIDE)
                if first and j == 0:
                    out[:, cols] = product
                else:
                    out[:, cols] += product
    square_ref[...] = squares


def project(layer, shards, table, table_at, norm_gain, w_raw, chans, low_w, before, earlier):
    count = len(shards)
    rows, width = shards[0].shape
    with_low = low_w is not None
    depth = min(width, WIDE)
    pieces = count * (width // depth)
    per = 2 * chans // LANES
    shapes = [(rows, chans), (rows, chans), (rows, 1)]
    operands = [table, *shards, norm_gain, w_raw]
    in_specs = [SMEM] + [VMEM] * (count + 1) + [HBM]
    if with_low:
        shapes.append((rows, low_w.shape[1]))
        operands.append(low_w)
        in_specs.append(VMEM)
    aliases = {}
    if before is not None:
        aliases = {len(operands) + j: j for j in range(len(shapes))}
        in_specs += [VMEM] * len(shapes)
        operands += list(before)
    in_specs += [ANY] * len(earlier)
    operands += earlier
    return pl.pallas_call(
        functools.partial(proj_kernel, count, before is None, layer, table_at, with_low),
        out_shape=[jax.ShapeDtypeStruct(shape, F32) for shape in shapes],
        in_specs=in_specs,
        out_specs=[VMEM] * len(shapes),
        scratch_shapes=[
            pltpu.VMEM((pieces, depth * per, LANES), BF16),
            pltpu.VMEM((pieces, per * fold_stride(depth), LANES), F32),
            pltpu.SemaphoreType.DMA((pieces,)),
        ],
        input_output_aliases=aliases,
        compiler_params=params(),
        cost_estimate=LONG,
        name="project",
    )(*operands)


def low_kernel(layer, table_ref, rows_ref, gain_ref, w_ref, *refs):
    width = rows_ref.shape[1]
    begin = pl.multiple_of(table_ref[0] * width, width)
    gain = gain_ref[layer : layer + 1, pl.ds(begin, width)]
    scaled = (rows_ref[...].astype(F32) * gain).astype(BF16)
    product = lax.dot_general(
        scaled, w_ref[layer], (((1,), (1,)), ((), ())), preferred_element_type=F32
    )
    refs[-1][...] = product.astype(BF16)


def project_low(layer, table, own_rows, norm_gain, w_low, earlier):
    return pl.pallas_call(
        functools.partial(low_kernel, layer),
        out_shape=jax.ShapeDtypeStruct((own_rows.shape[0], w_low.shape[1]), BF16),
        in_specs=[SMEM] + [VMEM] * 3 + [ANY] * len(earlier),
        out_specs=VMEM,
        compiler_params=params(),
        cost_estimate=COST,
        name="project_low",
    )(table, own_rows, norm_gain, w_low, *earlier)


def relay_kernel(value_ref, *refs):
    refs[-1][...] = value_ref[...]


def relay(value, *others):
    return pl.pallas_call(
        relay_kernel,
        out_shape=jax.ShapeDtypeStruct(value.shape, value.dtype),
        in_specs=[VMEM] + [ANY] * len(others),
        out_specs=VMEM,
        compiler_params=params(),
        cost_estimate=COST,
        name="relay",
    )(value, *others)


def scan_kernel(
    layer,
    states,
    width,
    sel_ref,
    low_ref,
    square_ref,
    cur_ref,
    w_dt_ref,
    bias_ref,
    rate_ref,
    out_ref,
    time_ref,
    final_ref,
    step_s,
    drive_s,
):
    rows, chans = cur_ref.shape
    fold = chans // LANES
    rank = w_dt_ref.shape[1]
    factor = row_factor(square_ref[...], width)
    rank_part = (low_ref[:, :rank] * factor).astype(BF16)
    apart = fold_stride(rows)
    twice = factor * factor
    for begin in range(0, chans, WIDE):
        cols = slice(begin, begin + WIDE)
        pre = jnp.dot(rank_part, w_dt_ref[layer, :, cols], preferred_element_type=F32)
        pre = pre + bias_ref[layer : layer + 1, cols]
        step = jnp.maximum(pre, 0.0) + jnp.log1p(jnp.exp(-jnp.abs(pre)))
        drive = step * (cur_ref[:, cols] * twice)
        for q in range(WIDE // LANES):
            part = slice(q * LANES, (q + 1) * LANES)
            place = pl.ds((begin // LANES + q) * apart, rows, stride=STRIDE)
            step_s[place, :] = step[:, part]
            drive_s[place, :] = drive[:, part]

    def advance(t, carried):
        time, held = carried
        here = pl.ds(t * STRIDE, fold, stride=apart)
        step = step_s[here, :]
        drive = drive_s[here, :]
        sums = [None] * 4
        after = []
        for s in range(states):
            decay = jnp.exp2(step * rate_ref[layer, s])
            now = decay * held[s] + drive * sel_ref[t, s]
            term = now * sel_ref[t, states + s]
            sums[s % 4] = term if sums[s % 4] is None else sums[s % 4] + term
            after.append(now)
        time = time + step
        out_ref[here, :] = (sums[0] + sums[1]) + (sums[2] + sums[3])
        time_ref[here, :] = time
        return time, tuple(after)

    zero = jnp.zeros((fold, LANES), F32)
    time, held = lax.fori_loop(0, rows, advance, (zero, (zero,) * states), unroll=8)
    for s in range(states):
        final_ref[s] = held[s].astype(BF16)
    final_ref[states] = time.astype(BF16)


def local_scan(layer, width, selectors, low, square, cur, w_dt, dt_bias, rate):
    rows, chans = cur.shape
    _, states, fold, _ = rate.shape
    folded = (fold * fold_stride(rows), LANES)
    return pl.pallas_call(
        functools.partial(scan_kernel, layer, states, width),
        out_shape=[
            jax.ShapeDtypeStruct(folded, F32),
            jax.ShapeDtypeStruct(folded, F32),
            jax.ShapeDtypeStruct((states + 1, fold, LANES), BF16),
        ],
        in_specs=[SMEM] + [VMEM] * 6,
        out_specs=[VMEM] * 3,
        scratch_shapes=[pltpu.VMEM(folded, F32), pltpu.VMEM(folded, F32)],
        compiler_params=params(),
        cost_estimate=COST,
        name="local_scan",
    )(selectors, low, square, cur, w_dt, dt_bias, rate)


def emit_chunks(layer, table_at, feat, gated_ref, table_ref, w_ref, chunks, w_s, sems, before=None):
    def copy(j):
        begin = pl.multiple_of(table_ref[table_at[j]] * feat, feat)
        return pltpu.make_async_copy(w_ref.at[layer, :, pl.ds(begin, feat)], w_s.at[j], sems.at[j])

    for j in range(len(chunks)):
        copy(j).start()
    if before is not None:
        before()
    for j, chunk in enumerate(chunks):
        copy(j).wait()
        for begin in range(0, feat, WIDE):
            cols = slice(begin, begin + WIDE)
            chunk[:, cols] = jnp.dot(
                gated_ref[...], w_s[j, :, cols], preferred_element_type=F32
            ).astype(BF16)


def close_kernel(layer, states, table_at, feat, width, table_ref, place_ref, sel_ref, *refs):
    out_ref, time_ref, cur_ref, gate_ref, square_ref, final_ref = refs[:6]
    rate_ref, skip_ref, thresh_ref, w_ref, gated_ref = refs[6:11]
    chunks = refs[11 : 11 + len(table_at)]
    enter_s, mixed_s, w_s, sems = refs[-4:]
    rows, chans = cur_ref.shape
    fold = chans // LANES
    apart = fold_stride(rows)

    def gate_all():
        def enter(p, state):
            time = final_ref[p, states].astype(F32)
            return tuple(
                jnp.exp2(time * rate_ref[layer, s]) * state[s] + final_ref[p, s].astype(F32)
                for s in range(states)
            )

        zero = jnp.zeros((fold, LANES), F32)
        state = lax.fori_loop(0, place_ref[0], enter, (zero,) * states)
        for s in range(states):
            enter_s[s] = state[s]

        def correct(t, carried):
            here = pl.ds(t * STRIDE, fold, stride=apart)
            time = time_ref[here, :]
            sums = [out_ref[here, :], None, None, None]
            for s in range(states):
                term = jnp.exp2(time * rate_ref[layer, s]) * (enter_s[s] * sel_ref[t, states + s])
                sums[s % 4] = term if sums[s % 4] is None else sums[s % 4] + term
            mixed_s[here, :] = (sums[0] + sums[1]) + (sums[2] + sums[3])
            return carried

        lax.fori_loop(0, rows, correct, 0, unroll=8)

        factor = row_factor(square_ref[...], width)
        for r in range(fold):
            cols = slice(r * LANES, (r + 1) * LANES)
            skip = skip_ref[layer : layer + 1, cols]
            mixed = mixed_s[pl.ds(r * apart, rows, stride=STRIDE), :] + skip * cur_ref[:, cols]
            mixed = mixed * factor
            normal = mixed * lax.rsqrt(jnp.mean(mixed * mixed, axis=1, keepdims=True) + EPS)
            thresh = thresh_ref[layer : layer + 1, cols]
            shrunk = jnp.maximum(normal - thresh, 0.0) - jnp.maximum(-normal - thresh, 0.0)
            gate = gate_ref[:, cols] * factor
            gated_ref[:, cols] = (shrunk * (gate * jax.nn.sigmoid(gate))).astype(BF16)

    emit_chunks(layer, table_at, feat, gated_ref, table_ref, w_ref, chunks, w_s, sems, gate_all)


def close_layer(
    layer, width, table, table_at, feat, seq_place, selectors, values, rate, skip, thresh, w_out
):
    rows, chans = values[2].shape
    _, states, fold, _ = rate.shape
    count = len(table_at)
    chunk = jax.ShapeDtypeStruct((rows, feat), BF16)
    results = pl.pallas_call(
        functools.partial(close_kernel, layer, states, table_at, feat, width),
        out_shape=[jax.ShapeDtypeStruct((rows, chans), BF16)] + [chunk] * count,
        in_specs=[SMEM] * 3 + [VMEM] * 9 + [HBM],
        out_specs=[VMEM] * (1 + count),
        scratch_shapes=[
            pltpu.VMEM((states, fold, LANES), F32),
            pltpu.VMEM((fold * fold_stride(rows), LANES), F32),
            pltpu.VMEM((count, chans, feat), BF16),
            pltpu.SemaphoreType.DMA((count,)),
        ],
        compiler_params=params(),
        cost_estimate=COST,
        name="close_layer",
    )(table, seq_place, selectors, *values, rate, skip, thresh, w_out)
    return results[0], results[1:]


def expand_kernel(layer, table_at, feat, table_ref, gated_ref, w_ref, *refs):
    chunks = refs[: len(table_at)]
    emit_chunks(layer, table_at, feat, gated_ref, table_ref, w_ref, chunks, *refs[-2:])


def expand(layer, table, table_at, feat, gated, w_out):
    rows, chans = gated.shape
    count = len(table_at)
    return pl.pallas_call(
        functools.partial(expand_kernel, layer, table_at, feat),
        out_shape=[jax.ShapeDtypeStruct((rows, feat), BF16)] * count,
        in_specs=[SMEM, VMEM, HBM],
        out_specs=[VMEM] * count,
        scratch_shapes=[
            pltpu.VMEM((count, chans, feat), BF16),
            pltpu.SemaphoreType.DMA((count,)),
        ],
        compiler_params=params(),
        cost_estimate=COST,
        name="expand",
    )(table, gated, w_out)


class Grid:
    def __init__(self, count):
        self.depth = DEPTH if count % DEPTH == 0 else 1
        self.side = count // self.depth

    def places(self):
        return [(z, y) for z in range(self.depth) for y in range(self.side)]

    def at(self, z, y):
        return (z % self.depth) * self.side + y % self.side

    def send(self, value, deep, across):
        pairs = [(self.at(z, y), self.at(z + deep, y + across)) for z, y in self.places()]
        return lax.ppermute(value, "tp", pairs)

    def swap(self, value, bit):
        pairs = [(self.at(z, y), self.at(z ^ bit, y)) for z, y in self.places()]
        return lax.ppermute(value, "tp", pairs)

    def table(self):
        own = lax.axis_index("tp")
        z, y = own // self.side, own % self.side
        offsets = jnp.arange(self.depth * self.side, dtype=jnp.int32)
        a, b = offsets // self.side, offsets % self.side
        both = []
        for sign in (-1, 1):
            deep = (z + sign * a + self.depth) % self.depth
            both.append(deep * self.side + (y + sign * b + self.side) % self.side)
        return jnp.concatenate(both).astype(jnp.int32)


def gather_columns(grid, own):
    columns = {0: own}
    half = grid.depth // 2
    for a in range(1, grid.depth - half + 1):
        columns[a] = grid.send(columns[a - 1], 1, 0)
        back = grid.depth - a
        if back > a:
            columns[back] = grid.send(columns[(back + 1) % grid.depth], -1, 0)
    return columns


def scatter_order(grid):
    order = []
    for a in range(grid.depth - grid.depth // 2, 0, -1):
        order.append(a)
        if grid.depth - a > a:
            order.append(grid.depth - a)
    return order + [0]


def scatter_sum(grid, own_rows, chunks):
    crossed = {
        (a, b): grid.send(chunks[a, b], 0, b)
        for a in scatter_order(grid)
        for b in range(1, grid.side)
    }
    half = grid.depth - grid.depth // 2
    arriving = {}
    for a in scatter_order(grid):
        part = chunks[a, 0].astype(F32)
        for b in range(1, grid.side):
            part = part + crossed[a, b].astype(F32)
        if a == 0:
            total = own_rows.astype(F32) + part
        elif a <= half:
            if a in arriving:
                part = part + arriving[a].astype(F32)
            arriving[a - 1] = grid.send(part.astype(BF16), 1, 0)
        else:
            if a in arriving:
                part = part + arriving[a].astype(F32)
            target = (a + 1) % grid.depth
            moved = grid.send(part.astype(BF16), -1, 0)
            if target == 0:
                last = moved
            else:
                arriving[target] = moved
    if grid.depth > 1:
        total = total + arriving[0].astype(F32)
    if grid.depth > 2:
        total = total + last.astype(F32)
    return total.astype(BF16)


def sum_selectors(grid, partial):
    total = partial.astype(F32)
    for b in range(1, grid.side):
        total = total + grid.send(partial, 0, b).astype(F32)
    stages = []
    bit = 1
    while bit < grid.depth:
        rounded = total.astype(BF16)
        stages.append(rounded)
        total = rounded.astype(F32) + grid.swap(rounded, bit).astype(F32)
        bit *= 2
    return total, stages


def per_device(
    n_tp, tokens, norm_gain, w_in, w_low, w_dt, a_rate, dt_bias, skip_gain, threshold, w_out
):
    grid = Grid(n_tp)
    feat = tokens.shape[1]
    layers, width, _, chans = w_in.shape
    states = a_rate.shape[1]
    rank = w_dt.shape[1]
    fold = chans // LANES
    table = grid.table()
    forth = lambda a, b: n_tp + a * grid.side + b
    seq_place = lax.axis_index("seq").astype(jnp.int32).reshape(1)
    rates = (a_rate * (-math.log2(math.e))).reshape(layers, states, fold, LANES)
    w_raw = w_in.reshape(layers, width, 2, fold, LANES).transpose(0, 1, 3, 2, 4)
    w_raw = w_raw.reshape(layers, width * 2 * fold, LANES)
    order = scatter_order(grid)
    own_rows = tokens
    low_t = jnp.swapaxes(w_low, 1, 2)
    arrivals = [0] + [a for a in order if a not in (0, order[0])] + order[:1]
    for layer in range(layers):
        columns = gather_columns(grid, own_rows)
        cross = lambda column: [grid.send(column, 0, b) for b in range(1, grid.side)]
        beside = {0: cross(own_rows)}
        low = project_low(layer, table, own_rows, norm_gain, low_t, beside[0])
        low, stages = sum_selectors(grid, low)
        selectors = low[:, rank:]
        state = None
        for n, a in enumerate(arrivals):
            if n:
                last = n + 1 == len(arrivals)
                beside[a] = cross(relay(columns[a], first) if last else columns[a])
            state = project(
                layer,
                [columns[a], *beside[a]],
                table,
                a * grid.side,
                norm_gain,
                w_raw,
                chans,
                None,
                state,
                stages[n - 1 : n] if n else [],
            )
            if n == 0:
                first = state[2]
        cur, gate, square = state
        out, time, final = local_scan(
            layer, width, selectors, low, square, cur, w_dt, dt_bias, rates
        )
        finals = lax.all_gather(final, "seq")
        keys = [(a, b) for a in order for b in range(1, grid.side)]
        keys += [(a, 0) for a in order]
        lead = grid.side - 1
        gated, chunks = close_layer(
            layer,
            width,
            table,
            [forth(*key) for key in keys[:lead]],
            feat,
            seq_place,
            selectors,
            (out, time, cur, gate, square, finals),
            rates,
            skip_gain,
            threshold,
            w_out,
        )
        chunks = dict(zip(keys, chunks))
        own_from = len(order) * lead
        for part in (keys[lead:own_from], keys[own_from:]):
            more = expand(layer, table, [forth(*key) for key in part], feat, gated, w_out)
            chunks.update(zip(part, more))
        own_rows = scatter_sum(grid, own_rows, chunks)
    return own_rows


def solution(mesh):
    in_specs = (
        P("seq", "tp"),
        P(),
        P(None, None, None, "tp"),
        P(None, "tp", None),
        P(None, None, "tp"),
        P(None, None, "tp"),
        P(None, "tp"),
        P(None, "tp"),
        P(None, "tp"),
        P(None, "tp", None),
    )
    return jax.shard_map(
        functools.partial(per_device, mesh.shape["tp"]),
        mesh=mesh,
        in_specs=in_specs,
        out_specs=P("seq", "tp"),
        check_vma=False,
    )
```

```python
import functools
import math

import jax
import jax.numpy as jnp
from jax import lax
from jax.experimental import pallas as pl
from jax.experimental.pallas import tpu as pltpu
from jax.sharding import PartitionSpec as P

LANES = 128
WIDE = 256
STRIDE = 3
EPS = 1e-05
DEPTH = 4
F32 = jnp.float32
BF16 = jnp.bfloat16
VMEM = pl.BlockSpec(memory_space=pltpu.VMEM)
SMEM = pl.BlockSpec(memory_space=pltpu.SMEM)
HBM = pl.BlockSpec(memory_space=pltpu.HBM)
ANY = pl.BlockSpec(memory_space=pl.ANY)
COST = pl.CostEstimate(flops=1, bytes_accessed=1, transcendentals=0)
LONG = pl.CostEstimate(flops=10**10, bytes_accessed=1, transcendentals=0)


def row_factor(square_sum, width):
    return lax.rsqrt(square_sum / width + EPS)


def fold_stride(count):
    return STRIDE * count + 1


def params(mebibytes):
    return pltpu.CompilerParams(vmem_limit_bytes=mebibytes * 1024 * 1024)


def proj_kernel(count, first, layer, table_at, table_ref, *refs):
    shards = refs[:count]
    gain_ref, w_ref = refs[count : count + 2]
    raw_s, split_s, sems = refs[-3:]
    cur_ref, gate_ref, square_ref = refs[-6:-3]
    rows, width = shards[0].shape
    chans = cur_ref.shape[1]
    pieces, size, _ = raw_s.shape
    pieces //= count
    per = 2 * chans // LANES
    depth = size // per
    apart = fold_stride(depth)
    taken = max(per, 16)
    places = [table_ref[table_at + j] for j in range(count)]

    def copy(j, q):
        n = j * pieces + q
        begin = (places[j] * width + q * depth) * per
        source = w_ref.at[layer, pl.ds(pl.multiple_of(begin, size), size), :]
        return pltpu.make_async_copy(source, raw_s.at[n], sems.at[n])

    for j in range(count):
        for q in range(pieces):
            copy(j, q).start()
    squares = jnp.zeros((rows, 1), F32) if first else square_ref[...]
    for j in range(count):
        values = shards[j][:, :width].astype(F32)
        gain = gain_ref[layer : layer + 1, pl.ds(pl.multiple_of(places[j] * width, width), width)]
        left = (values * gain).astype(BF16)
        squares = squares + jnp.sum(values * values, axis=1, keepdims=True)
        for q in range(pieces):
            copy(j, q).wait()
            slot = (j * pieces + q) % split_s.shape[0]
            for begin in range(0, size, taken):
                part = raw_s[j * pieces + q, begin : begin + taken, :].astype(F32)
                for k in range(taken // per):
                    d = begin // per + k
                    place = pl.ds(d * STRIDE, per, stride=apart)
                    split_s[slot, place, :] = part[k * per : (k + 1) * per]
        for e, out in enumerate((cur_ref, gate_ref)):
            for begin in range(0, chans, WIDE):
                tiles = [
                    jnp.concatenate(
                        [
                            split_s[
                                (j * pieces + q) % split_s.shape[0],
                                pl.ds((2 * t + e) * apart, depth, stride=STRIDE),
                                :,
                            ].astype(BF16)
                            for q in range(pieces)
                        ],
                        axis=0,
                    )
                    for t in range(begin // LANES, (begin + WIDE) // LANES)
                ]
                product = jnp.dot(left, jnp.concatenate(tiles, axis=1), preferred_element_type=F32)
                cols = slice(begin, begin + WIDE)
                if first and j == 0:
                    out[:, cols] = product
                else:
                    out[:, cols] += product
    square_ref[...] = squares


def project(layer, shards, table, table_at, norm_gain, w_raw, chans, before, earlier):
    count = len(shards)
    rows, width = shards[0].shape
    depth = min(width, WIDE)
    pieces = count * (width // depth)
    per = 2 * chans // LANES
    shapes = [(rows, chans), (rows, chans), (rows, 1)]
    operands = [table, *shards, norm_gain, w_raw]
    in_specs = [SMEM] + [VMEM] * (count + 1) + [HBM]
    aliases = {}
    if before is not None:
        aliases = {len(operands) + j: j for j in range(len(shapes))}
        in_specs += [VMEM] * len(shapes)
        operands += list(before)
    in_specs += [ANY] * len(earlier)
    operands += earlier
    return pl.pallas_call(
        functools.partial(proj_kernel, count, before is None, layer, table_at),
        out_shape=[jax.ShapeDtypeStruct(shape, F32) for shape in shapes],
        in_specs=in_specs,
        out_specs=[VMEM] * len(shapes),
        scratch_shapes=[
            pltpu.VMEM((pieces, depth * per, LANES), BF16),
            pltpu.VMEM((pieces, per * fold_stride(depth), LANES), F32),
            pltpu.SemaphoreType.DMA((pieces,)),
        ],
        input_output_aliases=aliases,
        compiler_params=params(36),
        cost_estimate=LONG,
        name="project",
    )(*operands)


def unpack_kernel(count, layer, table_at, width, table_ref, w_ref, *refs):
    out_ref, token_ref, raw_s, split_s, sems = refs[-5:]
    pieces, size, _ = raw_s.shape
    chans = out_ref.shape[2]
    per = 2 * chans // LANES
    depth = size // per
    apart = fold_stride(depth)
    taken = max(per, 16)
    each = width // depth

    def copy(n):
        begin = (table_ref[table_at + n // each] * width + n % each * depth) * per
        source = w_ref.at[layer, pl.ds(pl.multiple_of(begin, size), size), :]
        return pltpu.make_async_copy(source, raw_s.at[n], sems.at[n])

    for n in range(pieces):
        copy(n).start()
    token_ref[...] = jnp.zeros_like(token_ref)
    for n in range(pieces):
        copy(n).wait()
        slot = n % split_s.shape[0]
        for begin in range(0, size, taken):
            part = raw_s[n, begin : begin + taken, :].astype(F32)
            for k in range(taken // per):
                place = pl.ds((begin // per + k) * STRIDE, per, stride=apart)
                split_s[slot, place, :] = part[k * per : (k + 1) * per]
        for e in range(2):
            for begin in range(0, chans, WIDE):
                tiles = [
                    split_s[slot, pl.ds((2 * t + e) * apart, depth, stride=STRIDE), :].astype(BF16)
                    for t in range(begin // LANES, (begin + WIDE) // LANES)
                ]
                rows = slice(n * depth, (n + 1) * depth)
                out_ref[e, rows, begin : begin + WIDE] = jnp.concatenate(tiles, axis=1)


def unpack(layer, table, table_at, count, width, chans, w_raw, earlier):
    depth = min(width, WIDE)
    pieces = count * width // depth
    per = 2 * chans // LANES
    return pl.pallas_call(
        functools.partial(unpack_kernel, count, layer, table_at, width),
        out_shape=[
            jax.ShapeDtypeStruct((2, count * width, chans), BF16),
            jax.ShapeDtypeStruct((8, LANES), F32),
        ],
        in_specs=[SMEM, HBM] + [ANY] * len(earlier),
        out_specs=[VMEM, VMEM],
        scratch_shapes=[
            pltpu.VMEM((pieces, depth * per, LANES), BF16),
            pltpu.VMEM((2, per * fold_stride(depth), LANES), F32),
            pltpu.SemaphoreType.DMA((pieces,)),
        ],
        compiler_params=params(24),
        cost_estimate=COST,
        name="unpack",
    )(table, w_raw, *earlier)


def ready_kernel(count, first, layer, table_at, table_ref, *refs):
    shards = refs[:count]
    gain_ref, w_ref = refs[count : count + 2]
    cur_ref, gate_ref, square_ref = refs[-3:]
    rows, width = shards[0].shape
    chans = cur_ref.shape[1]
    squares = jnp.zeros((rows, 1), F32) if first else square_ref[...]
    parts = []
    for j in range(count):
        values = shards[j][:, :width].astype(F32)
        begin = pl.multiple_of(table_ref[table_at + j] * width, width)
        parts.append((values * gain_ref[layer : layer + 1, pl.ds(begin, width)]).astype(BF16))
        squares = squares + jnp.sum(values * values, axis=1, keepdims=True)
    square_ref[...] = squares
    left = jnp.concatenate(parts, axis=1)
    for e, out in enumerate((cur_ref, gate_ref)):
        for begin in range(0, chans, WIDE):
            cols = slice(begin, begin + WIDE)
            product = jnp.dot(left, w_ref[e, :, cols], preferred_element_type=F32)
            if first:
                out[:, cols] = product
            else:
                out[:, cols] += product


def project_ready(layer, shards, table, table_at, norm_gain, weights, before, earlier):
    count = len(shards)
    rows, width = shards[0].shape
    chans = weights.shape[2]
    state = [jax.ShapeDtypeStruct(s, F32) for s in ((rows, chans), (rows, chans), (rows, 1))]
    operands = [table, *shards, norm_gain, weights]
    in_specs = [SMEM] + [VMEM] * (count + 2)
    aliases = {}
    if before is not None:
        aliases = {len(operands) + j: j for j in range(3)}
        in_specs += [VMEM] * 3
        operands += list(before)
    return pl.pallas_call(
        functools.partial(ready_kernel, count, before is None, layer, table_at),
        out_shape=state,
        in_specs=in_specs + [ANY] * len(earlier),
        out_specs=[VMEM] * 3,
        input_output_aliases=aliases,
        compiler_params=params(12),
        cost_estimate=LONG,
        name="project_ready",
    )(*operands, *earlier)


def low_kernel(layer, table_ref, rows_ref, gain_ref, w_ref, *refs):
    width = rows_ref.shape[1]
    begin = pl.multiple_of(table_ref[0] * width, width)
    gain = gain_ref[layer : layer + 1, pl.ds(begin, width)]
    scaled = (rows_ref[...].astype(F32) * gain).astype(BF16)
    product = lax.dot_general(
        scaled, w_ref[layer], (((1,), (1,)), ((), ())), preferred_element_type=F32
    )
    refs[-1][:, :width] = rows_ref[...]
    refs[-1][:, width:] = product.astype(BF16)


def project_low(layer, table, own_rows, norm_gain, w_low):
    rows, width = own_rows.shape
    return pl.pallas_call(
        functools.partial(low_kernel, layer),
        out_shape=jax.ShapeDtypeStruct((rows, width + w_low.shape[1]), BF16),
        in_specs=[SMEM] + [VMEM] * 3,
        out_specs=VMEM,
        compiler_params=params(12),
        cost_estimate=COST,
        name="project_low",
    )(table, own_rows, norm_gain, w_low)


def relay_kernel(value_ref, *refs):
    refs[-1][...] = value_ref[...]


def relay(value, *others):
    return pl.pallas_call(
        relay_kernel,
        out_shape=jax.ShapeDtypeStruct(value.shape, value.dtype),
        in_specs=[VMEM] + [ANY] * len(others),
        out_specs=VMEM,
        compiler_params=params(8),
        cost_estimate=COST,
        name="relay",
    )(value, *others)


def scan_kernel(
    layer,
    states,
    width,
    sel_ref,
    low_ref,
    square_ref,
    cur_ref,
    w_dt_ref,
    bias_ref,
    rate_ref,
    out_ref,
    time_ref,
    final_ref,
    step_s,
    drive_s,
):
    rows, chans = cur_ref.shape
    fold = chans // LANES
    rank = w_dt_ref.shape[1]
    factor = row_factor(square_ref[...], width)
    rank_part = (low_ref[:, :rank] * factor).astype(BF16)
    apart = fold_stride(rows)
    twice = factor * factor
    for begin in range(0, chans, WIDE):
        cols = slice(begin, begin + WIDE)
        pre = jnp.dot(rank_part, w_dt_ref[layer, :, cols], preferred_element_type=F32)
        pre = pre + bias_ref[layer : layer + 1, cols]
        step = jnp.maximum(pre, 0.0) + jnp.log1p(jnp.exp(-jnp.abs(pre)))
        drive = step * (cur_ref[:, cols] * twice)
        for q in range(WIDE // LANES):
            part = slice(q * LANES, (q + 1) * LANES)
            place = pl.ds((begin // LANES + q) * apart, rows, stride=STRIDE)
            step_s[place, :] = step[:, part]
            drive_s[place, :] = drive[:, part]

    def advance(t, carried):
        time, held = carried
        here = pl.ds(t * STRIDE, fold, stride=apart)
        step = step_s[here, :]
        drive = drive_s[here, :]
        sums = [None] * 4
        after = []
        for s in range(states):
            decay = jnp.exp2(step * rate_ref[layer, s])
            now = decay * held[s] + drive * sel_ref[t, s]
            term = now * sel_ref[t, states + s]
            sums[s % 4] = term if sums[s % 4] is None else sums[s % 4] + term
            after.append(now)
        time = time + step
        out_ref[here, :] = (sums[0] + sums[1]) + (sums[2] + sums[3])
        time_ref[here, :] = time
        return time, tuple(after)

    zero = jnp.zeros((fold, LANES), F32)
    time, held = lax.fori_loop(0, rows, advance, (zero, (zero,) * states), unroll=8)
    for s in range(states):
        final_ref[s] = held[s].astype(BF16)
    final_ref[states] = time.astype(BF16)


def local_scan(layer, width, selectors, low, square, cur, w_dt, dt_bias, rate):
    rows, chans = cur.shape
    _, states, fold, _ = rate.shape
    folded = (fold * fold_stride(rows), LANES)
    return pl.pallas_call(
        functools.partial(scan_kernel, layer, states, width),
        out_shape=[
            jax.ShapeDtypeStruct(folded, F32),
            jax.ShapeDtypeStruct(folded, F32),
            jax.ShapeDtypeStruct((states + 1, fold, LANES), BF16),
        ],
        in_specs=[SMEM] + [VMEM] * 6,
        out_specs=[VMEM] * 3,
        scratch_shapes=[pltpu.VMEM(folded, F32), pltpu.VMEM(folded, F32)],
        compiler_params=params(20),
        cost_estimate=COST,
        name="local_scan",
    )(selectors, low, square, cur, w_dt, dt_bias, rate)


def emit_chunks(layer, table_at, feat, gated_ref, table_ref, w_ref, chunks, w_s, sems, before=None):
    def copy(j):
        begin = pl.multiple_of(table_ref[table_at[j]] * feat, feat)
        return pltpu.make_async_copy(w_ref.at[layer, :, pl.ds(begin, feat)], w_s.at[j], sems.at[j])

    for j in range(len(chunks)):
        copy(j).start()
    if before is not None:
        before()
    for j, chunk in enumerate(chunks):
        copy(j).wait()
        for begin in range(0, feat, WIDE):
            cols = slice(begin, begin + WIDE)
            chunk[:, cols] = jnp.dot(
                gated_ref[...], w_s[j, :, cols], preferred_element_type=F32
            ).astype(BF16)


def close_kernel(layer, states, table_at, feat, width, table_ref, place_ref, sel_ref, *refs):
    out_ref, time_ref, cur_ref, gate_ref, square_ref, final_ref = refs[:6]
    rate_ref, skip_ref, thresh_ref, w_ref, gated_ref = refs[6:11]
    chunks = refs[11 : 11 + len(table_at)]
    enter_s, mixed_s, w_s, sems = refs[-4:]
    rows, chans = cur_ref.shape
    fold = chans // LANES
    apart = fold_stride(rows)

    def gate_all():
        def enter(p, state):
            time = final_ref[p, states].astype(F32)
            return tuple(
                jnp.exp2(time * rate_ref[layer, s]) * state[s] + final_ref[p, s].astype(F32)
                for s in range(states)
            )

        zero = jnp.zeros((fold, LANES), F32)
        state = lax.fori_loop(0, place_ref[0], enter, (zero,) * states)
        for s in range(states):
            enter_s[s] = state[s]

        def correct(t, carried):
            here = pl.ds(t * STRIDE, fold, stride=apart)
            time = time_ref[here, :]
            sums = [out_ref[here, :], None, None, None]
            for s in range(states):
                term = jnp.exp2(time * rate_ref[layer, s]) * (enter_s[s] * sel_ref[t, states + s])
                sums[s % 4] = term if sums[s % 4] is None else sums[s % 4] + term
            mixed_s[here, :] = (sums[0] + sums[1]) + (sums[2] + sums[3])
            return carried

        lax.fori_loop(0, rows, correct, 0, unroll=8)

        factor = row_factor(square_ref[...], width)
        for r in range(fold):
            cols = slice(r * LANES, (r + 1) * LANES)
            skip = skip_ref[layer : layer + 1, cols]
            mixed = mixed_s[pl.ds(r * apart, rows, stride=STRIDE), :] + skip * cur_ref[:, cols]
            mixed = mixed * factor
            normal = mixed * lax.rsqrt(jnp.mean(mixed * mixed, axis=1, keepdims=True) + EPS)
            thresh = thresh_ref[layer : layer + 1, cols]
            shrunk = jnp.maximum(normal - thresh, 0.0) - jnp.maximum(-normal - thresh, 0.0)
            gate = gate_ref[:, cols] * factor
            gated_ref[:, cols] = (shrunk * (gate * jax.nn.sigmoid(gate))).astype(BF16)

    emit_chunks(layer, table_at, feat, gated_ref, table_ref, w_ref, chunks, w_s, sems, gate_all)


def close_layer(
    layer, width, table, table_at, feat, seq_place, selectors, values, rate, skip, thresh, w_out
):
    rows, chans = values[2].shape
    _, states, fold, _ = rate.shape
    count = len(table_at)
    chunk = jax.ShapeDtypeStruct((rows, feat), BF16)
    results = pl.pallas_call(
        functools.partial(close_kernel, layer, states, table_at, feat, width),
        out_shape=[jax.ShapeDtypeStruct((rows, chans), BF16)] + [chunk] * count,
        in_specs=[SMEM] * 3 + [VMEM] * 9 + [HBM],
        out_specs=[VMEM] * (1 + count),
        scratch_shapes=[
            pltpu.VMEM((states, fold, LANES), F32),
            pltpu.VMEM((fold * fold_stride(rows), LANES), F32),
            pltpu.VMEM((count, chans, feat), BF16),
            pltpu.SemaphoreType.DMA((count,)),
        ],
        compiler_params=params(48),
        cost_estimate=COST,
        name="close_layer",
    )(table, seq_place, selectors, *values, rate, skip, thresh, w_out)
    return results[0], results[1:]


def expand_kernel(layer, table_at, feat, table_ref, gated_ref, w_ref, *refs):
    chunks = refs[: len(table_at)]
    emit_chunks(layer, table_at, feat, gated_ref, table_ref, w_ref, chunks, *refs[-2:])


def expand(layer, table, table_at, feat, gated, w_out):
    rows, chans = gated.shape
    count = len(table_at)
    return pl.pallas_call(
        functools.partial(expand_kernel, layer, table_at, feat),
        out_shape=[jax.ShapeDtypeStruct((rows, feat), BF16)] * count,
        in_specs=[SMEM, VMEM, HBM],
        out_specs=[VMEM] * count,
        scratch_shapes=[
            pltpu.VMEM((count, chans, feat), BF16),
            pltpu.SemaphoreType.DMA((count,)),
        ],
        compiler_params=params(48),
        cost_estimate=COST,
        name="expand",
    )(table, gated, w_out)


def combine_kernel(count, *refs):
    total = refs[0][...].astype(F32)
    for ref in refs[1:count]:
        total = total + ref[...].astype(F32)
    refs[-1][...] = total.astype(BF16)


def combine(values, earlier):
    return pl.pallas_call(
        functools.partial(combine_kernel, len(values)),
        out_shape=jax.ShapeDtypeStruct(values[0].shape, BF16),
        in_specs=[VMEM] * len(values) + [ANY] * len(earlier),
        out_specs=VMEM,
        compiler_params=params(8),
        cost_estimate=COST,
        name="combine",
    )(*values, *earlier)


class Grid:
    def __init__(self, count):
        self.depth = DEPTH if count % DEPTH == 0 else 1
        self.side = count // self.depth

    def places(self):
        return [(z, y) for z in range(self.depth) for y in range(self.side)]

    def at(self, z, y):
        return (z % self.depth) * self.side + y % self.side

    def send(self, value, deep, across):
        pairs = [(self.at(z, y), self.at(z + deep, y + across)) for z, y in self.places()]
        return lax.ppermute(value, "tp", pairs)

    def swap(self, value, bit):
        pairs = [(self.at(z, y), self.at(z ^ bit, y)) for z, y in self.places()]
        return lax.ppermute(value, "tp", pairs)

    def table(self):
        own = lax.axis_index("tp")
        z, y = own // self.side, own % self.side
        offsets = jnp.arange(self.depth * self.side, dtype=jnp.int32)
        a, b = offsets // self.side, offsets % self.side
        both = []
        for sign in (-1, 1):
            deep = (z + sign * a + self.depth) % self.depth
            both.append(deep * self.side + (y + sign * b + self.side) % self.side)
        return jnp.concatenate(both).astype(jnp.int32)


def gather_columns(grid, own):
    columns = {0: own}
    half = grid.depth // 2
    for a in range(1, grid.depth - half + 1):
        columns[a] = grid.send(columns[a - 1], 1, 0)
        back = grid.depth - a
        if back > a:
            columns[back] = grid.send(columns[(back + 1) % grid.depth], -1, 0)
    return columns


def scatter_order(grid):
    order = []
    for a in range(grid.depth - grid.depth // 2, 0, -1):
        order.append(a)
        if grid.depth - a > a:
            order.append(grid.depth - a)
    return order + [0]


def scatter_sum(grid, own_rows, chunks, aside):
    order = scatter_order(grid)
    crossed = {
        a: [grid.send(chunks[a, b], 0, b) for b in range(1, grid.side)] for a in order
    }
    half = grid.depth - grid.depth // 2
    arriving = {a: [] for a in order}
    waiting = []
    for n, a in enumerate(order):
        parts = [chunks[a, 0], *crossed[a], *arriving[a]]
        if a == 0:
            aside(n, [*crossed[a], chunks[a, 0]][0])
            return combine([own_rows, *parts], waiting)
        part = combine(parts, waiting)
        step = 1 if a <= half else -1
        arriving[(a - step) % grid.depth].append(grid.send(part, step, 0))
        waiting = aside(n, part)


def sum_selectors(grid, partials):
    total = sum(partial.astype(F32) for partial in partials)
    stages = []
    bit = 1
    while bit < grid.depth:
        rounded = total.astype(BF16)
        stages.append(rounded)
        total = rounded.astype(F32) + grid.swap(rounded, bit).astype(F32)
        bit *= 2
    return total, stages


def per_device(
    n_tp, tokens, norm_gain, w_in, w_low, w_dt, a_rate, dt_bias, skip_gain, threshold, w_out
):
    grid = Grid(n_tp)
    feat = tokens.shape[1]
    layers, width, _, chans = w_in.shape
    states = a_rate.shape[1]
    rank = w_dt.shape[1]
    fold = chans // LANES
    table = grid.table()
    forth = lambda a, b: n_tp + a * grid.side + b
    seq_place = lax.axis_index("seq").astype(jnp.int32).reshape(1)
    rates = (a_rate * (-math.log2(math.e))).reshape(layers, states, fold, LANES)
    w_raw = w_in.reshape(layers, width, 2, fold, LANES).transpose(0, 1, 3, 2, 4)
    w_raw = w_raw.reshape(layers, width * 2 * fold, LANES)
    order = scatter_order(grid)
    own_rows = tokens
    low_t = jnp.swapaxes(w_low, 1, 2)
    arrivals = [0] + [a for a in order if a not in (0, order[0])] + order[:1]
    weights = {}
    for layer in range(layers):
        columns = gather_columns(grid, own_rows)
        cross = lambda column: [grid.send(column, 0, b) for b in range(1, grid.side)]
        packed = project_low(layer, table, own_rows, norm_gain, low_t)
        beside = {0: cross(packed)}
        low, stages = sum_selectors(grid, [each[:, feat:] for each in (packed, *beside[0])])
        selectors = low[:, rank:]
        state = None
        for n, a in enumerate(arrivals):
            if n:
                last = n + 1 == len(arrivals)
                beside[a] = cross(relay(columns[a], first) if last else columns[a])
            arrived = [columns[a], *beside[a]]
            place, earlier = a * grid.side, stages[n - 1 : n] if n else []
            if a in weights:
                state = project_ready(
                    layer, arrived, table, place, norm_gain, weights[a], state, earlier
                )
            else:
                state = project(
                    layer, arrived, table, place, norm_gain, w_raw, chans, state, earlier
                )
            if n == 0:
                first = state[2]
        cur, gate, square = state
        out, time, final = local_scan(
            layer, width, selectors, low, square, cur, w_dt, dt_bias, rates
        )
        finals = lax.all_gather(final, "seq")
        keys = [(a, b) for a in order for b in range(1, grid.side)]
        keys += [(a, 0) for a in order]
        lead = grid.side - 1
        gated, chunks = close_layer(
            layer,
            width,
            table,
            [forth(*key) for key in keys[:lead]],
            feat,
            seq_place,
            selectors,
            (out, time, cur, gate, square, finals),
            rates,
            skip_gain,
            threshold,
            w_out,
        )
        chunks = dict(zip(keys, chunks))
        split = len(order) * lead + 1
        for part in (keys[lead:split], keys[split:]):
            more = expand(layer, table, [forth(*key) for key in part], feat, gated, w_out)
            chunks.update(zip(part, more))
        weights = {}

        def aside(n, value):
            left = [a for a in arrivals if a not in weights]
            wanted = [1, 0, len(left) - 1, 1][min(n, 3)] if layer + 1 < layers else 0
            tokens = []
            for a in left[:wanted]:
                weights[a], token = unpack(
                    layer + 1, table, a * grid.side, grid.side, feat, chans, w_raw, [value]
                )
                tokens.append(token)
            return tokens

        own_rows = scatter_sum(grid, own_rows, chunks, aside)
    return own_rows


def solution(mesh):
    in_specs = (
        P("seq", "tp"),
        P(),
        P(None, None, None, "tp"),
        P(None, "tp", None),
        P(None, None, "tp"),
        P(None, None, "tp"),
        P(None, "tp"),
        P(None, "tp"),
        P(None, "tp"),
        P(None, "tp", None),
    )
    return jax.shard_map(
        functools.partial(per_device, mesh.shape["tp"]),
        mesh=mesh,
        in_specs=in_specs,
        out_specs=P("seq", "tp"),
        check_vma=False,
    )
```

```python
import functools
import math

import jax
import jax.numpy as jnp
from jax import lax
from jax.experimental import pallas as pl
from jax.experimental.pallas import tpu as pltpu
from jax.sharding import PartitionSpec as P

LANES = 128
WIDE = 256
STRIDE = 3
EPS = 1e-05
DEPTH = 4
F32 = jnp.float32
BF16 = jnp.bfloat16
VMEM = pl.BlockSpec(memory_space=pltpu.VMEM)
SMEM = pl.BlockSpec(memory_space=pltpu.SMEM)
HBM = pl.BlockSpec(memory_space=pltpu.HBM)
ANY = pl.BlockSpec(memory_space=pl.ANY)
COST = pl.CostEstimate(flops=1, bytes_accessed=1, transcendentals=0)
LONG = pl.CostEstimate(flops=10**10, bytes_accessed=1, transcendentals=0)


def row_factor(square_sum, width):
    return lax.rsqrt(square_sum / width + EPS)


def fold_stride(count):
    return STRIDE * count + 1


def params(mebibytes):
    return pltpu.CompilerParams(vmem_limit_bytes=mebibytes * 1024 * 1024)


def proj_kernel(count, first, layer, table_at, table_ref, *refs):
    shards = refs[:count]
    gain_ref, w_ref = refs[count : count + 2]
    raw_s, split_s, sems = refs[-3:]
    cur_ref, gate_ref, square_ref = refs[-6:-3]
    rows, width = shards[0].shape
    chans = cur_ref.shape[1]
    pieces, size, _ = raw_s.shape
    pieces //= count
    per = 2 * chans // LANES
    depth = size // per
    apart = fold_stride(depth)
    taken = max(per, 16)
    places = [table_ref[table_at + j] for j in range(count)]

    def copy(j, q):
        n = j * pieces + q
        begin = (places[j] * width + q * depth) * per
        source = w_ref.at[layer, pl.ds(pl.multiple_of(begin, size), size), :]
        return pltpu.make_async_copy(source, raw_s.at[n], sems.at[n])

    for j in range(count):
        for q in range(pieces):
            copy(j, q).start()
    squares = jnp.zeros((rows, 1), F32) if first else square_ref[...]
    for j in range(count):
        values = shards[j][:, :width].astype(F32)
        gain = gain_ref[layer : layer + 1, pl.ds(pl.multiple_of(places[j] * width, width), width)]
        left = (values * gain).astype(BF16)
        squares = squares + jnp.sum(values * values, axis=1, keepdims=True)
        for q in range(pieces):
            copy(j, q).wait()
            slot = (j * pieces + q) % split_s.shape[0]
            for begin in range(0, size, taken):
                part = raw_s[j * pieces + q, begin : begin + taken, :].astype(F32)
                for k in range(taken // per):
                    d = begin // per + k
                    place = pl.ds(d * STRIDE, per, stride=apart)
                    split_s[slot, place, :] = part[k * per : (k + 1) * per]
        for e, out in enumerate((cur_ref, gate_ref)):
            for begin in range(0, chans, WIDE):
                tiles = [
                    jnp.concatenate(
                        [
                            split_s[
                                (j * pieces + q) % split_s.shape[0],
                                pl.ds((2 * t + e) * apart, depth, stride=STRIDE),
                                :,
                            ].astype(BF16)
                            for q in range(pieces)
                        ],
                        axis=0,
                    )
                    for t in range(begin // LANES, (begin + WIDE) // LANES)
                ]
                product = jnp.dot(left, jnp.concatenate(tiles, axis=1), preferred_element_type=F32)
                cols = slice(begin, begin + WIDE)
                if first and j == 0:
                    out[:, cols] = product
                else:
                    out[:, cols] += product
    square_ref[...] = squares


def project(layer, shards, table, table_at, norm_gain, w_raw, chans, before, earlier):
    count = len(shards)
    rows, width = shards[0].shape
    depth = min(width, WIDE)
    pieces = count * (width // depth)
    per = 2 * chans // LANES
    shapes = [(rows, chans), (rows, chans), (rows, 1)]
    operands = [table, *shards, norm_gain, w_raw]
    in_specs = [SMEM] + [VMEM] * (count + 1) + [HBM]
    aliases = {}
    if before is not None:
        aliases = {len(operands) + j: j for j in range(len(shapes))}
        in_specs += [VMEM] * len(shapes)
        operands += list(before)
    in_specs += [ANY] * len(earlier)
    operands += earlier
    return pl.pallas_call(
        functools.partial(proj_kernel, count, before is None, layer, table_at),
        out_shape=[jax.ShapeDtypeStruct(shape, F32) for shape in shapes],
        in_specs=in_specs,
        out_specs=[VMEM] * len(shapes),
        scratch_shapes=[
            pltpu.VMEM((pieces, depth * per, LANES), BF16),
            pltpu.VMEM((pieces, per * fold_stride(depth), LANES), F32),
            pltpu.SemaphoreType.DMA((pieces,)),
        ],
        input_output_aliases=aliases,
        compiler_params=params(36),
        cost_estimate=LONG,
        name="project",
    )(*operands)


def unpack_kernel(count, layer, table_at, width, table_ref, w_ref, *refs):
    out_ref, token_ref, raw_s, split_s, sems = refs[-5:]
    pieces, size, _ = raw_s.shape
    chans = out_ref.shape[2]
    per = 2 * chans // LANES
    depth = size // per
    apart = fold_stride(depth)
    taken = max(per, 16)
    each = width // depth

    def copy(n):
        begin = (table_ref[table_at + n // each] * width + n % each * depth) * per
        source = w_ref.at[layer, pl.ds(pl.multiple_of(begin, size), size), :]
        return pltpu.make_async_copy(source, raw_s.at[n], sems.at[n])

    for n in range(pieces):
        copy(n).start()
    token_ref[...] = jnp.zeros_like(token_ref)
    for n in range(pieces):
        copy(n).wait()
        slot = n % split_s.shape[0]
        for begin in range(0, size, taken):
            part = raw_s[n, begin : begin + taken, :].astype(F32)
            for k in range(taken // per):
                place = pl.ds((begin // per + k) * STRIDE, per, stride=apart)
                split_s[slot, place, :] = part[k * per : (k + 1) * per]
        for e in range(2):
            for begin in range(0, chans, WIDE):
                tiles = [
                    split_s[slot, pl.ds((2 * t + e) * apart, depth, stride=STRIDE), :].astype(BF16)
                    for t in range(begin // LANES, (begin + WIDE) // LANES)
                ]
                rows = slice(n * depth, (n + 1) * depth)
                out_ref[e, rows, begin : begin + WIDE] = jnp.concatenate(tiles, axis=1)


def unpack(layer, table, table_at, count, width, chans, w_raw, earlier):
    depth = min(width, WIDE)
    pieces = count * width // depth
    per = 2 * chans // LANES
    return pl.pallas_call(
        functools.partial(unpack_kernel, count, layer, table_at, width),
        out_shape=[
            jax.ShapeDtypeStruct((2, count * width, chans), BF16),
            jax.ShapeDtypeStruct((8, LANES), F32),
        ],
        in_specs=[SMEM, HBM] + [ANY] * len(earlier),
        out_specs=[VMEM, VMEM],
        scratch_shapes=[
            pltpu.VMEM((pieces, depth * per, LANES), BF16),
            pltpu.VMEM((2, per * fold_stride(depth), LANES), F32),
            pltpu.SemaphoreType.DMA((pieces,)),
        ],
        compiler_params=params(24),
        cost_estimate=COST,
        name="unpack",
    )(table, w_raw, *earlier)


def ready_kernel(count, first, layer, table_at, table_ref, *refs):
    shards = refs[:count]
    gain_ref, w_ref = refs[count : count + 2]
    cur_ref, gate_ref, square_ref = refs[-3:]
    rows, width = shards[0].shape
    chans = cur_ref.shape[1]
    squares = jnp.zeros((rows, 1), F32) if first else square_ref[...]
    parts = []
    for j in range(count):
        values = shards[j][:, :width].astype(F32)
        begin = pl.multiple_of(table_ref[table_at + j] * width, width)
        parts.append((values * gain_ref[layer : layer + 1, pl.ds(begin, width)]).astype(BF16))
        squares = squares + jnp.sum(values * values, axis=1, keepdims=True)
    square_ref[...] = squares
    left = jnp.concatenate(parts, axis=1)
    for e, out in enumerate((cur_ref, gate_ref)):
        for begin in range(0, chans, WIDE):
            cols = slice(begin, begin + WIDE)
            product = jnp.dot(left, w_ref[e, :, cols], preferred_element_type=F32)
            if first:
                out[:, cols] = product
            else:
                out[:, cols] += product


def project_ready(layer, shards, table, table_at, norm_gain, weights, before, earlier):
    count = len(shards)
    rows, width = shards[0].shape
    chans = weights.shape[2]
    state = [jax.ShapeDtypeStruct(s, F32) for s in ((rows, chans), (rows, chans), (rows, 1))]
    operands = [table, *shards, norm_gain, weights]
    in_specs = [SMEM] + [VMEM] * (count + 2)
    aliases = {}
    if before is not None:
        aliases = {len(operands) + j: j for j in range(3)}
        in_specs += [VMEM] * 3
        operands += list(before)
    return pl.pallas_call(
        functools.partial(ready_kernel, count, before is None, layer, table_at),
        out_shape=state,
        in_specs=in_specs + [ANY] * len(earlier),
        out_specs=[VMEM] * 3,
        input_output_aliases=aliases,
        compiler_params=params(12),
        cost_estimate=LONG,
        name="project_ready",
    )(*operands, *earlier)


def low_kernel(layer, table_ref, rows_ref, gain_ref, w_ref, *refs):
    width = rows_ref.shape[1]
    begin = pl.multiple_of(table_ref[0] * width, width)
    gain = gain_ref[layer : layer + 1, pl.ds(begin, width)]
    scaled = (rows_ref[...].astype(F32) * gain).astype(BF16)
    product = lax.dot_general(
        scaled, w_ref[layer], (((1,), (1,)), ((), ())), preferred_element_type=F32
    )
    out_ref = refs[-1]
    before = out_ref.shape[1] - product.shape[1]
    if before:
        out_ref[:, :before] = rows_ref[...]
    out_ref[:, before:] = product.astype(BF16)


def project_low(layer, table, own_rows, norm_gain, w_low, before, earlier):
    rows = own_rows.shape[0]
    return pl.pallas_call(
        functools.partial(low_kernel, layer),
        out_shape=jax.ShapeDtypeStruct((rows, before + w_low.shape[1]), BF16),
        in_specs=[SMEM] + [VMEM] * 3 + [ANY] * len(earlier),
        out_specs=VMEM,
        compiler_params=params(12),
        cost_estimate=COST,
        name="project_low",
    )(table, own_rows, norm_gain, w_low, *earlier)


def relay_kernel(value_ref, *refs):
    refs[-1][...] = value_ref[...]


def relay(value, *others):
    return pl.pallas_call(
        relay_kernel,
        out_shape=jax.ShapeDtypeStruct(value.shape, value.dtype),
        in_specs=[VMEM] + [ANY] * len(others),
        out_specs=VMEM,
        compiler_params=params(8),
        cost_estimate=COST,
        name="relay",
    )(value, *others)


def scan_kernel(
    layer,
    states,
    width,
    sel_ref,
    low_ref,
    square_ref,
    cur_ref,
    w_dt_ref,
    bias_ref,
    rate_ref,
    out_ref,
    time_ref,
    final_ref,
    step_s,
    drive_s,
):
    rows, chans = cur_ref.shape
    fold = chans // LANES
    rank = w_dt_ref.shape[1]
    factor = row_factor(square_ref[...], width)
    rank_part = (low_ref[:, :rank] * factor).astype(BF16)
    apart = fold_stride(rows)
    twice = factor * factor
    for begin in range(0, chans, WIDE):
        cols = slice(begin, begin + WIDE)
        pre = jnp.dot(rank_part, w_dt_ref[layer, :, cols], preferred_element_type=F32)
        pre = pre + bias_ref[layer : layer + 1, cols]
        step = jnp.maximum(pre, 0.0) + jnp.log1p(jnp.exp(-jnp.abs(pre)))
        drive = step * (cur_ref[:, cols] * twice)
        for q in range(WIDE // LANES):
            part = slice(q * LANES, (q + 1) * LANES)
            place = pl.ds((begin // LANES + q) * apart, rows, stride=STRIDE)
            step_s[place, :] = step[:, part]
            drive_s[place, :] = drive[:, part]

    def advance(t, carried):
        time, held = carried
        here = pl.ds(t * STRIDE, fold, stride=apart)
        step = step_s[here, :]
        drive = drive_s[here, :]
        sums = [None] * 4
        after = []
        for s in range(states):
            decay = jnp.exp2(step * rate_ref[layer, s])
            now = decay * held[s] + drive * sel_ref[t, s]
            term = now * sel_ref[t, states + s]
            sums[s % 4] = term if sums[s % 4] is None else sums[s % 4] + term
            after.append(now)
        time = time + step
        out_ref[here, :] = (sums[0] + sums[1]) + (sums[2] + sums[3])
        time_ref[here, :] = time
        return time, tuple(after)

    zero = jnp.zeros((fold, LANES), F32)
    time, held = lax.fori_loop(0, rows, advance, (zero, (zero,) * states), unroll=8)
    for s in range(states):
        final_ref[s] = held[s].astype(BF16)
    final_ref[states] = time.astype(BF16)


def local_scan(layer, width, selectors, low, square, cur, w_dt, dt_bias, rate):
    rows, chans = cur.shape
    _, states, fold, _ = rate.shape
    folded = (fold * fold_stride(rows), LANES)
    return pl.pallas_call(
        functools.partial(scan_kernel, layer, states, width),
        out_shape=[
            jax.ShapeDtypeStruct(folded, F32),
            jax.ShapeDtypeStruct(folded, F32),
            jax.ShapeDtypeStruct((states + 1, fold, LANES), BF16),
        ],
        in_specs=[SMEM] + [VMEM] * 6,
        out_specs=[VMEM] * 3,
        scratch_shapes=[pltpu.VMEM(folded, F32), pltpu.VMEM(folded, F32)],
        compiler_params=params(20),
        cost_estimate=COST,
        name="local_scan",
    )(selectors, low, square, cur, w_dt, dt_bias, rate)


def emit_chunks(layer, table_at, feat, gated_ref, table_ref, w_ref, chunks, w_s, sems, before=None):
    def copy(j):
        begin = pl.multiple_of(table_ref[table_at[j]] * feat, feat)
        return pltpu.make_async_copy(w_ref.at[layer, :, pl.ds(begin, feat)], w_s.at[j], sems.at[j])

    for j in range(len(chunks)):
        copy(j).start()
    if before is not None:
        before()
    for j, chunk in enumerate(chunks):
        copy(j).wait()
        for begin in range(0, feat, WIDE):
            cols = slice(begin, begin + WIDE)
            chunk[:, cols] = jnp.dot(
                gated_ref[...], w_s[j, :, cols], preferred_element_type=F32
            ).astype(BF16)


def close_kernel(layer, states, table_at, feat, width, table_ref, place_ref, sel_ref, *refs):
    out_ref, time_ref, cur_ref, gate_ref, square_ref, final_ref = refs[:6]
    rate_ref, skip_ref, thresh_ref, w_ref, gated_ref = refs[6:11]
    chunks = refs[11 : 11 + len(table_at)]
    enter_s, mixed_s, w_s, sems = refs[-4:]
    rows, chans = cur_ref.shape
    fold = chans // LANES
    apart = fold_stride(rows)

    def gate_all():
        def enter(p, state):
            time = final_ref[p, states].astype(F32)
            return tuple(
                jnp.exp2(time * rate_ref[layer, s]) * state[s] + final_ref[p, s].astype(F32)
                for s in range(states)
            )

        zero = jnp.zeros((fold, LANES), F32)
        state = lax.fori_loop(0, place_ref[0], enter, (zero,) * states)
        for s in range(states):
            enter_s[s] = state[s]

        def correct(t, carried):
            here = pl.ds(t * STRIDE, fold, stride=apart)
            time = time_ref[here, :]
            sums = [out_ref[here, :], None, None, None]
            for s in range(states):
                term = jnp.exp2(time * rate_ref[layer, s]) * (enter_s[s] * sel_ref[t, states + s])
                sums[s % 4] = term if sums[s % 4] is None else sums[s % 4] + term
            mixed_s[here, :] = (sums[0] + sums[1]) + (sums[2] + sums[3])
            return carried

        lax.fori_loop(0, rows, correct, 0, unroll=8)

        factor = row_factor(square_ref[...], width)
        for r in range(fold):
            cols = slice(r * LANES, (r + 1) * LANES)
            skip = skip_ref[layer : layer + 1, cols]
            mixed = mixed_s[pl.ds(r * apart, rows, stride=STRIDE), :] + skip * cur_ref[:, cols]
            mixed = mixed * factor
            normal = mixed * lax.rsqrt(jnp.mean(mixed * mixed, axis=1, keepdims=True) + EPS)
            thresh = thresh_ref[layer : layer + 1, cols]
            shrunk = jnp.maximum(normal - thresh, 0.0) - jnp.maximum(-normal - thresh, 0.0)
            gate = gate_ref[:, cols] * factor
            gated_ref[:, cols] = (shrunk * (gate * jax.nn.sigmoid(gate))).astype(BF16)

    emit_chunks(layer, table_at, feat, gated_ref, table_ref, w_ref, chunks, w_s, sems, gate_all)


def close_layer(
    layer, width, table, table_at, feat, seq_place, selectors, values, rate, skip, thresh, w_out
):
    rows, chans = values[2].shape
    _, states, fold, _ = rate.shape
    count = len(table_at)
    chunk = jax.ShapeDtypeStruct((rows, feat), BF16)
    results = pl.pallas_call(
        functools.partial(close_kernel, layer, states, table_at, feat, width),
        out_shape=[jax.ShapeDtypeStruct((rows, chans), BF16)] + [chunk] * count,
        in_specs=[SMEM] * 3 + [VMEM] * 9 + [HBM],
        out_specs=[VMEM] * (1 + count),
        scratch_shapes=[
            pltpu.VMEM((states, fold, LANES), F32),
            pltpu.VMEM((fold * fold_stride(rows), LANES), F32),
            pltpu.VMEM((count, chans, feat), BF16),
            pltpu.SemaphoreType.DMA((count,)),
        ],
        compiler_params=params(40),
        cost_estimate=COST,
        name="close_layer",
    )(table, seq_place, selectors, *values, rate, skip, thresh, w_out)
    return results[0], results[1:]


def expand_kernel(layer, table_at, feat, table_ref, gated_ref, w_ref, *refs):
    chunks = refs[: len(table_at)]
    emit_chunks(layer, table_at, feat, gated_ref, table_ref, w_ref, chunks, *refs[-2:])


def expand(layer, table, table_at, feat, gated, w_out):
    rows, chans = gated.shape
    count = len(table_at)
    return pl.pallas_call(
        functools.partial(expand_kernel, layer, table_at, feat),
        out_shape=[jax.ShapeDtypeStruct((rows, feat), BF16)] * count,
        in_specs=[SMEM, VMEM, HBM],
        out_specs=[VMEM] * count,
        scratch_shapes=[
            pltpu.VMEM((count, chans, feat), BF16),
            pltpu.SemaphoreType.DMA((count,)),
        ],
        compiler_params=params(40),
        cost_estimate=COST,
        name="expand",
    )(table, gated, w_out)


def finish_kernel(rank, own_ref, arrived_ref, *refs):
    low_ref, selectors_ref = refs[-2:]
    total = own_ref[...].astype(F32) + arrived_ref[...].astype(F32)
    low_ref[...] = total
    selectors_ref[...] = total[:, rank:]


def finish_low(rank, own, arrived, earlier):
    rows, count = own.shape
    return pl.pallas_call(
        functools.partial(finish_kernel, rank),
        out_shape=[
            jax.ShapeDtypeStruct((rows, count), F32),
            jax.ShapeDtypeStruct((rows, count - rank), F32),
        ],
        in_specs=[VMEM] * 2 + [ANY] * len(earlier),
        out_specs=[VMEM] * 2,
        compiler_params=params(8),
        cost_estimate=COST,
        name="finish_low",
    )(own, arrived, *earlier)


def combine_kernel(count, *refs):
    total = refs[0][...].astype(F32)
    for ref in refs[1:count]:
        total = total + ref[...].astype(F32)
    refs[-1][...] = total.astype(BF16)


def combine(values, earlier):
    return pl.pallas_call(
        functools.partial(combine_kernel, len(values)),
        out_shape=jax.ShapeDtypeStruct(values[0].shape, BF16),
        in_specs=[VMEM] * len(values) + [ANY] * len(earlier),
        out_specs=VMEM,
        compiler_params=params(8),
        cost_estimate=COST,
        name="combine",
    )(*values, *earlier)


class Grid:
    def __init__(self, count):
        self.depth = DEPTH if count % DEPTH == 0 else 1
        self.side = count // self.depth

    def places(self):
        return [(z, y) for z in range(self.depth) for y in range(self.side)]

    def at(self, z, y):
        return (z % self.depth) * self.side + y % self.side

    def send(self, value, deep, across):
        pairs = [(self.at(z, y), self.at(z + deep, y + across)) for z, y in self.places()]
        return lax.ppermute(value, "tp", pairs)

    def swap(self, value, bit):
        pairs = [(self.at(z, y), self.at(z ^ bit, y)) for z, y in self.places()]
        return lax.ppermute(value, "tp", pairs)

    def table(self):
        own = lax.axis_index("tp")
        z, y = own // self.side, own % self.side
        offsets = jnp.arange(self.depth * self.side, dtype=jnp.int32)
        a, b = offsets // self.side, offsets % self.side
        both = []
        for sign in (-1, 1):
            deep = (z + sign * a + self.depth) % self.depth
            both.append(deep * self.side + (y + sign * b + self.side) % self.side)
        return jnp.concatenate(both).astype(jnp.int32)


def gather_columns(grid, own):
    columns = {0: own}
    half = grid.depth // 2
    for a in range(1, grid.depth - half + 1):
        columns[a] = grid.send(columns[a - 1], 1, 0)
        back = grid.depth - a
        if back > a:
            columns[back] = grid.send(columns[(back + 1) % grid.depth], -1, 0)
    return columns


def scatter_order(grid):
    order = []
    for a in range(grid.depth - grid.depth // 2, 0, -1):
        order.append(a)
        if grid.depth - a > a:
            order.append(grid.depth - a)
    return order + [0]


def scatter_sum(grid, own_rows, chunks, aside):
    order = scatter_order(grid)
    crossed = {
        a: [grid.send(chunks[a, b], 0, b) for b in range(1, grid.side)] for a in order
    }
    half = grid.depth - grid.depth // 2
    arriving = {a: [] for a in order}
    waiting = []
    for n, a in enumerate(order):
        parts = [chunks[a, 0], *crossed[a], *arriving[a]]
        if a == 0:
            aside(n, [*crossed[a], chunks[a, 0]][0])
            return combine([own_rows, *parts], waiting)
        part = combine(parts, waiting)
        step = 1 if a <= half else -1
        arriving[(a - step) % grid.depth].append(grid.send(part, step, 0))
        waiting = aside(n, part)


def sum_selectors(grid, partials):
    total = sum(partial.astype(F32) for partial in partials)
    pairs = []
    bit = 1
    while True:
        rounded = total.astype(BF16)
        arrived = grid.swap(rounded, bit) if bit < grid.depth else jnp.zeros_like(rounded)
        pairs.append((rounded, arrived))
        bit *= 2
        if bit >= grid.depth:
            return pairs
        total = rounded.astype(F32) + arrived.astype(F32)


def per_device(
    n_tp, tokens, norm_gain, w_in, w_low, w_dt, a_rate, dt_bias, skip_gain, threshold, w_out
):
    grid = Grid(n_tp)
    feat = tokens.shape[1]
    layers, width, _, chans = w_in.shape
    states = a_rate.shape[1]
    rank = w_dt.shape[1]
    fold = chans // LANES
    table = grid.table()
    forth = lambda a, b: n_tp + a * grid.side + b
    seq_place = lax.axis_index("seq").astype(jnp.int32).reshape(1)
    rates = (a_rate * (-math.log2(math.e))).reshape(layers, states, fold, LANES)
    w_raw = w_in.reshape(layers, width, 2, fold, LANES).transpose(0, 1, 3, 2, 4)
    w_raw = w_raw.reshape(layers, width * 2 * fold, LANES)
    order = scatter_order(grid)
    own_rows = tokens
    low_t = jnp.swapaxes(w_low, 1, 2)
    arrivals = [0] + [a for a in order if a not in (0, order[0])] + order[:1]
    weights = {}
    for layer in range(layers):
        columns = gather_columns(grid, own_rows)
        cross = lambda column: [grid.send(column, 0, b) for b in range(1, grid.side)]
        packed = layer > 0
        if packed:
            low = project_low(layer, table, own_rows, norm_gain, low_t, feat, [])
            beside = {0: cross(low)}
            lows = [each[:, feat:] for each in (low, *beside[0])]
        else:
            beside = {0: cross(own_rows)}
            low = project_low(layer, table, own_rows, norm_gain, low_t, 0, beside[0])
            lows = [low, *cross(low)]
            weights[0], _ = unpack(layer, table, 0, grid.side, feat, chans, w_raw, [])
        pairs = sum_selectors(grid, lows)
        stages = [own for own, _ in pairs]
        state = None
        for n, a in enumerate(arrivals):
            if n:
                last = n + 1 == len(arrivals)
                beside[a] = cross(relay(columns[a], *first) if last else columns[a])
            arrived = [columns[a], *beside[a]]
            place, earlier = a * grid.side, stages[n - 1 : n] if n else []
            if a in weights:
                state = project_ready(
                    layer, arrived, table, place, norm_gain, weights[a], state, earlier
                )
            else:
                state = project(
                    layer, arrived, table, place, norm_gain, w_raw, chans, state, earlier
                )
            if n == 0:
                first = [state[2], *stages[1:2]] if packed else [state[2]]
        cur, gate, square = state
        low, selectors = finish_low(rank, *pairs[-1], [square])
        out, time, final = local_scan(
            layer, width, selectors, low, square, cur, w_dt, dt_bias, rates
        )
        finals = lax.all_gather(final, "seq")
        keys = [(a, b) for a in order for b in range(1, grid.side)]
        keys += [(a, 0) for a in order]
        lead = grid.side - 1
        gated, chunks = close_layer(
            layer,
            width,
            table,
            [forth(*key) for key in keys[:lead]],
            feat,
            seq_place,
            selectors,
            (out, time, cur, gate, square, finals),
            rates,
            skip_gain,
            threshold,
            w_out,
        )
        chunks = dict(zip(keys, chunks))
        split = len(order) * lead + 1
        for part in (keys[lead:split], keys[split:]):
            more = expand(layer, table, [forth(*key) for key in part], feat, gated, w_out)
            chunks.update(zip(part, more))
        weights = {}

        def aside(n, value):
            left = [a for a in arrivals if a not in weights]
            wanted = [1, 0, len(left) - 1, 1][min(n, 3)] if layer + 1 < layers else 0
            tokens = []
            for a in left[:wanted]:
                weights[a], token = unpack(
                    layer + 1, table, a * grid.side, grid.side, feat, chans, w_raw, [value]
                )
                tokens.append(token)
            return tokens

        own_rows = scatter_sum(grid, own_rows, chunks, aside)
    return own_rows


def solution(mesh):
    in_specs = (
        P("seq", "tp"),
        P(),
        P(None, None, None, "tp"),
        P(None, "tp", None),
        P(None, None, "tp"),
        P(None, None, "tp"),
        P(None, "tp"),
        P(None, "tp"),
        P(None, "tp"),
        P(None, "tp", None),
    )
    return jax.shard_map(
        functools.partial(per_device, mesh.shape["tp"]),
        mesh=mesh,
        in_specs=in_specs,
        out_specs=P("seq", "tp"),
        check_vma=False,
    )
```

```python
import functools
import math

import jax
import jax.numpy as jnp
from jax import lax
from jax.experimental import pallas as pl
from jax.experimental.pallas import tpu as pltpu
from jax.sharding import PartitionSpec as P

LANES = 128
WIDE = 256
STRIDE = 3
EPS = 1e-05
DEPTH = 4
F32 = jnp.float32
BF16 = jnp.bfloat16
VMEM = pl.BlockSpec(memory_space=pltpu.VMEM)
SMEM = pl.BlockSpec(memory_space=pltpu.SMEM)
HBM = pl.BlockSpec(memory_space=pltpu.HBM)
ANY = pl.BlockSpec(memory_space=pl.ANY)
COST = pl.CostEstimate(flops=1, bytes_accessed=1, transcendentals=0)
LONG = pl.CostEstimate(flops=10**10, bytes_accessed=1, transcendentals=0)


def row_factor(square_sum, width):
    return lax.rsqrt(square_sum / width + EPS)


def fold_stride(count):
    return STRIDE * count + 1


def params(mebibytes):
    return pltpu.CompilerParams(vmem_limit_bytes=mebibytes * 1024 * 1024)


def proj_kernel(count, first, layer, table_at, table_ref, *refs):
    shards = refs[:count]
    gain_ref, w_ref = refs[count : count + 2]
    raw_s, split_s, sems = refs[-3:]
    cur_ref, gate_ref, square_ref = refs[-6:-3]
    rows, width = shards[0].shape
    chans = cur_ref.shape[1]
    pieces, size, _ = raw_s.shape
    pieces //= count
    per = 2 * chans // LANES
    depth = size // per
    apart = fold_stride(depth)
    taken = max(per, 16)
    places = [table_ref[table_at + j] for j in range(count)]

    def copy(j, q):
        n = j * pieces + q
        begin = (places[j] * width + q * depth) * per
        source = w_ref.at[layer, pl.ds(pl.multiple_of(begin, size), size), :]
        return pltpu.make_async_copy(source, raw_s.at[n], sems.at[n])

    for j in range(count):
        for q in range(pieces):
            copy(j, q).start()
    squares = jnp.zeros((rows, 1), F32) if first else square_ref[...]
    for j in range(count):
        values = shards[j][:, :width].astype(F32)
        gain = gain_ref[layer : layer + 1, pl.ds(pl.multiple_of(places[j] * width, width), width)]
        left = (values * gain).astype(BF16)
        squares = squares + jnp.sum(values * values, axis=1, keepdims=True)
        for q in range(pieces):
            copy(j, q).wait()
            slot = (j * pieces + q) % split_s.shape[0]
            for begin in range(0, size, taken):
                part = raw_s[j * pieces + q, begin : begin + taken, :].astype(F32)
                for k in range(taken // per):
                    d = begin // per + k
                    place = pl.ds(d * STRIDE, per, stride=apart)
                    split_s[slot, place, :] = part[k * per : (k + 1) * per]
        for e, out in enumerate((cur_ref, gate_ref)):
            for begin in range(0, chans, WIDE):
                tiles = [
                    jnp.concatenate(
                        [
                            split_s[
                                (j * pieces + q) % split_s.shape[0],
                                pl.ds((2 * t + e) * apart, depth, stride=STRIDE),
                                :,
                            ].astype(BF16)
                            for q in range(pieces)
                        ],
                        axis=0,
                    )
                    for t in range(begin // LANES, (begin + WIDE) // LANES)
                ]
                product = jnp.dot(left, jnp.concatenate(tiles, axis=1), preferred_element_type=F32)
                cols = slice(begin, begin + WIDE)
                if first and j == 0:
                    out[:, cols] = product
                else:
                    out[:, cols] += product
    square_ref[...] = squares


def project(layer, shards, table, table_at, norm_gain, w_raw, chans, before, earlier):
    count = len(shards)
    rows, width = shards[0].shape
    depth = min(width, WIDE)
    pieces = count * (width // depth)
    per = 2 * chans // LANES
    shapes = [(rows, chans), (rows, chans), (rows, 1)]
    operands = [table, *shards, norm_gain, w_raw]
    in_specs = [SMEM] + [VMEM] * (count + 1) + [HBM]
    aliases = {}
    if before is not None:
        aliases = {len(operands) + j: j for j in range(len(shapes))}
        in_specs += [VMEM] * len(shapes)
        operands += list(before)
    in_specs += [ANY] * len(earlier)
    operands += earlier
    return pl.pallas_call(
        functools.partial(proj_kernel, count, before is None, layer, table_at),
        out_shape=[jax.ShapeDtypeStruct(shape, F32) for shape in shapes],
        in_specs=in_specs,
        out_specs=[VMEM] * len(shapes),
        scratch_shapes=[
            pltpu.VMEM((pieces, depth * per, LANES), BF16),
            pltpu.VMEM((pieces, per * fold_stride(depth), LANES), F32),
            pltpu.SemaphoreType.DMA((pieces,)),
        ],
        input_output_aliases=aliases,
        compiler_params=params(36),
        cost_estimate=LONG,
        name="project",
    )(*operands)


def unpack_kernel(count, layer, table_at, width, table_ref, w_ref, *refs):
    out_ref, token_ref, raw_s, split_s, sems = refs[-5:]
    pieces, size, _ = raw_s.shape
    chans = out_ref.shape[2]
    per = 2 * chans // LANES
    depth = size // per
    apart = fold_stride(depth)
    taken = max(per, 16)
    each = width // depth

    def copy(n):
        begin = (table_ref[table_at + n // each] * width + n % each * depth) * per
        source = w_ref.at[layer, pl.ds(pl.multiple_of(begin, size), size), :]
        return pltpu.make_async_copy(source, raw_s.at[n], sems.at[n])

    for n in range(pieces):
        copy(n).start()
    token_ref[...] = jnp.zeros_like(token_ref)
    for n in range(pieces):
        copy(n).wait()
        slot = n % split_s.shape[0]
        for begin in range(0, size, taken):
            part = raw_s[n, begin : begin + taken, :].astype(F32)
            for k in range(taken // per):
                place = pl.ds((begin // per + k) * STRIDE, per, stride=apart)
                split_s[slot, place, :] = part[k * per : (k + 1) * per]
        for e in range(2):
            for begin in range(0, chans, WIDE):
                tiles = [
                    split_s[slot, pl.ds((2 * t + e) * apart, depth, stride=STRIDE), :].astype(BF16)
                    for t in range(begin // LANES, (begin + WIDE) // LANES)
                ]
                rows = slice(n * depth, (n + 1) * depth)
                out_ref[e, rows, begin : begin + WIDE] = jnp.concatenate(tiles, axis=1)


def unpack(layer, table, table_at, count, width, chans, w_raw, earlier):
    depth = min(width, WIDE)
    pieces = count * width // depth
    per = 2 * chans // LANES
    return pl.pallas_call(
        functools.partial(unpack_kernel, count, layer, table_at, width),
        out_shape=[
            jax.ShapeDtypeStruct((2, count * width, chans), BF16),
            jax.ShapeDtypeStruct((8, LANES), F32),
        ],
        in_specs=[SMEM, HBM] + [ANY] * len(earlier),
        out_specs=[VMEM, VMEM],
        scratch_shapes=[
            pltpu.VMEM((pieces, depth * per, LANES), BF16),
            pltpu.VMEM((2, per * fold_stride(depth), LANES), F32),
            pltpu.SemaphoreType.DMA((pieces,)),
        ],
        compiler_params=params(24),
        cost_estimate=COST,
        name="unpack",
    )(table, w_raw, *earlier)


def ready_kernel(count, first, layer, table_at, table_ref, *refs):
    shards = refs[:count]
    gain_ref, w_ref = refs[count : count + 2]
    cur_ref, gate_ref, square_ref = refs[-3:]
    rows, width = shards[0].shape
    chans = cur_ref.shape[1]
    squares = jnp.zeros((rows, 1), F32) if first else square_ref[...]
    parts = []
    for j in range(count):
        values = shards[j][:, :width].astype(F32)
        begin = pl.multiple_of(table_ref[table_at + j] * width, width)
        parts.append((values * gain_ref[layer : layer + 1, pl.ds(begin, width)]).astype(BF16))
        squares = squares + jnp.sum(values * values, axis=1, keepdims=True)
    square_ref[...] = squares
    left = jnp.concatenate(parts, axis=1)
    for e, out in enumerate((cur_ref, gate_ref)):
        for begin in range(0, chans, WIDE):
            cols = slice(begin, begin + WIDE)
            product = jnp.dot(left, w_ref[e, :, cols], preferred_element_type=F32)
            if first:
                out[:, cols] = product
            else:
                out[:, cols] += product


def project_ready(layer, shards, table, table_at, norm_gain, weights, before, earlier):
    count = len(shards)
    rows, width = shards[0].shape
    chans = weights.shape[2]
    state = [jax.ShapeDtypeStruct(s, F32) for s in ((rows, chans), (rows, chans), (rows, 1))]
    operands = [table, *shards, norm_gain, weights]
    in_specs = [SMEM] + [VMEM] * (count + 2)
    aliases = {}
    if before is not None:
        aliases = {len(operands) + j: j for j in range(3)}
        in_specs += [VMEM] * 3
        operands += list(before)
    return pl.pallas_call(
        functools.partial(ready_kernel, count, before is None, layer, table_at),
        out_shape=state,
        in_specs=in_specs + [ANY] * len(earlier),
        out_specs=[VMEM] * 3,
        input_output_aliases=aliases,
        compiler_params=params(12),
        cost_estimate=LONG,
        name="project_ready",
    )(*operands, *earlier)


def low_kernel(layer, table_ref, rows_ref, gain_ref, w_ref, *refs):
    width = rows_ref.shape[1]
    begin = pl.multiple_of(table_ref[0] * width, width)
    gain = gain_ref[layer : layer + 1, pl.ds(begin, width)]
    scaled = (rows_ref[...].astype(F32) * gain).astype(BF16)
    product = lax.dot_general(
        scaled, w_ref[layer], (((1,), (1,)), ((), ())), preferred_element_type=F32
    )
    out_ref = refs[-1]
    before = out_ref.shape[1] - product.shape[1]
    if before:
        out_ref[:, :before] = rows_ref[...]
    out_ref[:, before:] = product.astype(BF16)


def project_low(layer, table, own_rows, norm_gain, w_low, before, earlier):
    rows = own_rows.shape[0]
    return pl.pallas_call(
        functools.partial(low_kernel, layer),
        out_shape=jax.ShapeDtypeStruct((rows, before + w_low.shape[1]), BF16),
        in_specs=[SMEM] + [VMEM] * 3 + [ANY] * len(earlier),
        out_specs=VMEM,
        compiler_params=params(12),
        cost_estimate=COST,
        name="project_low",
    )(table, own_rows, norm_gain, w_low, *earlier)


def relay_kernel(value_ref, *refs):
    refs[-1][...] = value_ref[...]


def relay(value, *others):
    return pl.pallas_call(
        relay_kernel,
        out_shape=jax.ShapeDtypeStruct(value.shape, value.dtype),
        in_specs=[VMEM] + [ANY] * len(others),
        out_specs=VMEM,
        compiler_params=params(8),
        cost_estimate=COST,
        name="relay",
    )(value, *others)


def scan_kernel(
    layer,
    states,
    width,
    sel_ref,
    low_ref,
    square_ref,
    cur_ref,
    w_dt_ref,
    bias_ref,
    rate_ref,
    out_ref,
    time_ref,
    final_ref,
    step_s,
    drive_s,
):
    rows, chans = cur_ref.shape
    fold = chans // LANES
    rank = w_dt_ref.shape[1]
    factor = row_factor(square_ref[...], width)
    rank_part = (low_ref[:, :rank] * factor).astype(BF16)
    apart = fold_stride(rows)
    twice = factor * factor
    for begin in range(0, chans, WIDE):
        cols = slice(begin, begin + WIDE)
        pre = jnp.dot(rank_part, w_dt_ref[layer, :, cols], preferred_element_type=F32)
        pre = pre + bias_ref[layer : layer + 1, cols]
        step = jnp.maximum(pre, 0.0) + jnp.log1p(jnp.exp(-jnp.abs(pre)))
        drive = step * (cur_ref[:, cols] * twice)
        for q in range(WIDE // LANES):
            part = slice(q * LANES, (q + 1) * LANES)
            place = pl.ds((begin // LANES + q) * apart, rows, stride=STRIDE)
            step_s[place, :] = step[:, part]
            drive_s[place, :] = drive[:, part]

    def advance(t, carried):
        time, held = carried
        here = pl.ds(t * STRIDE, fold, stride=apart)
        step = step_s[here, :]
        drive = drive_s[here, :]
        sums = [None] * 4
        after = []
        for s in range(states):
            decay = jnp.exp2(step * rate_ref[layer, s])
            now = decay * held[s] + drive * sel_ref[t, s]
            term = now * sel_ref[t, states + s]
            sums[s % 4] = term if sums[s % 4] is None else sums[s % 4] + term
            after.append(now)
        time = time + step
        out_ref[here, :] = (sums[0] + sums[1]) + (sums[2] + sums[3])
        time_ref[here, :] = time
        return time, tuple(after)

    zero = jnp.zeros((fold, LANES), F32)
    time, held = lax.fori_loop(0, rows, advance, (zero, (zero,) * states), unroll=8)
    for s in range(states):
        final_ref[s] = held[s].astype(BF16)
    final_ref[states] = time.astype(BF16)


def local_scan(layer, width, selectors, low, square, cur, w_dt, dt_bias, rate):
    rows, chans = cur.shape
    _, states, fold, _ = rate.shape
    folded = (fold * fold_stride(rows), LANES)
    return pl.pallas_call(
        functools.partial(scan_kernel, layer, states, width),
        out_shape=[
            jax.ShapeDtypeStruct(folded, F32),
            jax.ShapeDtypeStruct(folded, F32),
            jax.ShapeDtypeStruct((states + 1, fold, LANES), BF16),
        ],
        in_specs=[SMEM] + [VMEM] * 6,
        out_specs=[VMEM] * 3,
        scratch_shapes=[pltpu.VMEM(folded, F32), pltpu.VMEM(folded, F32)],
        compiler_params=params(20),
        cost_estimate=COST,
        name="local_scan",
    )(selectors, low, square, cur, w_dt, dt_bias, rate)


def emit_chunks(layer, table_at, feat, gated_ref, table_ref, w_ref, chunks, w_s, sems, before=None):
    def copy(j):
        begin = pl.multiple_of(table_ref[table_at[j]] * feat, feat)
        return pltpu.make_async_copy(w_ref.at[layer, :, pl.ds(begin, feat)], w_s.at[j], sems.at[j])

    for j in range(len(chunks)):
        copy(j).start()
    if before is not None:
        before()
    for j, chunk in enumerate(chunks):
        copy(j).wait()
        for begin in range(0, feat, WIDE):
            cols = slice(begin, begin + WIDE)
            chunk[:, cols] = jnp.dot(
                gated_ref[...], w_s[j, :, cols], preferred_element_type=F32
            ).astype(BF16)


def close_kernel(layer, states, table_at, feat, width, table_ref, place_ref, sel_ref, *refs):
    out_ref, time_ref, cur_ref, gate_ref, square_ref, final_ref = refs[:6]
    rate_ref, skip_ref, thresh_ref, w_ref, gated_ref = refs[6:11]
    chunks = refs[11 : 11 + len(table_at)]
    enter_s, mixed_s, w_s, sems = refs[-4:]
    rows, chans = cur_ref.shape
    fold = chans // LANES
    apart = fold_stride(rows)

    def gate_all():
        def enter(p, state):
            time = final_ref[p, states].astype(F32)
            return tuple(
                jnp.exp2(time * rate_ref[layer, s]) * state[s] + final_ref[p, s].astype(F32)
                for s in range(states)
            )

        zero = jnp.zeros((fold, LANES), F32)
        state = lax.fori_loop(0, place_ref[0], enter, (zero,) * states)
        for s in range(states):
            enter_s[s] = state[s]

        def correct(t, carried):
            here = pl.ds(t * STRIDE, fold, stride=apart)
            time = time_ref[here, :]
            sums = [out_ref[here, :], None, None, None]
            for s in range(states):
                term = jnp.exp2(time * rate_ref[layer, s]) * (enter_s[s] * sel_ref[t, states + s])
                sums[s % 4] = term if sums[s % 4] is None else sums[s % 4] + term
            mixed_s[here, :] = (sums[0] + sums[1]) + (sums[2] + sums[3])
            return carried

        lax.fori_loop(0, rows, correct, 0, unroll=8)

        factor = row_factor(square_ref[...], width)
        for r in range(fold):
            cols = slice(r * LANES, (r + 1) * LANES)
            skip = skip_ref[layer : layer + 1, cols]
            mixed = mixed_s[pl.ds(r * apart, rows, stride=STRIDE), :] + skip * cur_ref[:, cols]
            mixed = mixed * factor
            normal = mixed * lax.rsqrt(jnp.mean(mixed * mixed, axis=1, keepdims=True) + EPS)
            thresh = thresh_ref[layer : layer + 1, cols]
            shrunk = jnp.maximum(normal - thresh, 0.0) - jnp.maximum(-normal - thresh, 0.0)
            gate = gate_ref[:, cols] * factor
            gated_ref[:, cols] = (shrunk * (gate * jax.nn.sigmoid(gate))).astype(BF16)

    emit_chunks(layer, table_at, feat, gated_ref, table_ref, w_ref, chunks, w_s, sems, gate_all)


def close_layer(
    layer, width, table, table_at, feat, seq_place, selectors, values, rate, skip, thresh, w_out
):
    rows, chans = values[2].shape
    _, states, fold, _ = rate.shape
    count = len(table_at)
    chunk = jax.ShapeDtypeStruct((rows, feat), BF16)
    results = pl.pallas_call(
        functools.partial(close_kernel, layer, states, table_at, feat, width),
        out_shape=[jax.ShapeDtypeStruct((rows, chans), BF16)] + [chunk] * count,
        in_specs=[SMEM] * 3 + [VMEM] * 9 + [HBM],
        out_specs=[VMEM] * (1 + count),
        scratch_shapes=[
            pltpu.VMEM((states, fold, LANES), F32),
            pltpu.VMEM((fold * fold_stride(rows), LANES), F32),
            pltpu.VMEM((count, chans, feat), BF16),
            pltpu.SemaphoreType.DMA((count,)),
        ],
        compiler_params=params(40),
        cost_estimate=COST,
        name="close_layer",
    )(table, seq_place, selectors, *values, rate, skip, thresh, w_out)
    return results[0], results[1:]


def expand_kernel(layer, table_at, feat, table_ref, gated_ref, w_ref, *refs):
    chunks = refs[: len(table_at)]
    emit_chunks(layer, table_at, feat, gated_ref, table_ref, w_ref, chunks, *refs[-2:])


def expand(layer, table, table_at, feat, gated, w_out):
    rows, chans = gated.shape
    count = len(table_at)
    return pl.pallas_call(
        functools.partial(expand_kernel, layer, table_at, feat),
        out_shape=[jax.ShapeDtypeStruct((rows, feat), BF16)] * count,
        in_specs=[SMEM, VMEM, HBM],
        out_specs=[VMEM] * count,
        scratch_shapes=[
            pltpu.VMEM((count, chans, feat), BF16),
            pltpu.SemaphoreType.DMA((count,)),
        ],
        compiler_params=params(40),
        cost_estimate=COST,
        name="expand",
    )(table, gated, w_out)


def finish_kernel(rank, own_ref, arrived_ref, *refs):
    low_ref, selectors_ref = refs[-2:]
    total = own_ref[...].astype(F32) + arrived_ref[...].astype(F32)
    low_ref[...] = total
    selectors_ref[...] = total[:, rank:]


def finish_low(rank, own, arrived, earlier):
    rows, count = own.shape
    return pl.pallas_call(
        functools.partial(finish_kernel, rank),
        out_shape=[
            jax.ShapeDtypeStruct((rows, count), F32),
            jax.ShapeDtypeStruct((rows, count - rank), F32),
        ],
        in_specs=[VMEM] * 2 + [ANY] * len(earlier),
        out_specs=[VMEM] * 2,
        compiler_params=params(8),
        cost_estimate=COST,
        name="finish_low",
    )(own, arrived, *earlier)


def combine_kernel(count, *refs):
    total = refs[0][...].astype(F32)
    for ref in refs[1:count]:
        total = total + ref[...].astype(F32)
    refs[-1][...] = total.astype(BF16)


def combine(values, earlier):
    return pl.pallas_call(
        functools.partial(combine_kernel, len(values)),
        out_shape=jax.ShapeDtypeStruct(values[0].shape, BF16),
        in_specs=[VMEM] * len(values) + [ANY] * len(earlier),
        out_specs=VMEM,
        compiler_params=params(8),
        cost_estimate=COST,
        name="combine",
    )(*values, *earlier)


class Grid:
    def __init__(self, count):
        self.depth = DEPTH if count % DEPTH == 0 else 1
        self.side = count // self.depth

    def places(self):
        return [(z, y) for z in range(self.depth) for y in range(self.side)]

    def at(self, z, y):
        return (z % self.depth) * self.side + y % self.side

    def send(self, value, deep, across):
        pairs = [(self.at(z, y), self.at(z + deep, y + across)) for z, y in self.places()]
        return lax.ppermute(value, "tp", pairs)

    def swap(self, value, bit):
        pairs = [(self.at(z, y), self.at(z ^ bit, y)) for z, y in self.places()]
        return lax.ppermute(value, "tp", pairs)

    def table(self):
        own = lax.axis_index("tp")
        z, y = own // self.side, own % self.side
        offsets = jnp.arange(self.depth * self.side, dtype=jnp.int32)
        a, b = offsets // self.side, offsets % self.side
        both = []
        for sign in (-1, 1):
            deep = (z + sign * a + self.depth) % self.depth
            both.append(deep * self.side + (y + sign * b + self.side) % self.side)
        return jnp.concatenate(both).astype(jnp.int32)


def gather_columns(grid, own):
    columns = {0: own}
    half = grid.depth // 2
    for a in range(1, grid.depth - half + 1):
        columns[a] = grid.send(columns[a - 1], 1, 0)
        back = grid.depth - a
        if back > a:
            columns[back] = grid.send(columns[(back + 1) % grid.depth], -1, 0)
    return columns


def scatter_order(grid):
    order = []
    for a in range(grid.depth - grid.depth // 2, 0, -1):
        order.append(a)
        if grid.depth - a > a:
            order.append(grid.depth - a)
    return order + [0]


def scatter_sum(grid, own_rows, chunks, aside):
    order = scatter_order(grid)
    crossed = {
        a: [grid.send(chunks[a, b], 0, b) for b in range(1, grid.side)] for a in order
    }
    half = grid.depth - grid.depth // 2
    arriving = {a: [] for a in order}
    waiting = []
    for n, a in enumerate(order):
        parts = [chunks[a, 0], *crossed[a], *arriving[a]]
        if a == 0:
            aside(n, [*crossed[a], chunks[a, 0]][0])
            return combine([own_rows, *parts], waiting)
        part = combine(parts, waiting)
        step = 1 if a <= half else -1
        arriving[(a - step) % grid.depth].append(grid.send(part, step, 0))
        waiting = aside(n, part)


def sum_selectors(grid, partials):
    total = sum(partial.astype(F32) for partial in partials)
    pairs = []
    bit = 1
    while True:
        rounded = total.astype(BF16)
        arrived = grid.swap(rounded, bit) if bit < grid.depth else jnp.zeros_like(rounded)
        pairs.append((rounded, arrived))
        bit *= 2
        if bit >= grid.depth:
            return pairs
        total = rounded.astype(F32) + arrived.astype(F32)


def per_device(
    n_tp, tokens, norm_gain, w_in, w_low, w_dt, a_rate, dt_bias, skip_gain, threshold, w_out
):
    grid = Grid(n_tp)
    feat = tokens.shape[1]
    layers, width, _, chans = w_in.shape
    states = a_rate.shape[1]
    rank = w_dt.shape[1]
    fold = chans // LANES
    table = grid.table()
    forth = lambda a, b: n_tp + a * grid.side + b
    seq_place = lax.axis_index("seq").astype(jnp.int32).reshape(1)
    rates = (a_rate * (-math.log2(math.e))).reshape(layers, states, fold, LANES)
    w_raw = w_in.reshape(layers, width, 2, fold, LANES).transpose(0, 1, 3, 2, 4)
    w_raw = w_raw.reshape(layers, width * 2 * fold, LANES)
    order = scatter_order(grid)
    own_rows = tokens
    low_t = jnp.swapaxes(w_low, 1, 2)
    arrivals = [0] + [a for a in order if a not in (0, order[0])] + order[:1]
    weights = {}
    for layer in range(layers):
        columns = gather_columns(grid, own_rows)
        cross = lambda column: [grid.send(column, 0, b) for b in range(1, grid.side)]
        packed = layer > 0
        if packed:
            low = project_low(layer, table, own_rows, norm_gain, low_t, feat, [])
            beside = {0: cross(low)}
            lows = [each[:, feat:] for each in (low, *beside[0])]
        else:
            beside = {0: cross(own_rows)}
            low = project_low(layer, table, own_rows, norm_gain, low_t, 0, beside[0])
            lows = [low, *cross(low)]
            weights[0], _ = unpack(layer, table, 0, grid.side, feat, chans, w_raw, [rates])
        pairs = sum_selectors(grid, lows)
        stages = [own for own, _ in pairs]
        state = None
        for n, a in enumerate(arrivals):
            if n:
                last = n + 1 == len(arrivals)
                beside[a] = cross(relay(columns[a], *first) if last else columns[a])
            arrived = [columns[a], *beside[a]]
            place, earlier = a * grid.side, stages[n - 1 + packed : n + packed] if n else []
            if a in weights:
                state = project_ready(
                    layer, arrived, table, place, norm_gain, weights[a], state, earlier
                )
            else:
                state = project(
                    layer, arrived, table, place, norm_gain, w_raw, chans, state, earlier
                )
            if n == 0:
                first = [state[2]]
        cur, gate, square = state
        low, selectors = finish_low(rank, *pairs[-1], [square])
        out, time, final = local_scan(
            layer, width, selectors, low, square, cur, w_dt, dt_bias, rates
        )
        finals = lax.all_gather(final, "seq")
        keys = [(a, b) for a in order for b in range(1, grid.side)]
        keys += [(a, 0) for a in order]
        lead = grid.side - 1
        gated, chunks = close_layer(
            layer,
            width,
            table,
            [forth(*key) for key in keys[:lead]],
            feat,
            seq_place,
            selectors,
            (out, time, cur, gate, square, finals),
            rates,
            skip_gain,
            threshold,
            w_out,
        )
        chunks = dict(zip(keys, chunks))
        split = len(order) * lead + 1
        for part in (keys[lead:split], keys[split:]):
            more = expand(layer, table, [forth(*key) for key in part], feat, gated, w_out)
            chunks.update(zip(part, more))
        weights = {}

        def aside(n, value):
            left = [a for a in arrivals if a not in weights]
            wanted = [1, 0, len(left) - 1, 1][min(n, 3)] if layer + 1 < layers else 0
            tokens = []
            for a in left[:wanted]:
                weights[a], token = unpack(
                    layer + 1, table, a * grid.side, grid.side, feat, chans, w_raw, [value]
                )
                tokens.append(token)
            return tokens

        own_rows = scatter_sum(grid, own_rows, chunks, aside)
    return own_rows


def solution(mesh):
    in_specs = (
        P("seq", "tp"),
        P(),
        P(None, None, None, "tp"),
        P(None, "tp", None),
        P(None, None, "tp"),
        P(None, None, "tp"),
        P(None, "tp"),
        P(None, "tp"),
        P(None, "tp"),
        P(None, "tp", None),
    )
    return jax.shard_map(
        functools.partial(per_device, mesh.shape["tp"]),
        mesh=mesh,
        in_specs=in_specs,
        out_specs=P("seq", "tp"),
        check_vma=False,
    )
```

```python
import functools
import math

import jax
import jax.numpy as jnp
from jax import lax
from jax.experimental import pallas as pl
from jax.experimental.pallas import tpu as pltpu
from jax.sharding import PartitionSpec as P

LANES = 128
WIDE = 256
STRIDE = 3
EPS = 1e-05
DEPTH = 4
F32 = jnp.float32
BF16 = jnp.bfloat16
VMEM = pl.BlockSpec(memory_space=pltpu.VMEM)
SMEM = pl.BlockSpec(memory_space=pltpu.SMEM)
HBM = pl.BlockSpec(memory_space=pltpu.HBM)
ANY = pl.BlockSpec(memory_space=pl.ANY)
COST = pl.CostEstimate(flops=1, bytes_accessed=1, transcendentals=0)
LONG = pl.CostEstimate(flops=10**10, bytes_accessed=1, transcendentals=0)


def row_factor(square_sum, width):
    return lax.rsqrt(square_sum / width + EPS)


def fold_stride(count):
    return STRIDE * count + 1


def params(mebibytes):
    return pltpu.CompilerParams(vmem_limit_bytes=mebibytes * 1024 * 1024)


def proj_kernel(count, first, layer, table_at, table_ref, *refs):
    shards = refs[:count]
    gain_ref, w_ref = refs[count : count + 2]
    raw_s, split_s, sems = refs[-3:]
    cur_ref, gate_ref, square_ref = refs[-6:-3]
    rows, width = shards[0].shape
    chans = cur_ref.shape[1]
    pieces, size, _ = raw_s.shape
    pieces //= count
    per = 2 * chans // LANES
    depth = size // per
    apart = fold_stride(depth)
    taken = max(per, 16)
    places = [table_ref[table_at + j] for j in range(count)]

    def copy(j, q):
        n = j * pieces + q
        begin = (places[j] * width + q * depth) * per
        source = w_ref.at[layer, pl.ds(pl.multiple_of(begin, size), size), :]
        return pltpu.make_async_copy(source, raw_s.at[n], sems.at[n])

    for j in range(count):
        for q in range(pieces):
            copy(j, q).start()
    squares = jnp.zeros((rows, 1), F32) if first else square_ref[...]
    for j in range(count):
        values = shards[j][:, :width].astype(F32)
        gain = gain_ref[layer : layer + 1, pl.ds(pl.multiple_of(places[j] * width, width), width)]
        left = (values * gain).astype(BF16)
        squares = squares + jnp.sum(values * values, axis=1, keepdims=True)
        for q in range(pieces):
            copy(j, q).wait()
            slot = (j * pieces + q) % split_s.shape[0]
            for begin in range(0, size, taken):
                part = raw_s[j * pieces + q, begin : begin + taken, :].astype(F32)
                for k in range(taken // per):
                    d = begin // per + k
                    place = pl.ds(d * STRIDE, per, stride=apart)
                    split_s[slot, place, :] = part[k * per : (k + 1) * per]
        for e, out in enumerate((cur_ref, gate_ref)):
            for begin in range(0, chans, WIDE):
                tiles = [
                    jnp.concatenate(
                        [
                            split_s[
                                (j * pieces + q) % split_s.shape[0],
                                pl.ds((2 * t + e) * apart, depth, stride=STRIDE),
                                :,
                            ].astype(BF16)
                            for q in range(pieces)
                        ],
                        axis=0,
                    )
                    for t in range(begin // LANES, (begin + WIDE) // LANES)
                ]
                product = jnp.dot(left, jnp.concatenate(tiles, axis=1), preferred_element_type=F32)
                cols = slice(begin, begin + WIDE)
                if first and j == 0:
                    out[:, cols] = product
                else:
                    out[:, cols] += product
    square_ref[...] = squares


def project(layer, shards, table, table_at, norm_gain, w_raw, chans, before, earlier):
    count = len(shards)
    rows, width = shards[0].shape
    depth = min(width, WIDE)
    pieces = count * (width // depth)
    per = 2 * chans // LANES
    shapes = [(rows, chans), (rows, chans), (rows, 1)]
    operands = [table, *shards, norm_gain, w_raw]
    in_specs = [SMEM] + [VMEM] * (count + 1) + [HBM]
    aliases = {}
    if before is not None:
        aliases = {len(operands) + j: j for j in range(len(shapes))}
        in_specs += [VMEM] * len(shapes)
        operands += list(before)
    in_specs += [ANY] * len(earlier)
    operands += earlier
    return pl.pallas_call(
        functools.partial(proj_kernel, count, before is None, layer, table_at),
        out_shape=[jax.ShapeDtypeStruct(shape, F32) for shape in shapes],
        in_specs=in_specs,
        out_specs=[VMEM] * len(shapes),
        scratch_shapes=[
            pltpu.VMEM((pieces, depth * per, LANES), BF16),
            pltpu.VMEM((pieces, per * fold_stride(depth), LANES), F32),
            pltpu.SemaphoreType.DMA((pieces,)),
        ],
        input_output_aliases=aliases,
        compiler_params=params(36),
        cost_estimate=LONG,
        name="project",
    )(*operands)


def unpack_kernel(count, layer, table_at, width, table_ref, w_ref, *refs):
    out_ref, token_ref, raw_s, split_s, sems = refs[-5:]
    pieces, size, _ = raw_s.shape
    chans = out_ref.shape[2]
    per = 2 * chans // LANES
    depth = size // per
    apart = fold_stride(depth)
    taken = max(per, 16)
    each = width // depth

    def copy(n):
        begin = (table_ref[table_at + n // each] * width + n % each * depth) * per
        source = w_ref.at[layer, pl.ds(pl.multiple_of(begin, size), size), :]
        return pltpu.make_async_copy(source, raw_s.at[n], sems.at[n])

    for n in range(pieces):
        copy(n).start()
    token_ref[...] = jnp.zeros_like(token_ref)
    for n in range(pieces):
        copy(n).wait()
        slot = n % split_s.shape[0]
        for begin in range(0, size, taken):
            part = raw_s[n, begin : begin + taken, :].astype(F32)
            for k in range(taken // per):
                place = pl.ds((begin // per + k) * STRIDE, per, stride=apart)
                split_s[slot, place, :] = part[k * per : (k + 1) * per]
        for e in range(2):
            for begin in range(0, chans, WIDE):
                tiles = [
                    split_s[slot, pl.ds((2 * t + e) * apart, depth, stride=STRIDE), :].astype(BF16)
                    for t in range(begin // LANES, (begin + WIDE) // LANES)
                ]
                rows = slice(n * depth, (n + 1) * depth)
                out_ref[e, rows, begin : begin + WIDE] = jnp.concatenate(tiles, axis=1)


def unpack(layer, table, table_at, count, width, chans, w_raw, earlier):
    depth = min(width, WIDE)
    pieces = count * width // depth
    per = 2 * chans // LANES
    return pl.pallas_call(
        functools.partial(unpack_kernel, count, layer, table_at, width),
        out_shape=[
            jax.ShapeDtypeStruct((2, count * width, chans), BF16),
            jax.ShapeDtypeStruct((8, LANES), F32),
        ],
        in_specs=[SMEM, HBM] + [ANY] * len(earlier),
        out_specs=[VMEM, VMEM],
        scratch_shapes=[
            pltpu.VMEM((pieces, depth * per, LANES), BF16),
            pltpu.VMEM((2, per * fold_stride(depth), LANES), F32),
            pltpu.SemaphoreType.DMA((pieces,)),
        ],
        compiler_params=params(24),
        cost_estimate=COST,
        name="unpack",
    )(table, w_raw, *earlier)


def ready_kernel(count, first, layer, table_at, table_ref, *refs):
    shards = refs[:count]
    gain_ref, w_ref = refs[count : count + 2]
    cur_ref, gate_ref, square_ref = refs[-3:]
    rows, width = shards[0].shape
    chans = cur_ref.shape[1]
    squares = jnp.zeros((rows, 1), F32) if first else square_ref[...]
    parts = []
    for j in range(count):
        values = shards[j][:, :width].astype(F32)
        begin = pl.multiple_of(table_ref[table_at + j] * width, width)
        parts.append((values * gain_ref[layer : layer + 1, pl.ds(begin, width)]).astype(BF16))
        squares = squares + jnp.sum(values * values, axis=1, keepdims=True)
    square_ref[...] = squares
    left = jnp.concatenate(parts, axis=1)
    for e, out in enumerate((cur_ref, gate_ref)):
        for begin in range(0, chans, WIDE):
            cols = slice(begin, begin + WIDE)
            product = jnp.dot(left, w_ref[e, :, cols], preferred_element_type=F32)
            if first:
                out[:, cols] = product
            else:
                out[:, cols] += product


def project_ready(layer, shards, table, table_at, norm_gain, weights, before, earlier):
    count = len(shards)
    rows, width = shards[0].shape
    chans = weights.shape[2]
    state = [jax.ShapeDtypeStruct(s, F32) for s in ((rows, chans), (rows, chans), (rows, 1))]
    operands = [table, *shards, norm_gain, weights]
    in_specs = [SMEM] + [VMEM] * (count + 2)
    aliases = {}
    if before is not None:
        aliases = {len(operands) + j: j for j in range(3)}
        in_specs += [VMEM] * 3
        operands += list(before)
    return pl.pallas_call(
        functools.partial(ready_kernel, count, before is None, layer, table_at),
        out_shape=state,
        in_specs=in_specs + [ANY] * len(earlier),
        out_specs=[VMEM] * 3,
        input_output_aliases=aliases,
        compiler_params=params(12),
        cost_estimate=LONG,
        name="project_ready",
    )(*operands, *earlier)


def low_kernel(layer, table_ref, rows_ref, gain_ref, w_ref, *refs):
    width = rows_ref.shape[1]
    begin = pl.multiple_of(table_ref[0] * width, width)
    gain = gain_ref[layer : layer + 1, pl.ds(begin, width)]
    scaled = (rows_ref[...].astype(F32) * gain).astype(BF16)
    product = lax.dot_general(
        scaled, w_ref[layer], (((1,), (1,)), ((), ())), preferred_element_type=F32
    )
    out_ref = refs[-1]
    before = out_ref.shape[1] - product.shape[1]
    if before:
        out_ref[:, :before] = rows_ref[...]
    out_ref[:, before:] = product.astype(BF16)


def project_low(layer, table, own_rows, norm_gain, w_low, before, earlier):
    rows = own_rows.shape[0]
    return pl.pallas_call(
        functools.partial(low_kernel, layer),
        out_shape=jax.ShapeDtypeStruct((rows, before + w_low.shape[1]), BF16),
        in_specs=[SMEM] + [VMEM] * 3 + [ANY] * len(earlier),
        out_specs=VMEM,
        compiler_params=params(12),
        cost_estimate=COST,
        name="project_low",
    )(table, own_rows, norm_gain, w_low, *earlier)


def relay_kernel(value_ref, *refs):
    refs[-1][...] = value_ref[...]


def relay(value, *others):
    return pl.pallas_call(
        relay_kernel,
        out_shape=jax.ShapeDtypeStruct(value.shape, value.dtype),
        in_specs=[VMEM] + [ANY] * len(others),
        out_specs=VMEM,
        compiler_params=params(8),
        cost_estimate=COST,
        name="relay",
    )(value, *others)


def scan_kernel(
    layer,
    states,
    width,
    sel_ref,
    low_ref,
    square_ref,
    cur_ref,
    w_dt_ref,
    bias_ref,
    rate_ref,
    out_ref,
    time_ref,
    final_ref,
    step_s,
    drive_s,
):
    rows, chans = cur_ref.shape
    fold = chans // LANES
    rank = w_dt_ref.shape[1]
    factor = row_factor(square_ref[...], width)
    rank_part = (low_ref[:, :rank] * factor).astype(BF16)
    apart = fold_stride(rows)
    twice = factor * factor
    for begin in range(0, chans, WIDE):
        cols = slice(begin, begin + WIDE)
        pre = jnp.dot(rank_part, w_dt_ref[layer, :, cols], preferred_element_type=F32)
        pre = pre + bias_ref[layer : layer + 1, cols]
        step = jnp.maximum(pre, 0.0) + jnp.log1p(jnp.exp(-jnp.abs(pre)))
        drive = step * (cur_ref[:, cols] * twice)
        for q in range(WIDE // LANES):
            part = slice(q * LANES, (q + 1) * LANES)
            place = pl.ds((begin // LANES + q) * apart, rows, stride=STRIDE)
            step_s[place, :] = step[:, part]
            drive_s[place, :] = drive[:, part]

    def advance(t, carried):
        time, held = carried
        here = pl.ds(t * STRIDE, fold, stride=apart)
        step = step_s[here, :]
        drive = drive_s[here, :]
        sums = [None] * 4
        after = []
        for s in range(states):
            decay = jnp.exp2(step * rate_ref[layer, s])
            now = decay * held[s] + drive * sel_ref[t, s]
            term = now * sel_ref[t, states + s]
            sums[s % 4] = term if sums[s % 4] is None else sums[s % 4] + term
            after.append(now)
        time = time + step
        out_ref[here, :] = (sums[0] + sums[1]) + (sums[2] + sums[3])
        time_ref[here, :] = time
        return time, tuple(after)

    zero = jnp.zeros((fold, LANES), F32)
    time, held = lax.fori_loop(0, rows, advance, (zero, (zero,) * states), unroll=8)
    for s in range(states):
        final_ref[s] = held[s].astype(BF16)
    final_ref[states] = time.astype(BF16)


def local_scan(layer, width, selectors, low, square, cur, w_dt, dt_bias, rate):
    rows, chans = cur.shape
    _, states, fold, _ = rate.shape
    folded = (fold * fold_stride(rows), LANES)
    return pl.pallas_call(
        functools.partial(scan_kernel, layer, states, width),
        out_shape=[
            jax.ShapeDtypeStruct(folded, F32),
            jax.ShapeDtypeStruct(folded, F32),
            jax.ShapeDtypeStruct((states + 1, fold, LANES), BF16),
        ],
        in_specs=[SMEM] + [VMEM] * 6,
        out_specs=[VMEM] * 3,
        scratch_shapes=[pltpu.VMEM(folded, F32), pltpu.VMEM(folded, F32)],
        compiler_params=params(20),
        cost_estimate=COST,
        name="local_scan",
    )(selectors, low, square, cur, w_dt, dt_bias, rate)


def emit_chunks(layer, table_at, feat, gated_ref, table_ref, w_ref, chunks, w_s, sems, before=None):
    def copy(j):
        begin = pl.multiple_of(table_ref[table_at[j]] * feat, feat)
        return pltpu.make_async_copy(w_ref.at[layer, :, pl.ds(begin, feat)], w_s.at[j], sems.at[j])

    for j in range(len(chunks)):
        copy(j).start()
    if before is not None:
        before()
    for j, chunk in enumerate(chunks):
        copy(j).wait()
        for begin in range(0, feat, WIDE):
            cols = slice(begin, begin + WIDE)
            chunk[:, cols] = jnp.dot(
                gated_ref[...], w_s[j, :, cols], preferred_element_type=F32
            ).astype(BF16)


def close_kernel(layer, states, table_at, feat, width, table_ref, place_ref, sel_ref, *refs):
    out_ref, time_ref, cur_ref, gate_ref, square_ref, final_ref = refs[:6]
    rate_ref, skip_ref, thresh_ref, w_ref, gated_ref = refs[6:11]
    chunks = refs[11 : 11 + len(table_at)]
    enter_s, mixed_s, w_s, sems = refs[-4:]
    rows, chans = cur_ref.shape
    fold = chans // LANES
    apart = fold_stride(rows)

    def gate_all():
        def enter(p, state):
            time = final_ref[p, states].astype(F32)
            return tuple(
                jnp.exp2(time * rate_ref[layer, s]) * state[s] + final_ref[p, s].astype(F32)
                for s in range(states)
            )

        zero = jnp.zeros((fold, LANES), F32)
        state = lax.fori_loop(0, place_ref[0], enter, (zero,) * states)
        for s in range(states):
            enter_s[s] = state[s]

        def correct(t, carried):
            here = pl.ds(t * STRIDE, fold, stride=apart)
            time = time_ref[here, :]
            sums = [out_ref[here, :], None, None, None]
            for s in range(states):
                term = jnp.exp2(time * rate_ref[layer, s]) * (enter_s[s] * sel_ref[t, states + s])
                sums[s % 4] = term if sums[s % 4] is None else sums[s % 4] + term
            mixed_s[here, :] = (sums[0] + sums[1]) + (sums[2] + sums[3])
            return carried

        lax.fori_loop(0, rows, correct, 0, unroll=8)

        factor = row_factor(square_ref[...], width)
        for r in range(fold):
            cols = slice(r * LANES, (r + 1) * LANES)
            skip = skip_ref[layer : layer + 1, cols]
            mixed = mixed_s[pl.ds(r * apart, rows, stride=STRIDE), :] + skip * cur_ref[:, cols]
            mixed = mixed * factor
            normal = mixed * lax.rsqrt(jnp.mean(mixed * mixed, axis=1, keepdims=True) + EPS)
            thresh = thresh_ref[layer : layer + 1, cols]
            shrunk = jnp.maximum(normal - thresh, 0.0) - jnp.maximum(-normal - thresh, 0.0)
            gate = gate_ref[:, cols] * factor
            gated_ref[:, cols] = (shrunk * (gate * jax.nn.sigmoid(gate))).astype(BF16)

    emit_chunks(layer, table_at, feat, gated_ref, table_ref, w_ref, chunks, w_s, sems, gate_all)


def close_layer(
    layer, width, table, table_at, feat, seq_place, selectors, values, rate, skip, thresh, w_out
):
    rows, chans = values[2].shape
    _, states, fold, _ = rate.shape
    count = len(table_at)
    chunk = jax.ShapeDtypeStruct((rows, feat), BF16)
    results = pl.pallas_call(
        functools.partial(close_kernel, layer, states, table_at, feat, width),
        out_shape=[jax.ShapeDtypeStruct((rows, chans), BF16)] + [chunk] * count,
        in_specs=[SMEM] * 3 + [VMEM] * 9 + [HBM],
        out_specs=[VMEM] * (1 + count),
        scratch_shapes=[
            pltpu.VMEM((states, fold, LANES), F32),
            pltpu.VMEM((fold * fold_stride(rows), LANES), F32),
            pltpu.VMEM((count, chans, feat), BF16),
            pltpu.SemaphoreType.DMA((count,)),
        ],
        compiler_params=params(40),
        cost_estimate=COST,
        name="close_layer",
    )(table, seq_place, selectors, *values, rate, skip, thresh, w_out)
    return results[0], results[1:]


def expand_kernel(layer, table_at, feat, table_ref, gated_ref, w_ref, *refs):
    chunks = refs[: len(table_at)]
    emit_chunks(layer, table_at, feat, gated_ref, table_ref, w_ref, chunks, *refs[-2:])


def expand(layer, table, table_at, feat, gated, w_out):
    rows, chans = gated.shape
    count = len(table_at)
    return pl.pallas_call(
        functools.partial(expand_kernel, layer, table_at, feat),
        out_shape=[jax.ShapeDtypeStruct((rows, feat), BF16)] * count,
        in_specs=[SMEM, VMEM, HBM],
        out_specs=[VMEM] * count,
        scratch_shapes=[
            pltpu.VMEM((count, chans, feat), BF16),
            pltpu.SemaphoreType.DMA((count,)),
        ],
        compiler_params=params(40),
        cost_estimate=COST,
        name="expand",
    )(table, gated, w_out)


def finish_kernel(rank, own_ref, arrived_ref, *refs):
    low_ref, selectors_ref = refs[-2:]
    total = own_ref[...].astype(F32) + arrived_ref[...].astype(F32)
    low_ref[...] = total
    selectors_ref[...] = total[:, rank:]


def finish_low(rank, own, arrived, earlier):
    rows, count = own.shape
    return pl.pallas_call(
        functools.partial(finish_kernel, rank),
        out_shape=[
            jax.ShapeDtypeStruct((rows, count), F32),
            jax.ShapeDtypeStruct((rows, count - rank), F32),
        ],
        in_specs=[VMEM] * 2 + [ANY] * len(earlier),
        out_specs=[VMEM] * 2,
        compiler_params=params(8),
        cost_estimate=COST,
        name="finish_low",
    )(own, arrived, *earlier)


def combine_kernel(count, *refs):
    total = refs[0][...].astype(F32)
    for ref in refs[1:count]:
        total = total + ref[...].astype(F32)
    refs[-1][...] = total.astype(BF16)


def combine(values, earlier):
    return pl.pallas_call(
        functools.partial(combine_kernel, len(values)),
        out_shape=jax.ShapeDtypeStruct(values[0].shape, BF16),
        in_specs=[VMEM] * len(values) + [ANY] * len(earlier),
        out_specs=VMEM,
        compiler_params=params(8),
        cost_estimate=COST,
        name="combine",
    )(*values, *earlier)


class Grid:
    def __init__(self, count):
        self.depth = DEPTH if count % DEPTH == 0 else 1
        self.side = count // self.depth

    def places(self):
        return [(z, y) for z in range(self.depth) for y in range(self.side)]

    def at(self, z, y):
        return (z % self.depth) * self.side + y % self.side

    def send(self, value, deep, across):
        pairs = [(self.at(z, y), self.at(z + deep, y + across)) for z, y in self.places()]
        return lax.ppermute(value, "tp", pairs)

    def swap(self, value, bit):
        pairs = [(self.at(z, y), self.at(z ^ bit, y)) for z, y in self.places()]
        return lax.ppermute(value, "tp", pairs)

    def table(self):
        own = lax.axis_index("tp")
        z, y = own // self.side, own % self.side
        offsets = jnp.arange(self.depth * self.side, dtype=jnp.int32)
        a, b = offsets // self.side, offsets % self.side
        both = []
        for sign in (-1, 1):
            deep = (z + sign * a + self.depth) % self.depth
            both.append(deep * self.side + (y + sign * b + self.side) % self.side)
        return jnp.concatenate(both).astype(jnp.int32)


def gather_columns(grid, own):
    columns = {0: own}
    half = grid.depth // 2
    for a in range(1, grid.depth - half + 1):
        columns[a] = grid.send(columns[a - 1], 1, 0)
        back = grid.depth - a
        if back > a:
            columns[back] = grid.send(columns[(back + 1) % grid.depth], -1, 0)
    return columns


def scatter_order(grid):
    order = []
    for a in range(grid.depth - grid.depth // 2, 0, -1):
        order.append(a)
        if grid.depth - a > a:
            order.append(grid.depth - a)
    return order + [0]


def scatter_sum(grid, own_rows, chunks, aside):
    order = scatter_order(grid)
    crossed = {
        a: [grid.send(chunks[a, b], 0, b) for b in range(1, grid.side)] for a in order
    }
    half = grid.depth - grid.depth // 2
    arriving = {a: [] for a in order}
    waiting = []
    for n, a in enumerate(order):
        parts = [chunks[a, 0], *crossed[a], *arriving[a]]
        if a == 0:
            aside(n, [*crossed[a], chunks[a, 0]][0])
            return combine([own_rows, *parts], waiting)
        part = combine(parts, waiting)
        step = 1 if a <= half else -1
        arriving[(a - step) % grid.depth].append(grid.send(part, step, 0))
        waiting = aside(n, part)


def sum_selectors(grid, partials):
    total = sum(partial.astype(F32) for partial in partials)
    pairs = []
    bit = grid.depth // 2
    while True:
        rounded = total.astype(BF16)
        arrived = grid.swap(rounded, bit) if bit else jnp.zeros_like(rounded)
        pairs.append((rounded, arrived))
        bit //= 2
        if not bit:
            return pairs
        total = rounded.astype(F32) + arrived.astype(F32)


def per_device(
    n_tp, tokens, norm_gain, w_in, w_low, w_dt, a_rate, dt_bias, skip_gain, threshold, w_out
):
    grid = Grid(n_tp)
    feat = tokens.shape[1]
    layers, width, _, chans = w_in.shape
    states = a_rate.shape[1]
    rank = w_dt.shape[1]
    fold = chans // LANES
    table = grid.table()
    forth = lambda a, b: n_tp + a * grid.side + b
    seq_place = lax.axis_index("seq").astype(jnp.int32).reshape(1)
    rates = (a_rate * (-math.log2(math.e))).reshape(layers, states, fold, LANES)
    w_raw = w_in.reshape(layers, width, 2, fold, LANES).transpose(0, 1, 3, 2, 4)
    w_raw = w_raw.reshape(layers, width * 2 * fold, LANES)
    order = scatter_order(grid)
    own_rows = tokens
    low_t = jnp.swapaxes(w_low, 1, 2)
    arrivals = [0] + [a for a in order if a not in (0, order[0])] + order[:1]
    weights = {}
    for layer in range(layers):
        columns = gather_columns(grid, own_rows)
        cross = lambda column: [grid.send(column, 0, b) for b in range(1, grid.side)]
        packed = layer > 0
        state = None
        if packed:
            low = project_low(layer, table, own_rows, norm_gain, low_t, feat, [])
            beside = {0: cross(low)}
            lows = [each[:, feat:] for each in (low, *beside[0])]
        else:
            beside = {0: cross(own_rows)}
            state = project(layer, [own_rows], table, 0, norm_gain, w_raw, chans, None, [rates])
            low = project_low(
                layer, table, own_rows, norm_gain, low_t, 0, [*beside[0], state[2]]
            )
            lows = [low, *cross(low)]
        pairs = sum_selectors(grid, lows)
        stages = [own for own, _ in pairs]
        for n, a in enumerate(arrivals):
            if n:
                last = n + 1 == len(arrivals)
                beside[a] = cross(relay(columns[a], *first) if last else columns[a])
            arrived = [columns[a], *beside[a]]
            if not n and state is not None:
                arrived = beside[a]
            place, earlier = (a + 1) * grid.side - len(arrived), stages[n - 1 + packed : n + packed] if n else []
            if a in weights:
                state = project_ready(
                    layer, arrived, table, place, norm_gain, weights[a], state, earlier
                )
            else:
                state = project(
                    layer, arrived, table, place, norm_gain, w_raw, chans, state, earlier
                )
            if n == 0:
                first = [state[2]]
        cur, gate, square = state
        low, selectors = finish_low(rank, *pairs[-1], [square])
        out, time, final = local_scan(
            layer, width, selectors, low, square, cur, w_dt, dt_bias, rates
        )
        finals = lax.all_gather(final, "seq")
        keys = [(a, b) for a in order for b in range(1, grid.side)]
        keys += [(a, 0) for a in order]
        lead = grid.side - 1
        gated, chunks = close_layer(
            layer,
            width,
            table,
            [forth(*key) for key in keys[:lead]],
            feat,
            seq_place,
            selectors,
            (out, time, cur, gate, square, finals),
            rates,
            skip_gain,
            threshold,
            w_out,
        )
        chunks = dict(zip(keys, chunks))
        split = len(order) * lead + 1
        for part in (keys[lead:split], keys[split:]):
            more = expand(layer, table, [forth(*key) for key in part], feat, gated, w_out)
            chunks.update(zip(part, more))
        weights = {}

        def aside(n, value):
            left = [a for a in arrivals if a not in weights]
            wanted = [1, 0, len(left) - 1, 1][min(n, 3)] if layer + 1 < layers else 0
            tokens = []
            for a in left[:wanted]:
                weights[a], token = unpack(
                    layer + 1, table, a * grid.side, grid.side, feat, chans, w_raw, [value]
                )
                tokens.append(token)
            return tokens

        own_rows = scatter_sum(grid, own_rows, chunks, aside)
    return own_rows


def solution(mesh):
    in_specs = (
        P("seq", "tp"),
        P(),
        P(None, None, None, "tp"),
        P(None, "tp", None),
        P(None, None, "tp"),
        P(None, None, "tp"),
        P(None, "tp"),
        P(None, "tp"),
        P(None, "tp"),
        P(None, "tp", None),
    )
    return jax.shard_map(
        functools.partial(per_device, mesh.shape["tp"]),
        mesh=mesh,
        in_specs=in_specs,
        out_specs=P("seq", "tp"),
        check_vma=False,
    )
```

```python
import functools
import math

import jax
import jax.numpy as jnp
from jax import lax
from jax.experimental import pallas as pl
from jax.experimental.pallas import tpu as pltpu
from jax.sharding import PartitionSpec as P

LANES = 128
WIDE = 256
STRIDE = 3
EPS = 1e-05
DEPTH = 4
F32 = jnp.float32
BF16 = jnp.bfloat16
VMEM = pl.BlockSpec(memory_space=pltpu.VMEM)
SMEM = pl.BlockSpec(memory_space=pltpu.SMEM)
HBM = pl.BlockSpec(memory_space=pltpu.HBM)
ANY = pl.BlockSpec(memory_space=pl.ANY)
COST = pl.CostEstimate(flops=1, bytes_accessed=1, transcendentals=0)
LONG = pl.CostEstimate(flops=10**10, bytes_accessed=1, transcendentals=0)


def row_factor(square_sum, width):
    return lax.rsqrt(square_sum / width + EPS)


def fold_stride(count):
    return STRIDE * count + 1


def params(mebibytes):
    return pltpu.CompilerParams(vmem_limit_bytes=mebibytes * 1024 * 1024)


def proj_kernel(count, first, layer, table_at, table_ref, *refs):
    shards = refs[:count]
    gain_ref, w_ref = refs[count : count + 2]
    raw_s, split_s, sems = refs[-3:]
    cur_ref, gate_ref, square_ref = refs[-6:-3]
    rows, width = shards[0].shape
    chans = cur_ref.shape[1]
    pieces, size, _ = raw_s.shape
    pieces //= count
    per = 2 * chans // LANES
    depth = size // per
    apart = fold_stride(depth)
    taken = max(per, 16)
    places = [table_ref[table_at + j] for j in range(count)]

    def copy(j, q):
        n = j * pieces + q
        begin = (places[j] * width + q * depth) * per
        source = w_ref.at[layer, pl.ds(pl.multiple_of(begin, size), size), :]
        return pltpu.make_async_copy(source, raw_s.at[n], sems.at[n])

    for j in range(count):
        for q in range(pieces):
            copy(j, q).start()
    squares = jnp.zeros((rows, 1), F32) if first else square_ref[...]
    for j in range(count):
        values = shards[j][:, :width].astype(F32)
        gain = gain_ref[layer : layer + 1, pl.ds(pl.multiple_of(places[j] * width, width), width)]
        left = (values * gain).astype(BF16)
        squares = squares + jnp.sum(values * values, axis=1, keepdims=True)
        for q in range(pieces):
            copy(j, q).wait()
            slot = (j * pieces + q) % split_s.shape[0]
            for begin in range(0, size, taken):
                part = raw_s[j * pieces + q, begin : begin + taken, :].astype(F32)
                for k in range(taken // per):
                    d = begin // per + k
                    place = pl.ds(d * STRIDE, per, stride=apart)
                    split_s[slot, place, :] = part[k * per : (k + 1) * per]
        for e, out in enumerate((cur_ref, gate_ref)):
            for begin in range(0, chans, WIDE):
                tiles = [
                    jnp.concatenate(
                        [
                            split_s[
                                (j * pieces + q) % split_s.shape[0],
                                pl.ds((2 * t + e) * apart, depth, stride=STRIDE),
                                :,
                            ].astype(BF16)
                            for q in range(pieces)
                        ],
                        axis=0,
                    )
                    for t in range(begin // LANES, (begin + WIDE) // LANES)
                ]
                product = jnp.dot(left, jnp.concatenate(tiles, axis=1), preferred_element_type=F32)
                cols = slice(begin, begin + WIDE)
                if first and j == 0:
                    out[:, cols] = product
                else:
                    out[:, cols] += product
    square_ref[...] = squares


def project(layer, shards, table, table_at, norm_gain, w_raw, chans, before, earlier):
    count = len(shards)
    rows, width = shards[0].shape
    depth = min(width, WIDE)
    pieces = count * (width // depth)
    per = 2 * chans // LANES
    shapes = [(rows, chans), (rows, chans), (rows, 1)]
    operands = [table, *shards, norm_gain, w_raw]
    in_specs = [SMEM] + [VMEM] * (count + 1) + [HBM]
    aliases = {}
    if before is not None:
        aliases = {len(operands) + j: j for j in range(len(shapes))}
        in_specs += [VMEM] * len(shapes)
        operands += list(before)
    in_specs += [ANY] * len(earlier)
    operands += earlier
    return pl.pallas_call(
        functools.partial(proj_kernel, count, before is None, layer, table_at),
        out_shape=[jax.ShapeDtypeStruct(shape, F32) for shape in shapes],
        in_specs=in_specs,
        out_specs=[VMEM] * len(shapes),
        scratch_shapes=[
            pltpu.VMEM((pieces, depth * per, LANES), BF16),
            pltpu.VMEM((pieces, per * fold_stride(depth), LANES), F32),
            pltpu.SemaphoreType.DMA((pieces,)),
        ],
        input_output_aliases=aliases,
        compiler_params=params(36),
        cost_estimate=LONG,
        name="project",
    )(*operands)


def unpack_kernel(count, layer, table_at, width, table_ref, w_ref, *refs):
    out_ref, token_ref, raw_s, split_s, sems = refs[-5:]
    pieces, size, _ = raw_s.shape
    chans = out_ref.shape[2]
    per = 2 * chans // LANES
    depth = size // per
    apart = fold_stride(depth)
    taken = max(per, 16)
    each = width // depth

    def copy(n):
        begin = (table_ref[table_at + n // each] * width + n % each * depth) * per
        source = w_ref.at[layer, pl.ds(pl.multiple_of(begin, size), size), :]
        return pltpu.make_async_copy(source, raw_s.at[n], sems.at[n])

    for n in range(pieces):
        copy(n).start()
    token_ref[...] = jnp.zeros_like(token_ref)
    for n in range(pieces):
        copy(n).wait()
        slot = n % split_s.shape[0]
        for begin in range(0, size, taken):
            part = raw_s[n, begin : begin + taken, :].astype(F32)
            for k in range(taken // per):
                place = pl.ds((begin // per + k) * STRIDE, per, stride=apart)
                split_s[slot, place, :] = part[k * per : (k + 1) * per]
        for e in range(2):
            for begin in range(0, chans, WIDE):
                tiles = [
                    split_s[slot, pl.ds((2 * t + e) * apart, depth, stride=STRIDE), :].astype(BF16)
                    for t in range(begin // LANES, (begin + WIDE) // LANES)
                ]
                rows = slice(n * depth, (n + 1) * depth)
                out_ref[e, rows, begin : begin + WIDE] = jnp.concatenate(tiles, axis=1)


def unpack(layer, table, table_at, count, width, chans, w_raw, earlier):
    depth = min(width, WIDE)
    pieces = count * width // depth
    per = 2 * chans // LANES
    return pl.pallas_call(
        functools.partial(unpack_kernel, count, layer, table_at, width),
        out_shape=[
            jax.ShapeDtypeStruct((2, count * width, chans), BF16),
            jax.ShapeDtypeStruct((8, LANES), F32),
        ],
        in_specs=[SMEM, HBM] + [ANY] * len(earlier),
        out_specs=[VMEM, VMEM],
        scratch_shapes=[
            pltpu.VMEM((pieces, depth * per, LANES), BF16),
            pltpu.VMEM((2, per * fold_stride(depth), LANES), F32),
            pltpu.SemaphoreType.DMA((pieces,)),
        ],
        compiler_params=params(24),
        cost_estimate=COST,
        name="unpack",
    )(table, w_raw, *earlier)


def ready_kernel(count, first, layer, table_at, table_ref, *refs):
    shards = refs[:count]
    gain_ref, w_ref = refs[count : count + 2]
    cur_ref, gate_ref, square_ref = refs[-3:]
    rows, width = shards[0].shape
    chans = cur_ref.shape[1]
    squares = jnp.zeros((rows, 1), F32) if first else square_ref[...]
    parts = []
    for j in range(count):
        values = shards[j][:, :width].astype(F32)
        begin = pl.multiple_of(table_ref[table_at + j] * width, width)
        parts.append((values * gain_ref[layer : layer + 1, pl.ds(begin, width)]).astype(BF16))
        squares = squares + jnp.sum(values * values, axis=1, keepdims=True)
    square_ref[...] = squares
    left = jnp.concatenate(parts, axis=1)
    for e, out in enumerate((cur_ref, gate_ref)):
        for begin in range(0, chans, WIDE):
            cols = slice(begin, begin + WIDE)
            product = jnp.dot(left, w_ref[e, :, cols], preferred_element_type=F32)
            if first:
                out[:, cols] = product
            else:
                out[:, cols] += product


def project_ready(layer, shards, table, table_at, norm_gain, weights, before, earlier):
    count = len(shards)
    rows, width = shards[0].shape
    chans = weights.shape[2]
    state = [jax.ShapeDtypeStruct(s, F32) for s in ((rows, chans), (rows, chans), (rows, 1))]
    operands = [table, *shards, norm_gain, weights]
    in_specs = [SMEM] + [VMEM] * (count + 2)
    aliases = {}
    if before is not None:
        aliases = {len(operands) + j: j for j in range(3)}
        in_specs += [VMEM] * 3
        operands += list(before)
    return pl.pallas_call(
        functools.partial(ready_kernel, count, before is None, layer, table_at),
        out_shape=state,
        in_specs=in_specs + [ANY] * len(earlier),
        out_specs=[VMEM] * 3,
        input_output_aliases=aliases,
        compiler_params=params(12),
        cost_estimate=LONG,
        name="project_ready",
    )(*operands, *earlier)


def low_kernel(layer, table_ref, rows_ref, gain_ref, w_ref, *refs):
    width = rows_ref.shape[1]
    begin = pl.multiple_of(table_ref[0] * width, width)
    gain = gain_ref[layer : layer + 1, pl.ds(begin, width)]
    scaled = (rows_ref[...].astype(F32) * gain).astype(BF16)
    product = lax.dot_general(
        scaled, w_ref[layer], (((1,), (1,)), ((), ())), preferred_element_type=F32
    )
    out_ref = refs[-1]
    before = out_ref.shape[1] - product.shape[1]
    if before:
        out_ref[:, :before] = rows_ref[...]
    out_ref[:, before:] = product.astype(BF16)


def project_low(layer, table, own_rows, norm_gain, w_low, before, earlier):
    rows = own_rows.shape[0]
    return pl.pallas_call(
        functools.partial(low_kernel, layer),
        out_shape=jax.ShapeDtypeStruct((rows, before + w_low.shape[1]), BF16),
        in_specs=[SMEM] + [VMEM] * 3 + [ANY] * len(earlier),
        out_specs=VMEM,
        compiler_params=params(12),
        cost_estimate=COST,
        name="project_low",
    )(table, own_rows, norm_gain, w_low, *earlier)


def relay_kernel(value_ref, *refs):
    refs[-1][...] = value_ref[...]


def relay(value, *others):
    return pl.pallas_call(
        relay_kernel,
        out_shape=jax.ShapeDtypeStruct(value.shape, value.dtype),
        in_specs=[VMEM] + [ANY] * len(others),
        out_specs=VMEM,
        compiler_params=params(8),
        cost_estimate=COST,
        name="relay",
    )(value, *others)


def scan_kernel(
    layer,
    states,
    width,
    sel_ref,
    low_ref,
    square_ref,
    cur_ref,
    w_dt_ref,
    bias_ref,
    rate_ref,
    out_ref,
    time_ref,
    final_ref,
    step_s,
    drive_s,
):
    rows, chans = cur_ref.shape
    fold = chans // LANES
    rank = w_dt_ref.shape[1]
    factor = row_factor(square_ref[...], width)
    rank_part = (low_ref[:, :rank] * factor).astype(BF16)
    apart = fold_stride(rows)
    twice = factor * factor
    for begin in range(0, chans, WIDE):
        cols = slice(begin, begin + WIDE)
        pre = jnp.dot(rank_part, w_dt_ref[layer, :, cols], preferred_element_type=F32)
        pre = pre + bias_ref[layer : layer + 1, cols]
        step = jnp.maximum(pre, 0.0) + jnp.log1p(jnp.exp(-jnp.abs(pre)))
        drive = step * (cur_ref[:, cols] * twice)
        for q in range(WIDE // LANES):
            part = slice(q * LANES, (q + 1) * LANES)
            place = pl.ds((begin // LANES + q) * apart, rows, stride=STRIDE)
            step_s[place, :] = step[:, part]
            drive_s[place, :] = drive[:, part]

    def advance(t, carried):
        time, held = carried
        here = pl.ds(t * STRIDE, fold, stride=apart)
        step = step_s[here, :]
        drive = drive_s[here, :]
        sums = [None] * 4
        after = []
        for s in range(states):
            decay = jnp.exp2(step * rate_ref[layer, s])
            now = decay * held[s] + drive * sel_ref[t, s]
            term = now * sel_ref[t, states + s]
            sums[s % 4] = term if sums[s % 4] is None else sums[s % 4] + term
            after.append(now)
        time = time + step
        out_ref[here, :] = (sums[0] + sums[1]) + (sums[2] + sums[3])
        time_ref[here, :] = time
        return time, tuple(after)

    zero = jnp.zeros((fold, LANES), F32)
    time, held = lax.fori_loop(0, rows, advance, (zero, (zero,) * states), unroll=8)
    for s in range(states):
        final_ref[s] = held[s].astype(BF16)
    final_ref[states] = time.astype(BF16)


def local_scan(layer, width, selectors, low, square, cur, w_dt, dt_bias, rate):
    rows, chans = cur.shape
    _, states, fold, _ = rate.shape
    folded = (fold * fold_stride(rows), LANES)
    return pl.pallas_call(
        functools.partial(scan_kernel, layer, states, width),
        out_shape=[
            jax.ShapeDtypeStruct(folded, F32),
            jax.ShapeDtypeStruct(folded, F32),
            jax.ShapeDtypeStruct((states + 1, fold, LANES), BF16),
        ],
        in_specs=[SMEM] + [VMEM] * 6,
        out_specs=[VMEM] * 3,
        scratch_shapes=[pltpu.VMEM(folded, F32), pltpu.VMEM(folded, F32)],
        compiler_params=params(20),
        cost_estimate=COST,
        name="local_scan",
    )(selectors, low, square, cur, w_dt, dt_bias, rate)


def emit_chunks(layer, table_at, feat, gated_ref, table_ref, w_ref, chunks, w_s, sems, before=None):
    def copy(j):
        begin = pl.multiple_of(table_ref[table_at[j]] * feat, feat)
        return pltpu.make_async_copy(w_ref.at[layer, :, pl.ds(begin, feat)], w_s.at[j], sems.at[j])

    for j in range(len(chunks)):
        copy(j).start()
    if before is not None:
        before()
    for j, chunk in enumerate(chunks):
        copy(j).wait()
        for begin in range(0, feat, WIDE):
            cols = slice(begin, begin + WIDE)
            chunk[:, cols] = jnp.dot(
                gated_ref[...], w_s[j, :, cols], preferred_element_type=F32
            ).astype(BF16)


def close_kernel(layer, states, table_at, feat, width, table_ref, place_ref, sel_ref, *refs):
    out_ref, time_ref, cur_ref, gate_ref, square_ref, final_ref = refs[:6]
    rate_ref, skip_ref, thresh_ref, w_ref, gated_ref = refs[6:11]
    chunks = refs[11 : 11 + len(table_at)]
    enter_s, mixed_s, w_s, sems = refs[-4:]
    rows, chans = cur_ref.shape
    fold = chans // LANES
    apart = fold_stride(rows)

    def gate_all():
        def enter(p, state):
            time = final_ref[p, states].astype(F32)
            return tuple(
                jnp.exp2(time * rate_ref[layer, s]) * state[s] + final_ref[p, s].astype(F32)
                for s in range(states)
            )

        zero = jnp.zeros((fold, LANES), F32)
        state = lax.fori_loop(0, place_ref[0], enter, (zero,) * states)
        for s in range(states):
            enter_s[s] = state[s]

        def correct(t, carried):
            here = pl.ds(t * STRIDE, fold, stride=apart)
            time = time_ref[here, :]
            sums = [out_ref[here, :], None, None, None]
            for s in range(states):
                term = jnp.exp2(time * rate_ref[layer, s]) * (enter_s[s] * sel_ref[t, states + s])
                sums[s % 4] = term if sums[s % 4] is None else sums[s % 4] + term
            mixed_s[here, :] = (sums[0] + sums[1]) + (sums[2] + sums[3])
            return carried

        lax.fori_loop(0, rows, correct, 0, unroll=8)

        factor = row_factor(square_ref[...], width)
        for r in range(fold):
            cols = slice(r * LANES, (r + 1) * LANES)
            skip = skip_ref[layer : layer + 1, cols]
            mixed = mixed_s[pl.ds(r * apart, rows, stride=STRIDE), :] + skip * cur_ref[:, cols]
            mixed = mixed * factor
            normal = mixed * lax.rsqrt(jnp.mean(mixed * mixed, axis=1, keepdims=True) + EPS)
            thresh = thresh_ref[layer : layer + 1, cols]
            shrunk = jnp.maximum(normal - thresh, 0.0) - jnp.maximum(-normal - thresh, 0.0)
            gate = gate_ref[:, cols] * factor
            gated_ref[:, cols] = (shrunk * (gate * jax.nn.sigmoid(gate))).astype(BF16)

    emit_chunks(layer, table_at, feat, gated_ref, table_ref, w_ref, chunks, w_s, sems, gate_all)


def close_layer(
    layer, width, table, table_at, feat, seq_place, selectors, values, rate, skip, thresh, w_out
):
    rows, chans = values[2].shape
    _, states, fold, _ = rate.shape
    count = len(table_at)
    chunk = jax.ShapeDtypeStruct((rows, feat), BF16)
    results = pl.pallas_call(
        functools.partial(close_kernel, layer, states, table_at, feat, width),
        out_shape=[jax.ShapeDtypeStruct((rows, chans), BF16)] + [chunk] * count,
        in_specs=[SMEM] * 3 + [VMEM] * 9 + [HBM],
        out_specs=[VMEM] * (1 + count),
        scratch_shapes=[
            pltpu.VMEM((states, fold, LANES), F32),
            pltpu.VMEM((fold * fold_stride(rows), LANES), F32),
            pltpu.VMEM((count, chans, feat), BF16),
            pltpu.SemaphoreType.DMA((count,)),
        ],
        compiler_params=params(40),
        cost_estimate=COST,
        name="close_layer",
    )(table, seq_place, selectors, *values, rate, skip, thresh, w_out)
    return results[0], results[1:]


def expand_kernel(layer, table_at, feat, table_ref, gated_ref, w_ref, *refs):
    chunks = refs[: len(table_at)]
    emit_chunks(layer, table_at, feat, gated_ref, table_ref, w_ref, chunks, *refs[-2:])


def expand(layer, table, table_at, feat, gated, w_out):
    rows, chans = gated.shape
    count = len(table_at)
    return pl.pallas_call(
        functools.partial(expand_kernel, layer, table_at, feat),
        out_shape=[jax.ShapeDtypeStruct((rows, feat), BF16)] * count,
        in_specs=[SMEM, VMEM, HBM],
        out_specs=[VMEM] * count,
        scratch_shapes=[
            pltpu.VMEM((count, chans, feat), BF16),
            pltpu.SemaphoreType.DMA((count,)),
        ],
        compiler_params=params(40),
        cost_estimate=COST,
        name="expand",
    )(table, gated, w_out)


def finish_kernel(rank, own_ref, arrived_ref, *refs):
    low_ref, selectors_ref = refs[-2:]
    total = own_ref[...].astype(F32) + arrived_ref[...].astype(F32)
    low_ref[...] = total
    selectors_ref[...] = total[:, rank:]


def finish_low(rank, own, arrived, earlier):
    rows, count = own.shape
    return pl.pallas_call(
        functools.partial(finish_kernel, rank),
        out_shape=[
            jax.ShapeDtypeStruct((rows, count), F32),
            jax.ShapeDtypeStruct((rows, count - rank), F32),
        ],
        in_specs=[VMEM] * 2 + [ANY] * len(earlier),
        out_specs=[VMEM] * 2,
        compiler_params=params(8),
        cost_estimate=COST,
        name="finish_low",
    )(own, arrived, *earlier)


def combine_kernel(count, *refs):
    total = refs[0][...].astype(F32)
    for ref in refs[1:count]:
        total = total + ref[...].astype(F32)
    refs[-1][...] = total.astype(BF16)


def combine(values, earlier):
    return pl.pallas_call(
        functools.partial(combine_kernel, len(values)),
        out_shape=jax.ShapeDtypeStruct(values[0].shape, BF16),
        in_specs=[VMEM] * len(values) + [ANY] * len(earlier),
        out_specs=VMEM,
        compiler_params=params(8),
        cost_estimate=COST,
        name="combine",
    )(*values, *earlier)


class Grid:
    def __init__(self, count):
        self.depth = DEPTH if count % DEPTH == 0 else 1
        self.side = count // self.depth

    def places(self):
        return [(z, y) for z in range(self.depth) for y in range(self.side)]

    def at(self, z, y):
        return (z % self.depth) * self.side + y % self.side

    def send(self, value, deep, across):
        pairs = [(self.at(z, y), self.at(z + deep, y + across)) for z, y in self.places()]
        return lax.ppermute(value, "tp", pairs)

    def swap(self, value, bit):
        pairs = [(self.at(z, y), self.at(z ^ bit, y)) for z, y in self.places()]
        return lax.ppermute(value, "tp", pairs)

    def table(self):
        own = lax.axis_index("tp")
        z, y = own // self.side, own % self.side
        offsets = jnp.arange(self.depth * self.side, dtype=jnp.int32)
        a, b = offsets // self.side, offsets % self.side
        both = []
        for sign in (-1, 1):
            deep = (z + sign * a + self.depth) % self.depth
            both.append(deep * self.side + (y + sign * b + self.side) % self.side)
        return jnp.concatenate(both).astype(jnp.int32)


def gather_columns(grid, own):
    columns = {0: own}
    half = grid.depth // 2
    for a in range(1, grid.depth - half + 1):
        columns[a] = grid.send(columns[a - 1], 1, 0)
        back = grid.depth - a
        if back > a:
            columns[back] = grid.send(columns[(back + 1) % grid.depth], -1, 0)
    return columns


def scatter_order(grid):
    order = []
    for a in range(grid.depth - grid.depth // 2, 0, -1):
        order.append(a)
        if grid.depth - a > a:
            order.append(grid.depth - a)
    return order + [0]


def scatter_sum(grid, own_rows, chunks, aside):
    order = scatter_order(grid)
    crossed = {
        a: [grid.send(chunks[a, b], 0, b) for b in range(1, grid.side)] for a in order
    }
    half = grid.depth - grid.depth // 2
    arriving = {a: [] for a in order}
    waiting = []
    for n, a in enumerate(order):
        parts = [chunks[a, 0], *crossed[a], *arriving[a]]
        if a == 0:
            aside(n, [*crossed[a], chunks[a, 0]][0])
            return combine([own_rows, *parts], waiting)
        part = combine(parts, waiting)
        step = 1 if a <= half else -1
        arriving[(a - step) % grid.depth].append(grid.send(part, step, 0))
        waiting = aside(n, part)


def sum_selectors(grid, partials):
    total = sum(partial.astype(F32) for partial in partials)
    pairs = []
    bit = 1
    while True:
        rounded = total.astype(BF16)
        arrived = grid.swap(rounded, bit) if bit < grid.depth else jnp.zeros_like(rounded)
        pairs.append((rounded, arrived))
        bit *= 2
        if bit >= grid.depth:
            return pairs
        total = rounded.astype(F32) + arrived.astype(F32)


def per_device(
    n_tp, tokens, norm_gain, w_in, w_low, w_dt, a_rate, dt_bias, skip_gain, threshold, w_out
):
    grid = Grid(n_tp)
    feat = tokens.shape[1]
    layers, width, _, chans = w_in.shape
    states = a_rate.shape[1]
    rank = w_dt.shape[1]
    fold = chans // LANES
    table = grid.table()
    forth = lambda a, b: n_tp + a * grid.side + b
    seq_place = lax.axis_index("seq").astype(jnp.int32).reshape(1)
    rates = (a_rate * (-math.log2(math.e))).reshape(layers, states, fold, LANES)
    w_raw = w_in.reshape(layers, width, 2, fold, LANES).transpose(0, 1, 3, 2, 4)
    w_raw = w_raw.reshape(layers, width * 2 * fold, LANES)
    order = scatter_order(grid)
    own_rows = tokens
    low_t = jnp.swapaxes(w_low, 1, 2)
    arrivals = [0] + [a for a in order if a not in (0, order[0])] + order[:1]
    weights = {}
    for layer in range(layers):
        columns = gather_columns(grid, own_rows)
        cross = lambda column: [grid.send(column, 0, b) for b in range(1, grid.side)]
        packed = layer > 0
        if packed:
            low = project_low(layer, table, own_rows, norm_gain, low_t, feat, [])
            beside = {0: cross(low)}
            lows = [each[:, feat:] for each in (low, *beside[0])]
        else:
            beside = {0: cross(own_rows)}
            low = project_low(layer, table, own_rows, norm_gain, low_t, 0, beside[0])
            lows = [low, *cross(low)]
            weights[0], _ = unpack(layer, table, 0, grid.side, feat, chans, w_raw, [rates])
        pairs = sum_selectors(grid, lows)
        stages = [own for own, _ in pairs]
        state = None
        for n, a in enumerate(arrivals):
            if n:
                late = n > 1 if packed else n + 1 == len(arrivals)
                beside[a] = cross(relay(columns[a], *first) if late else columns[a])
            arrived = [columns[a], *beside[a]]
            place, earlier = a * grid.side, stages[n - 1 + packed : n + packed] if n else []
            if a in weights:
                state = project_ready(
                    layer, arrived, table, place, norm_gain, weights[a], state, earlier
                )
            else:
                state = project(
                    layer, arrived, table, place, norm_gain, w_raw, chans, state, earlier
                )
            if n == 0:
                first = [state[2]]
        cur, gate, square = state
        low, selectors = finish_low(rank, *pairs[-1], [square])
        out, time, final = local_scan(
            layer, width, selectors, low, square, cur, w_dt, dt_bias, rates
        )
        finals = lax.all_gather(final, "seq")
        keys = [(a, b) for a in order for b in range(1, grid.side)]
        keys += [(a, 0) for a in order]
        lead = grid.side - 1
        gated, chunks = close_layer(
            layer,
            width,
            table,
            [forth(*key) for key in keys[:lead]],
            feat,
            seq_place,
            selectors,
            (out, time, cur, gate, square, finals),
            rates,
            skip_gain,
            threshold,
            w_out,
        )
        chunks = dict(zip(keys, chunks))
        split = len(order) * lead + 1
        for part in (keys[lead:split], keys[split:]):
            more = expand(layer, table, [forth(*key) for key in part], feat, gated, w_out)
            chunks.update(zip(part, more))
        weights = {}

        def aside(n, value):
            left = [a for a in arrivals if a not in weights]
            wanted = [1, 0, len(left) - 1, 1][min(n, 3)] if layer + 1 < layers else 0
            tokens = []
            for a in left[:wanted]:
                weights[a], token = unpack(
                    layer + 1, table, a * grid.side, grid.side, feat, chans, w_raw, [value]
                )
                tokens.append(token)
            return tokens

        own_rows = scatter_sum(grid, own_rows, chunks, aside)
    return own_rows


def solution(mesh):
    in_specs = (
        P("seq", "tp"),
        P(),
        P(None, None, None, "tp"),
        P(None, "tp", None),
        P(None, None, "tp"),
        P(None, None, "tp"),
        P(None, "tp"),
        P(None, "tp"),
        P(None, "tp"),
        P(None, "tp", None),
    )
    return jax.shard_map(
        functools.partial(per_device, mesh.shape["tp"]),
        mesh=mesh,
        in_specs=in_specs,
        out_specs=P("seq", "tp"),
        check_vma=False,
    )
```

```python
import functools
import math

import jax
import jax.numpy as jnp
from jax import lax
from jax.experimental import pallas as pl
from jax.experimental.pallas import tpu as pltpu
from jax.sharding import PartitionSpec as P

LANES = 128
WIDE = 256
STRIDE = 3
EPS = 1e-05
DEPTH = 4
F32 = jnp.float32
BF16 = jnp.bfloat16
VMEM = pl.BlockSpec(memory_space=pltpu.VMEM)
SMEM = pl.BlockSpec(memory_space=pltpu.SMEM)
HBM = pl.BlockSpec(memory_space=pltpu.HBM)
ANY = pl.BlockSpec(memory_space=pl.ANY)
COST = pl.CostEstimate(flops=1, bytes_accessed=1, transcendentals=0)
LONG = pl.CostEstimate(flops=10**10, bytes_accessed=1, transcendentals=0)


def row_factor(square_sum, width):
    return lax.rsqrt(square_sum / width + EPS)


def fold_stride(count):
    return STRIDE * count + 1


def params(mebibytes):
    return pltpu.CompilerParams(vmem_limit_bytes=mebibytes * 1024 * 1024)


def proj_kernel(count, first, layer, table_at, table_ref, *refs):
    shards = refs[:count]
    gain_ref, w_ref = refs[count : count + 2]
    raw_s, split_s, sems = refs[-3:]
    cur_ref, gate_ref, square_ref = refs[-6:-3]
    rows, width = shards[0].shape
    chans = cur_ref.shape[1]
    pieces, size, _ = raw_s.shape
    pieces //= count
    per = 2 * chans // LANES
    depth = size // per
    apart = fold_stride(depth)
    taken = max(per, 16)
    places = [table_ref[table_at + j] for j in range(count)]

    def copy(j, q):
        n = j * pieces + q
        begin = (places[j] * width + q * depth) * per
        source = w_ref.at[layer, pl.ds(pl.multiple_of(begin, size), size), :]
        return pltpu.make_async_copy(source, raw_s.at[n], sems.at[n])

    for j in range(count):
        for q in range(pieces):
            copy(j, q).start()
    squares = jnp.zeros((rows, 1), F32) if first else square_ref[...]
    for j in range(count):
        values = shards[j][:, :width].astype(F32)
        gain = gain_ref[layer : layer + 1, pl.ds(pl.multiple_of(places[j] * width, width), width)]
        left = (values * gain).astype(BF16)
        squares = squares + jnp.sum(values * values, axis=1, keepdims=True)
        for q in range(pieces):
            copy(j, q).wait()
            slot = (j * pieces + q) % split_s.shape[0]
            for begin in range(0, size, taken):
                part = raw_s[j * pieces + q, begin : begin + taken, :].astype(F32)
                for k in range(taken // per):
                    d = begin // per + k
                    place = pl.ds(d * STRIDE, per, stride=apart)
                    split_s[slot, place, :] = part[k * per : (k + 1) * per]
        for e, out in enumerate((cur_ref, gate_ref)):
            for begin in range(0, chans, WIDE):
                tiles = [
                    jnp.concatenate(
                        [
                            split_s[
                                (j * pieces + q) % split_s.shape[0],
                                pl.ds((2 * t + e) * apart, depth, stride=STRIDE),
                                :,
                            ].astype(BF16)
                            for q in range(pieces)
                        ],
                        axis=0,
                    )
                    for t in range(begin // LANES, (begin + WIDE) // LANES)
                ]
                product = jnp.dot(left, jnp.concatenate(tiles, axis=1), preferred_element_type=F32)
                cols = slice(begin, begin + WIDE)
                if first and j == 0:
                    out[:, cols] = product
                else:
                    out[:, cols] += product
    square_ref[...] = squares


def project(layer, shards, table, table_at, norm_gain, w_raw, chans, before, earlier):
    count = len(shards)
    rows, width = shards[0].shape
    depth = min(width, WIDE)
    pieces = count * (width // depth)
    per = 2 * chans // LANES
    shapes = [(rows, chans), (rows, chans), (rows, 1)]
    operands = [table, *shards, norm_gain, w_raw]
    in_specs = [SMEM] + [VMEM] * (count + 1) + [HBM]
    aliases = {}
    if before is not None:
        aliases = {len(operands) + j: j for j in range(len(shapes))}
        in_specs += [VMEM] * len(shapes)
        operands += list(before)
    in_specs += [ANY] * len(earlier)
    operands += earlier
    return pl.pallas_call(
        functools.partial(proj_kernel, count, before is None, layer, table_at),
        out_shape=[jax.ShapeDtypeStruct(shape, F32) for shape in shapes],
        in_specs=in_specs,
        out_specs=[VMEM] * len(shapes),
        scratch_shapes=[
            pltpu.VMEM((pieces, depth * per, LANES), BF16),
            pltpu.VMEM((pieces, per * fold_stride(depth), LANES), F32),
            pltpu.SemaphoreType.DMA((pieces,)),
        ],
        input_output_aliases=aliases,
        compiler_params=params(36),
        cost_estimate=LONG,
        name="project",
    )(*operands)


def unpack_kernel(count, layer, table_at, width, table_ref, w_ref, *refs):
    out_ref, token_ref, raw_s, split_s, sems = refs[-5:]
    pieces, size, _ = raw_s.shape
    chans = out_ref.shape[2]
    per = 2 * chans // LANES
    depth = size // per
    apart = fold_stride(depth)
    taken = max(per, 16)
    each = width // depth

    def copy(n):
        begin = (table_ref[table_at + n // each] * width + n % each * depth) * per
        source = w_ref.at[layer, pl.ds(pl.multiple_of(begin, size), size), :]
        return pltpu.make_async_copy(source, raw_s.at[n], sems.at[n])

    for n in range(pieces):
        copy(n).start()
    token_ref[...] = jnp.zeros_like(token_ref)
    for n in range(pieces):
        copy(n).wait()
        slot = n % split_s.shape[0]
        for begin in range(0, size, taken):
            part = raw_s[n, begin : begin + taken, :].astype(F32)
            for k in range(taken // per):
                place = pl.ds((begin // per + k) * STRIDE, per, stride=apart)
                split_s[slot, place, :] = part[k * per : (k + 1) * per]
        for e in range(2):
            for begin in range(0, chans, WIDE):
                tiles = [
                    split_s[slot, pl.ds((2 * t + e) * apart, depth, stride=STRIDE), :].astype(BF16)
                    for t in range(begin // LANES, (begin + WIDE) // LANES)
                ]
                rows = slice(n * depth, (n + 1) * depth)
                out_ref[e, rows, begin : begin + WIDE] = jnp.concatenate(tiles, axis=1)


def unpack(layer, table, table_at, count, width, chans, w_raw, earlier):
    depth = min(width, WIDE)
    pieces = count * width // depth
    per = 2 * chans // LANES
    return pl.pallas_call(
        functools.partial(unpack_kernel, count, layer, table_at, width),
        out_shape=[
            jax.ShapeDtypeStruct((2, count * width, chans), BF16),
            jax.ShapeDtypeStruct((8, LANES), F32),
        ],
        in_specs=[SMEM, HBM] + [ANY] * len(earlier),
        out_specs=[VMEM, VMEM],
        scratch_shapes=[
            pltpu.VMEM((pieces, depth * per, LANES), BF16),
            pltpu.VMEM((2, per * fold_stride(depth), LANES), F32),
            pltpu.SemaphoreType.DMA((pieces,)),
        ],
        compiler_params=params(24),
        cost_estimate=COST,
        name="unpack",
    )(table, w_raw, *earlier)


def ready_kernel(count, first, layer, table_at, table_ref, *refs):
    shards = refs[:count]
    gain_ref, w_ref = refs[count : count + 2]
    cur_ref, gate_ref, square_ref = refs[-3:]
    rows, width = shards[0].shape
    chans = cur_ref.shape[1]
    squares = jnp.zeros((rows, 1), F32) if first else square_ref[...]
    parts = []
    for j in range(count):
        values = shards[j][:, :width].astype(F32)
        begin = pl.multiple_of(table_ref[table_at + j] * width, width)
        parts.append((values * gain_ref[layer : layer + 1, pl.ds(begin, width)]).astype(BF16))
        squares = squares + jnp.sum(values * values, axis=1, keepdims=True)
    square_ref[...] = squares
    left = jnp.concatenate(parts, axis=1)
    for e, out in enumerate((cur_ref, gate_ref)):
        for begin in range(0, chans, WIDE):
            cols = slice(begin, begin + WIDE)
            product = jnp.dot(left, w_ref[e, :, cols], preferred_element_type=F32)
            if first:
                out[:, cols] = product
            else:
                out[:, cols] += product


def project_ready(layer, shards, table, table_at, norm_gain, weights, before, earlier):
    count = len(shards)
    rows, width = shards[0].shape
    chans = weights.shape[2]
    state = [jax.ShapeDtypeStruct(s, F32) for s in ((rows, chans), (rows, chans), (rows, 1))]
    operands = [table, *shards, norm_gain, weights]
    in_specs = [SMEM] + [VMEM] * (count + 2)
    aliases = {}
    if before is not None:
        aliases = {len(operands) + j: j for j in range(3)}
        in_specs += [VMEM] * 3
        operands += list(before)
    return pl.pallas_call(
        functools.partial(ready_kernel, count, before is None, layer, table_at),
        out_shape=state,
        in_specs=in_specs + [ANY] * len(earlier),
        out_specs=[VMEM] * 3,
        input_output_aliases=aliases,
        compiler_params=params(12),
        cost_estimate=LONG,
        name="project_ready",
    )(*operands, *earlier)


def low_kernel(layer, table_ref, rows_ref, gain_ref, w_ref, *refs):
    width = rows_ref.shape[1]
    begin = pl.multiple_of(table_ref[0] * width, width)
    gain = gain_ref[layer : layer + 1, pl.ds(begin, width)]
    scaled = (rows_ref[...].astype(F32) * gain).astype(BF16)
    product = lax.dot_general(
        scaled, w_ref[layer], (((1,), (1,)), ((), ())), preferred_element_type=F32
    )
    out_ref = refs[-1]
    before = out_ref.shape[1] - product.shape[1]
    if before:
        out_ref[:, :before] = rows_ref[...]
    out_ref[:, before:] = product.astype(BF16)


def project_low(layer, table, own_rows, norm_gain, w_low, before, earlier):
    rows = own_rows.shape[0]
    return pl.pallas_call(
        functools.partial(low_kernel, layer),
        out_shape=jax.ShapeDtypeStruct((rows, before + w_low.shape[1]), BF16),
        in_specs=[SMEM] + [VMEM] * 3 + [ANY] * len(earlier),
        out_specs=VMEM,
        compiler_params=params(12),
        cost_estimate=COST,
        name="project_low",
    )(table, own_rows, norm_gain, w_low, *earlier)


def relay_kernel(value_ref, *refs):
    refs[-1][...] = value_ref[...]


def relay(value, *others):
    return pl.pallas_call(
        relay_kernel,
        out_shape=jax.ShapeDtypeStruct(value.shape, value.dtype),
        in_specs=[VMEM] + [ANY] * len(others),
        out_specs=VMEM,
        compiler_params=params(8),
        cost_estimate=COST,
        name="relay",
    )(value, *others)


def scan_kernel(
    layer,
    states,
    width,
    sel_ref,
    low_ref,
    square_ref,
    cur_ref,
    w_dt_ref,
    bias_ref,
    rate_ref,
    out_ref,
    time_ref,
    final_ref,
    step_s,
    drive_s,
):
    rows, chans = cur_ref.shape
    fold = chans // LANES
    rank = w_dt_ref.shape[1]
    factor = row_factor(square_ref[...], width)
    rank_part = (low_ref[:, :rank] * factor).astype(BF16)
    apart = fold_stride(rows)
    twice = factor * factor
    for begin in range(0, chans, WIDE):
        cols = slice(begin, begin + WIDE)
        pre = jnp.dot(rank_part, w_dt_ref[layer, :, cols], preferred_element_type=F32)
        pre = pre + bias_ref[layer : layer + 1, cols]
        step = jnp.maximum(pre, 0.0) + jnp.log1p(jnp.exp(-jnp.abs(pre)))
        drive = step * (cur_ref[:, cols] * twice)
        for q in range(WIDE // LANES):
            part = slice(q * LANES, (q + 1) * LANES)
            place = pl.ds((begin // LANES + q) * apart, rows, stride=STRIDE)
            step_s[place, :] = step[:, part]
            drive_s[place, :] = drive[:, part]

    def advance(t, carried):
        time, held = carried
        here = pl.ds(t * STRIDE, fold, stride=apart)
        step = step_s[here, :]
        drive = drive_s[here, :]
        sums = [None] * 4
        after = []
        for s in range(states):
            decay = jnp.exp2(step * rate_ref[layer, s])
            now = decay * held[s] + drive * sel_ref[t, s]
            term = now * sel_ref[t, states + s]
            sums[s % 4] = term if sums[s % 4] is None else sums[s % 4] + term
            after.append(now)
        time = time + step
        out_ref[here, :] = (sums[0] + sums[1]) + (sums[2] + sums[3])
        time_ref[here, :] = time
        return time, tuple(after)

    zero = jnp.zeros((fold, LANES), F32)
    time, held = lax.fori_loop(0, rows, advance, (zero, (zero,) * states), unroll=16)
    for s in range(states):
        final_ref[s] = held[s].astype(BF16)
    final_ref[states] = time.astype(BF16)


def local_scan(layer, width, selectors, low, square, cur, w_dt, dt_bias, rate):
    rows, chans = cur.shape
    _, states, fold, _ = rate.shape
    folded = (fold * fold_stride(rows), LANES)
    return pl.pallas_call(
        functools.partial(scan_kernel, layer, states, width),
        out_shape=[
            jax.ShapeDtypeStruct(folded, F32),
            jax.ShapeDtypeStruct(folded, F32),
            jax.ShapeDtypeStruct((states + 1, fold, LANES), BF16),
        ],
        in_specs=[SMEM] + [VMEM] * 6,
        out_specs=[VMEM] * 3,
        scratch_shapes=[pltpu.VMEM(folded, F32), pltpu.VMEM(folded, F32)],
        compiler_params=params(20),
        cost_estimate=COST,
        name="local_scan",
    )(selectors, low, square, cur, w_dt, dt_bias, rate)


def emit_chunks(layer, table_at, feat, gated_ref, table_ref, w_ref, chunks, w_s, sems, before=None):
    def copy(j):
        begin = pl.multiple_of(table_ref[table_at[j]] * feat, feat)
        return pltpu.make_async_copy(w_ref.at[layer, :, pl.ds(begin, feat)], w_s.at[j], sems.at[j])

    for j in range(len(chunks)):
        copy(j).start()
    if before is not None:
        before()
    for j, chunk in enumerate(chunks):
        copy(j).wait()
        for begin in range(0, feat, WIDE):
            cols = slice(begin, begin + WIDE)
            chunk[:, cols] = jnp.dot(
                gated_ref[...], w_s[j, :, cols], preferred_element_type=F32
            ).astype(BF16)


def close_kernel(layer, states, table_at, feat, width, table_ref, place_ref, sel_ref, *refs):
    out_ref, time_ref, cur_ref, gate_ref, square_ref, final_ref = refs[:6]
    rate_ref, skip_ref, thresh_ref, w_ref, gated_ref = refs[6:11]
    chunks = refs[11 : 11 + len(table_at)]
    enter_s, mixed_s, w_s, sems = refs[-4:]
    rows, chans = cur_ref.shape
    fold = chans // LANES
    apart = fold_stride(rows)

    def gate_all():
        def enter(p, state):
            time = final_ref[p, states].astype(F32)
            return tuple(
                jnp.exp2(time * rate_ref[layer, s]) * state[s] + final_ref[p, s].astype(F32)
                for s in range(states)
            )

        zero = jnp.zeros((fold, LANES), F32)
        state = lax.fori_loop(0, place_ref[0], enter, (zero,) * states)
        for s in range(states):
            enter_s[s] = state[s]

        def correct(t, carried):
            here = pl.ds(t * STRIDE, fold, stride=apart)
            time = time_ref[here, :]
            sums = [out_ref[here, :], None, None, None]
            for s in range(states):
                term = jnp.exp2(time * rate_ref[layer, s]) * (enter_s[s] * sel_ref[t, states + s])
                sums[s % 4] = term if sums[s % 4] is None else sums[s % 4] + term
            mixed_s[here, :] = (sums[0] + sums[1]) + (sums[2] + sums[3])
            return carried

        lax.fori_loop(0, rows, correct, 0, unroll=16)

        factor = row_factor(square_ref[...], width)
        for r in range(fold):
            cols = slice(r * LANES, (r + 1) * LANES)
            skip = skip_ref[layer : layer + 1, cols]
            mixed = mixed_s[pl.ds(r * apart, rows, stride=STRIDE), :] + skip * cur_ref[:, cols]
            mixed = mixed * factor
            normal = mixed * lax.rsqrt(jnp.mean(mixed * mixed, axis=1, keepdims=True) + EPS)
            thresh = thresh_ref[layer : layer + 1, cols]
            shrunk = jnp.maximum(normal - thresh, 0.0) - jnp.maximum(-normal - thresh, 0.0)
            gate = gate_ref[:, cols] * factor
            gated_ref[:, cols] = (shrunk * (gate * jax.nn.sigmoid(gate))).astype(BF16)

    emit_chunks(layer, table_at, feat, gated_ref, table_ref, w_ref, chunks, w_s, sems, gate_all)


def close_layer(
    layer, width, table, table_at, feat, seq_place, selectors, values, rate, skip, thresh, w_out
):
    rows, chans = values[2].shape
    _, states, fold, _ = rate.shape
    count = len(table_at)
    chunk = jax.ShapeDtypeStruct((rows, feat), BF16)
    results = pl.pallas_call(
        functools.partial(close_kernel, layer, states, table_at, feat, width),
        out_shape=[jax.ShapeDtypeStruct((rows, chans), BF16)] + [chunk] * count,
        in_specs=[SMEM] * 3 + [VMEM] * 9 + [HBM],
        out_specs=[VMEM] * (1 + count),
        scratch_shapes=[
            pltpu.VMEM((states, fold, LANES), F32),
            pltpu.VMEM((fold * fold_stride(rows), LANES), F32),
            pltpu.VMEM((count, chans, feat), BF16),
            pltpu.SemaphoreType.DMA((count,)),
        ],
        compiler_params=params(40),
        cost_estimate=COST,
        name="close_layer",
    )(table, seq_place, selectors, *values, rate, skip, thresh, w_out)
    return results[0], results[1:]


def expand_kernel(layer, table_at, feat, table_ref, gated_ref, w_ref, *refs):
    chunks = refs[: len(table_at)]
    emit_chunks(layer, table_at, feat, gated_ref, table_ref, w_ref, chunks, *refs[-2:])


def expand(layer, table, table_at, feat, gated, w_out):
    rows, chans = gated.shape
    count = len(table_at)
    return pl.pallas_call(
        functools.partial(expand_kernel, layer, table_at, feat),
        out_shape=[jax.ShapeDtypeStruct((rows, feat), BF16)] * count,
        in_specs=[SMEM, VMEM, HBM],
        out_specs=[VMEM] * count,
        scratch_shapes=[
            pltpu.VMEM((count, chans, feat), BF16),
            pltpu.SemaphoreType.DMA((count,)),
        ],
        compiler_params=params(40),
        cost_estimate=COST,
        name="expand",
    )(table, gated, w_out)


def finish_kernel(rank, own_ref, arrived_ref, *refs):
    low_ref, selectors_ref = refs[-2:]
    total = own_ref[...].astype(F32) + arrived_ref[...].astype(F32)
    low_ref[...] = total
    selectors_ref[...] = total[:, rank:]


def finish_low(rank, own, arrived, earlier):
    rows, count = own.shape
    return pl.pallas_call(
        functools.partial(finish_kernel, rank),
        out_shape=[
            jax.ShapeDtypeStruct((rows, count), F32),
            jax.ShapeDtypeStruct((rows, count - rank), F32),
        ],
        in_specs=[VMEM] * 2 + [ANY] * len(earlier),
        out_specs=[VMEM] * 2,
        compiler_params=params(8),
        cost_estimate=COST,
        name="finish_low",
    )(own, arrived, *earlier)


def combine_kernel(count, *refs):
    total = refs[0][...].astype(F32)
    for ref in refs[1:count]:
        total = total + ref[...].astype(F32)
    refs[-1][...] = total.astype(BF16)


def combine(values, earlier):
    return pl.pallas_call(
        functools.partial(combine_kernel, len(values)),
        out_shape=jax.ShapeDtypeStruct(values[0].shape, BF16),
        in_specs=[VMEM] * len(values) + [ANY] * len(earlier),
        out_specs=VMEM,
        compiler_params=params(8),
        cost_estimate=COST,
        name="combine",
    )(*values, *earlier)


class Grid:
    def __init__(self, count):
        self.depth = DEPTH if count % DEPTH == 0 else 1
        self.side = count // self.depth

    def places(self):
        return [(z, y) for z in range(self.depth) for y in range(self.side)]

    def at(self, z, y):
        return (z % self.depth) * self.side + y % self.side

    def send(self, value, deep, across):
        pairs = [(self.at(z, y), self.at(z + deep, y + across)) for z, y in self.places()]
        return lax.ppermute(value, "tp", pairs)

    def swap(self, value, bit):
        pairs = [(self.at(z, y), self.at(z ^ bit, y)) for z, y in self.places()]
        return lax.ppermute(value, "tp", pairs)

    def table(self):
        own = lax.axis_index("tp")
        z, y = own // self.side, own % self.side
        offsets = jnp.arange(self.depth * self.side, dtype=jnp.int32)
        a, b = offsets // self.side, offsets % self.side
        both = []
        for sign in (-1, 1):
            deep = (z + sign * a + self.depth) % self.depth
            both.append(deep * self.side + (y + sign * b + self.side) % self.side)
        return jnp.concatenate(both).astype(jnp.int32)


def gather_columns(grid, own):
    columns = {0: own}
    half = grid.depth // 2
    for a in range(1, grid.depth - half + 1):
        columns[a] = grid.send(columns[a - 1], 1, 0)
        back = grid.depth - a
        if back > a:
            columns[back] = grid.send(columns[(back + 1) % grid.depth], -1, 0)
    return columns


def scatter_order(grid):
    order = []
    for a in range(grid.depth - grid.depth // 2, 0, -1):
        order.append(a)
        if grid.depth - a > a:
            order.append(grid.depth - a)
    return order + [0]


def scatter_sum(grid, own_rows, chunks, aside):
    order = scatter_order(grid)
    crossed = {
        a: [grid.send(chunks[a, b], 0, b) for b in range(1, grid.side)] for a in order
    }
    half = grid.depth - grid.depth // 2
    arriving = {a: [] for a in order}
    waiting = []
    for n, a in enumerate(order):
        parts = [chunks[a, 0], *crossed[a], *arriving[a]]
        if a == 0:
            aside(n, [*crossed[a], chunks[a, 0]][0])
            return combine([own_rows, *parts], waiting)
        part = combine(parts, waiting)
        step = 1 if a <= half else -1
        arriving[(a - step) % grid.depth].append(grid.send(part, step, 0))
        waiting = aside(n, part)


def sum_selectors(grid, partials):
    total = sum(partial.astype(F32) for partial in partials)
    pairs = []
    bit = 1
    while True:
        rounded = total.astype(BF16)
        arrived = grid.swap(rounded, bit) if bit < grid.depth else jnp.zeros_like(rounded)
        pairs.append((rounded, arrived))
        bit *= 2
        if bit >= grid.depth:
            return pairs
        total = rounded.astype(F32) + arrived.astype(F32)


def per_device(
    n_tp, tokens, norm_gain, w_in, w_low, w_dt, a_rate, dt_bias, skip_gain, threshold, w_out
):
    grid = Grid(n_tp)
    feat = tokens.shape[1]
    layers, width, _, chans = w_in.shape
    states = a_rate.shape[1]
    rank = w_dt.shape[1]
    fold = chans // LANES
    table = grid.table()
    forth = lambda a, b: n_tp + a * grid.side + b
    seq_place = lax.axis_index("seq").astype(jnp.int32).reshape(1)
    rates = (a_rate * (-math.log2(math.e))).reshape(layers, states, fold, LANES)
    w_raw = w_in.reshape(layers, width, 2, fold, LANES).transpose(0, 1, 3, 2, 4)
    w_raw = w_raw.reshape(layers, width * 2 * fold, LANES)
    order = scatter_order(grid)
    own_rows = tokens
    low_t = jnp.swapaxes(w_low, 1, 2)
    arrivals = [0] + [a for a in order if a not in (0, order[0])] + order[:1]
    weights = {}
    for layer in range(layers):
        columns = gather_columns(grid, own_rows)
        cross = lambda column: [grid.send(column, 0, b) for b in range(1, grid.side)]
        packed = layer > 0
        if packed:
            low = project_low(layer, table, own_rows, norm_gain, low_t, feat, [])
            beside = {0: cross(low)}
            lows = [each[:, feat:] for each in (low, *beside[0])]
        else:
            beside = {0: cross(own_rows)}
            low = project_low(layer, table, own_rows, norm_gain, low_t, 0, beside[0])
            lows = [low, *cross(low)]
            weights[0], _ = unpack(layer, table, 0, grid.side, feat, chans, w_raw, [])
        pairs = sum_selectors(grid, lows)
        stages = [own for own, _ in pairs]
        state = None
        for n, a in enumerate(arrivals):
            if n:
                last = n + 1 == len(arrivals)
                beside[a] = cross(relay(columns[a], *first) if last else columns[a])
            arrived = [columns[a], *beside[a]]
            place, earlier = a * grid.side, stages[n - 1 : n] if n else []
            if a in weights:
                state = project_ready(
                    layer, arrived, table, place, norm_gain, weights[a], state, earlier
                )
            else:
                state = project(
                    layer, arrived, table, place, norm_gain, w_raw, chans, state, earlier
                )
            if n == 0:
                first = [state[2], *stages[1:2]] if packed else [state[2]]
        cur, gate, square = state
        low, selectors = finish_low(rank, *pairs[-1], [square])
        out, time, final = local_scan(
            layer, width, selectors, low, square, cur, w_dt, dt_bias, rates
        )
        finals = lax.all_gather(final, "seq")
        keys = [(a, b) for a in order for b in range(1, grid.side)]
        keys += [(a, 0) for a in order]
        lead = grid.side - 1
        gated, chunks = close_layer(
            layer,
            width,
            table,
            [forth(*key) for key in keys[:lead]],
            feat,
            seq_place,
            selectors,
            (out, time, cur, gate, square, finals),
            rates,
            skip_gain,
            threshold,
            w_out,
        )
        chunks = dict(zip(keys, chunks))
        split = len(order) * lead + 1
        for part in (keys[lead:split], keys[split:]):
            more = expand(layer, table, [forth(*key) for key in part], feat, gated, w_out)
            chunks.update(zip(part, more))
        weights = {}

        def aside(n, value):
            left = [a for a in arrivals if a not in weights]
            wanted = [1, 0, len(left) - 1, 1][min(n, 3)] if layer + 1 < layers else 0
            tokens = []
            for a in left[:wanted]:
                weights[a], token = unpack(
                    layer + 1, table, a * grid.side, grid.side, feat, chans, w_raw, [value]
                )
                tokens.append(token)
            return tokens

        own_rows = scatter_sum(grid, own_rows, chunks, aside)
    return own_rows


def solution(mesh):
    in_specs = (
        P("seq", "tp"),
        P(),
        P(None, None, None, "tp"),
        P(None, "tp", None),
        P(None, None, "tp"),
        P(None, None, "tp"),
        P(None, "tp"),
        P(None, "tp"),
        P(None, "tp"),
        P(None, "tp", None),
    )
    return jax.shard_map(
        functools.partial(per_device, mesh.shape["tp"]),
        mesh=mesh,
        in_specs=in_specs,
        out_specs=P("seq", "tp"),
        check_vma=False,
    )
```
